32 devices in a mesh: dp: 8 (over z, x), rep: 4 (over y, core).
Axes of the slice: x: 2, y: 2, z: 4, core: 2. Of those that a mesh axis runs over, the one named last changes fastest.
Arguments:
- patches: bfloat16 [512, 50, 1024], P(('dp', 'rep')), may hold values from -6 to 6
- keep: int32 [512, 50], P(('dp', 'rep')), may hold values from 0 to 1, as said below
- ln1_gain: float32 [1024], replicated, may hold values from 0.5 to 1.5
- ln1_bias: float32 [1024], replicated, may hold values from -3 to 3
- w_qkv: bfloat16 [1024, 3072], replicated, may hold values from -0.1875 to 0.1875
- b_query: float32 [1024], replicated, may hold values from -3 to 3
- b_value: float32 [1024], replicated, may hold values from -3 to 3
- w_out: bfloat16 [1024, 1024], replicated, may hold values from -0.4375 to 0.4375
- b_out: float32 [1024], replicated, may hold values from -3 to 3
- ln2_gain: float32 [1024], replicated, may hold values from 0.5 to 1.5
- ln2_bias: float32 [1024], replicated, may hold values from -3 to 3
- w_fc1: bfloat16 [1024, 4096], replicated, may hold values from -0.1875 to 0.1875
- b_fc1: float32 [4096], replicated, may hold values from -3 to 3
- w_fc2: bfloat16 [4096, 1024], replicated, may hold values from -0.125 to 0.125
- b_fc2: float32 [1024], replicated, may hold values from -3 to 3
- cotangent: bfloat16 [512, 50, 1024], P(('dp', 'rep')), may hold values from -6 to 6
Outputs:
- layer_out: bfloat16 [512, 50, 1024], P(('dp', 'rep'))
- grad_patches: float32 [512, 50, 1024], P(('dp', 'rep'))
- grad_ln1_gain: float32 [1024], P(('dp', 'rep'))
- grad_ln1_bias: float32 [1024], P(('dp', 'rep'))
- grad_w_qkv: float32 [1024, 3072], P(('dp', 'rep'))
- grad_b_query: float32 [1024], P(('dp', 'rep'))
- grad_b_value: float32 [1024], P(('dp', 'rep'))
- grad_w_out: float32 [1024, 1024], P(('dp', 'rep'))
- grad_b_out: float32 [1024], P(('dp', 'rep'))
- grad_ln2_gain: float32 [1024], P(('dp', 'rep'))
- grad_ln2_bias: float32 [1024], P(('dp', 'rep'))
- grad_w_fc1: float32 [1024, 4096], P(('dp', 'rep'))
- grad_b_fc1: float32 [4096], P(('dp', 'rep'))
- grad_w_fc2: float32 [4096, 1024], P(('dp', 'rep'))
- grad_b_fc2: float32 [1024], P(('dp', 'rep'))
The draws below stay inside these ranges and needn't reach their ends.
Inputs may be any that keep to these rules, and one draw needn't show every extreme that they name: `keep`: each row keeps position 0 and between 25 and 50 positions in all; some image keeps exactly 50 and some exactly 25.
All inputs are finite; a program needn't handle non-finite values.
Results may differ from the reference program's by a relative error of at most 0.011.
Values sent between devices are 32-bit elements; how exact they have to be, the bound alone decides.
A program may use at most 256 MiB of HBM per device.

```python
import jax
import jax.numpy as jnp
from jax import lax

D = 1024
HEADS = 16
HEAD_DIM = 64
FF = 4096
SLOTS = 50
MIN_KEEP = 25
IMG_DEV = 16
IMAGES = 512


def draw_keep(key, part):
    key = jax.random.fold_in(key, 11)
    count_key, order_key = jax.random.split(key)
    counts = jax.random.randint(count_key, (IMAGES,), MIN_KEEP, SLOTS + 1)
    counts = counts.at[0].set(SLOTS).at[1].set(MIN_KEEP)
    image_keys = jax.random.split(order_key, IMAGES)
    orders = jax.vmap(lambda k: jax.random.permutation(k, SLOTS - 1))(image_keys)
    patch_keep = (orders < counts[:, None] - 1).astype(jnp.int32)
    first = jnp.ones((IMAGES, 1), jnp.int32)
    return jnp.concatenate([first, patch_keep], axis=1)


def shard_levels(rng, shape, cuts, low, top_value):
    loudness, own = 1.0, jax.random.fold_in(rng, 6)
    for position, parts in cuts:
        draws = jnp.exp(jax.random.uniform(jax.random.fold_in(own, position), (parts,), jnp.float32, low / len(cuts), top_value / len(cuts)))
        loudness = loudness * jnp.repeat(draws, shape[position] // parts).reshape([-1 if axis == position else 1 for axis in range(len(shape))])
    return loudness


def scatter_about(rng, dims, spread, limit, cuts=(), held_as=jnp.bfloat16):
    drawn = spread * jax.random.normal(rng, dims, jnp.float32)
    if cuts:
        drawn = drawn * shard_levels(rng, dims, cuts, -0.22, 0.18)
    return jnp.clip(drawn, -limit, limit).astype(held_as)


def setup_inputs(seed: int = 0) -> dict:
    seeds = jax.random.split(jax.random.key(seed), 17)
    return {
        "patches": scatter_about(seeds[0], (IMAGES, SLOTS, D), 1.0, 6.0, ((0, 32),)),
        "keep": draw_keep(jax.random.fold_in(seeds[16], 71), 0),
        "ln1_gain": jnp.clip(1.0 + 0.1 * jax.random.normal(seeds[2], (D,), jnp.float32), 0.5, 1.5),
        "ln1_bias": scatter_about(seeds[3], (D,), 0.3, 3.0, (), jnp.float32),
        "w_qkv": scatter_about(seeds[4], (D, 3 * D), D ** -0.5, 0.1875),
        "b_query": scatter_about(seeds[5], (D,), 0.3, 3.0, (), jnp.float32),
        "b_value": scatter_about(seeds[6], (D,), 0.3, 3.0, (), jnp.float32),
        "w_out": scatter_about(seeds[7], (D, D), (D // 6) ** -0.5, 0.4375),
        "b_out": scatter_about(seeds[8], (D,), 0.3, 3.0, (), jnp.float32),
        "ln2_gain": jnp.clip(1.0 + 0.1 * jax.random.normal(seeds[9], (D,), jnp.float32), 0.5, 1.5),
        "ln2_bias": scatter_about(seeds[10], (D,), 0.3, 3.0, (), jnp.float32),
        "w_fc1": scatter_about(seeds[11], (D, FF), D ** -0.5, 0.1875),
        "b_fc1": scatter_about(seeds[12], (FF,), 0.3, 3.0, (), jnp.float32),
        "w_fc2": scatter_about(seeds[13], (FF, D), (FF // 2) ** -0.5, 0.125),
        "b_fc2": scatter_about(seeds[14], (D,), 0.3, 3.0, (), jnp.float32),
        "cotangent": scatter_about(seeds[15], (IMAGES, SLOTS, D), 1.0, 6.0, ((0, 32),)),
    }


NORM_EPSILON = 1e-06
SCORE_SCALE = 0.125
HIGH = lax.Precision.HIGHEST

@jax.custom_vjp
def low(v):
    return lax.optimization_barrier(v.astype(jnp.bfloat16)).astype(jnp.float32)

@jax.custom_vjp
def low_back(v):
    return v

def low_keep(v):
    return (low(v), None)

def low_pass(kept, grad):
    return (grad,)

def back_keep(v):
    return (v, None)

def back_low(kept, grad):
    return (low(grad),)
low.defvjp(low_keep, low_pass)
low_back.defvjp(back_keep, back_low)

def select_parts(keep):
    slot_ids = jnp.arange(SLOTS, dtype=jnp.int32)
    ranks = jnp.cumsum(keep, axis=1).astype(jnp.int32) - 1
    table = (ranks[:, None, :] == slot_ids[None, :, None]) & (keep[:, None, :] == 1)
    counts = lax.optimization_barrier(jnp.sum(keep, axis=1)).astype(jnp.int32)
    valid_slots = (slot_ids[None, :] < counts[:, None]).astype(jnp.float32)
    return (table.astype(jnp.float32), valid_slots)

def normalize(v):
    centred = v - lax.optimization_barrier(jnp.mean(v, axis=-1, keepdims=True))
    return centred * lax.rsqrt(lax.optimization_barrier(jnp.mean(centred * centred, axis=-1, keepdims=True)) + NORM_EPSILON)

def layer_forward(parameters, inputs, table, valid_slots):
    ln1_gain, ln1_bias, w_qkv, b_query, b_value, w_out, b_out, ln2_gain, ln2_bias, w_fc1, b_fc1, w_fc2, b_fc2 = parameters
    images = inputs.shape[0]
    row_count = images * SLOTS
    kept = jnp.einsum('bsp,bpd->bsd', table, inputs, precision=HIGH).reshape(row_count, D)
    act_one = low(normalize(kept) * ln1_gain + ln1_bias)
    bias_all = jnp.concatenate([b_query, jnp.zeros_like(b_query), b_value])
    qkv = low(low_back(jnp.dot(act_one, w_qkv, precision=HIGH) + bias_all))
    qkv = qkv.reshape(images, SLOTS, 3, HEADS, HEAD_DIM)
    queries, key_part, values = (qkv[:, :, 0], qkv[:, :, 1], qkv[:, :, 2])
    scores = jnp.einsum('blhe,bmhe->bhlm', queries, key_part, precision=HIGH) * SCORE_SCALE
    scores = jnp.where(valid_slots[:, None, None, :] > 0, scores, -1000000000.0)
    scores = low_back(scores)
    attn_probs = low(jax.nn.softmax(scores, axis=-1))
    mixed_heads = jnp.einsum('bhlm,bmhe->blhe', attn_probs, values, precision=HIGH).reshape(row_count, D)
    mixed_heads = low(low_back(mixed_heads))
    branch = low_back(jnp.dot(mixed_heads, w_out, precision=HIGH) + b_out)
    after_attn = kept + branch
    act_two = low(normalize(after_attn) * ln2_gain + ln2_bias)
    pre_gelu = low_back(jnp.dot(act_two, w_fc1, precision=HIGH) + b_fc1)
    gelu_out = low(jax.nn.gelu(pre_gelu, approximate=False))
    mlp_out = low_back(jnp.dot(gelu_out, w_fc2, precision=HIGH) + b_fc2)
    result = (after_attn + mlp_out).reshape(images, SLOTS, D)
    return result * valid_slots[:, :, None]

def reference(patches, keep, ln1_gain, ln1_bias, w_qkv, b_query, b_value, w_out, b_out, ln2_gain, ln2_bias, w_fc1, b_fc1, w_fc2, b_fc2, cotangent):
    parameters = tuple((p.astype(jnp.float32) for p in (ln1_gain, ln1_bias, w_qkv, b_query, b_value, w_out, b_out, ln2_gain, ln2_bias, w_fc1, b_fc1, w_fc2, b_fc2)))
    table, valid_slots = select_parts(keep)
    groups = IMAGES // IMG_DEV
    inputs = patches.astype(jnp.float32).reshape(groups, IMG_DEV, SLOTS, D)
    tables = table.reshape(groups, IMG_DEV, SLOTS, SLOTS)
    valids = valid_slots.reshape(groups, IMG_DEV, SLOTS)
    cotans = cotangent.astype(jnp.float32).reshape(groups, IMG_DEV, SLOTS, D)

    def step(totals, pieces):
        block_in, block_table, block_valid, block_cot = pieces
        result, pullback = jax.vjp(lambda prm, xin: layer_forward(prm, xin, block_table, block_valid), parameters, block_in)
        grad_params, grad_in = pullback(block_cot)
        totals = jax.tree.map(lambda a, b: a + b, totals, grad_params)
        return (totals, (result.astype(jnp.bfloat16), grad_in))
    start = tuple((jnp.zeros(p.shape, jnp.float32) for p in parameters))
    totals, (outputs, grad_inputs) = lax.scan(step, start, (inputs, tables, valids, cotans))
    layer_out = outputs.reshape(IMAGES, SLOTS, D)
    grad_patches = grad_inputs.reshape(IMAGES, SLOTS, D)
    return (layer_out, grad_patches, totals[0], totals[1], totals[2], totals[3], totals[4], totals[5], totals[6], totals[7], totals[8], totals[9], totals[10], totals[11], totals[12])
```

```python
from functools import partial

import jax
import jax.numpy as jnp
from jax import lax
from jax.sharding import PartitionSpec as P

HEADS = 16
HEAD_DIM = 64


NORM_EPSILON = 1e-06
SCORE_SCALE = 0.125


def select_parts(keep, slot_count):
    slot_ids = jnp.arange(slot_count, dtype=jnp.int32)
    ranks = jnp.cumsum(keep, axis=1) - 1
    table = (ranks[:, None, :] == slot_ids[None, :, None]) & (keep[:, None, :] == 1)
    counts = jnp.sum(keep, axis=1)
    valid_slots = (slot_ids[None, :] < counts[:, None]).astype(jnp.float32)
    return (table.astype(jnp.float32), valid_slots)


def normalize(v):
    centred = v - jnp.mean(v, axis=-1, keepdims=True)
    return centred * lax.rsqrt(jnp.mean(centred * centred, axis=-1, keepdims=True) + NORM_EPSILON)


def affine_norm(v, gain, shift):
    return normalize(v) * gain + shift


def matmul(left, right):
    return jnp.dot(left, right, preferred_element_type=jnp.float32)


def exchange(parts, axis, stride, count):
    size = lax.axis_size(axis)
    index = lax.axis_index(axis)
    place = (index // stride) % count
    total = lax.dynamic_index_in_dim(parts, place, 0, keepdims=False)
    for step in range(1, count):
        pairs = []
        for source in range(size):
            own = (source // stride) % count
            target = source + (((own + step) % count) - own) * stride
            pairs.append((source, target))
        sent = lax.dynamic_index_in_dim(parts, (place + step) % count, 0, keepdims=False)
        total = total + lax.ppermute(sent, axis, pairs)
    return total


def scatter_sum(grad):
    rows, columns = grad.shape
    dp, rep = lax.axis_size("dp"), lax.axis_size("rep")
    z, y = dp // 2, rep // 2
    share = rows // (dp * rep)
    parts = grad.reshape(z, 2, y, 2, share, columns)
    parts = exchange(jnp.moveaxis(parts, 3, 0), "rep", 1, 2)
    half = columns // 2
    x_first, y_first = parts[..., :half], parts[..., half:]
    x_first = exchange(jnp.moveaxis(x_first, 1, 0), "dp", 1, 2)
    y_first = exchange(jnp.moveaxis(y_first, 2, 0), "rep", 2, y)
    x_first = exchange(jnp.moveaxis(x_first, 1, 0), "rep", 2, y)
    y_first = exchange(jnp.moveaxis(y_first, 1, 0), "dp", 1, 2)
    both = jnp.concatenate([x_first, y_first], axis=-1)
    return exchange(both, "dp", 2, z)


def scatter_vectors(vectors):
    joined = jnp.concatenate([v.reshape(lax.axis_size("dp") * lax.axis_size("rep"), -1) for v in vectors], axis=1)
    total = lax.psum_scatter(joined, ("dp", "rep"), scatter_dimension=0, tiled=True)[0]
    out, start = [], 0
    for v in vectors:
        length = v.shape[0] // (lax.axis_size("dp") * lax.axis_size("rep"))
        out.append(total[start : start + length])
        start += length
    return out


def local(
    patches,
    keep,
    ln1_gain,
    ln1_bias,
    w_qkv,
    b_query,
    b_value,
    w_out,
    b_out,
    ln2_gain,
    ln2_bias,
    w_fc1,
    b_fc1,
    w_fc2,
    b_fc2,
    cotangent,
):
    images, slot_count, width = patches.shape
    row_count = images * slot_count
    table, valid_slots = select_parts(keep, slot_count)
    kept = jnp.einsum(
        "bsp,bpd->bsd", table.astype(jnp.bfloat16), patches, preferred_element_type=jnp.float32
    ).reshape(row_count, width)
    normed_one, norm_one_back = jax.vjp(affine_norm, kept, ln1_gain, ln1_bias)
    act_one = normed_one.astype(jnp.bfloat16)
    bias_all = jnp.concatenate([b_query, jnp.zeros_like(b_query), b_value])
    qkv = (matmul(act_one, w_qkv) + bias_all).astype(jnp.bfloat16)
    qkv = qkv.reshape(images, slot_count, 3, HEADS, HEAD_DIM)
    queries, key_part, values = (qkv[:, :, 0], qkv[:, :, 1], qkv[:, :, 2])
    scores = (
        jnp.einsum("blhe,bmhe->bhlm", queries, key_part, preferred_element_type=jnp.float32)
        * SCORE_SCALE
    )
    scores = jnp.where(valid_slots[:, None, None, :] > 0, scores, -1000000000.0)
    attn_probs, softmax_back = jax.vjp(partial(jax.nn.softmax, axis=-1), scores)
    probs_low = attn_probs.astype(jnp.bfloat16)
    mixed_heads = jnp.einsum(
        "bhlm,bmhe->blhe", probs_low, values, preferred_element_type=jnp.float32
    )
    mixed_heads = mixed_heads.reshape(row_count, width).astype(jnp.bfloat16)
    after_attn = kept + (matmul(mixed_heads, w_out) + b_out)
    normed_two, norm_two_back = jax.vjp(affine_norm, after_attn, ln2_gain, ln2_bias)
    act_two = normed_two.astype(jnp.bfloat16)
    pre_gelu = matmul(act_two, w_fc1) + b_fc1
    gelu_full, gelu_back = jax.vjp(partial(jax.nn.gelu, approximate=False), pre_gelu)
    gelu_out = gelu_full.astype(jnp.bfloat16)
    mlp_out = matmul(gelu_out, w_fc2) + b_fc2
    row_mask = valid_slots.reshape(row_count, 1)
    layer_out = ((after_attn + mlp_out) * row_mask).astype(jnp.bfloat16)
    layer_out = layer_out.reshape(images, slot_count, width)
    grad_out = cotangent.astype(jnp.float32).reshape(row_count, width) * row_mask
    grad_top = grad_out.astype(jnp.bfloat16)
    grad_w_fc2 = matmul(gelu_out.T, grad_top)
    grad_b_fc2 = jnp.sum(grad_top.astype(jnp.float32), axis=0)
    (grad_pre_full,) = gelu_back(matmul(grad_top, w_fc2.T))
    grad_pre = grad_pre_full.astype(jnp.bfloat16)
    grad_w_fc1 = matmul(act_two.T, grad_pre)
    grad_b_fc1 = jnp.sum(grad_pre.astype(jnp.float32), axis=0)
    grad_norm_two, grad_ln2_gain, grad_ln2_bias = norm_two_back(matmul(grad_pre, w_fc1.T))
    grad_after = grad_out + grad_norm_two
    share_w_fc2 = scatter_sum(grad_w_fc2)
    share_w_fc1 = scatter_sum(grad_w_fc1)
    grad_branch = grad_after.astype(jnp.bfloat16)
    grad_w_out = matmul(mixed_heads.T, grad_branch)
    grad_b_out = jnp.sum(grad_branch.astype(jnp.float32), axis=0)
    grad_mixed = matmul(grad_branch, w_out.T).astype(jnp.bfloat16)
    grad_mixed = grad_mixed.reshape(images, slot_count, HEADS, HEAD_DIM)
    grad_probs = jnp.einsum(
        "blhe,bmhe->bhlm", grad_mixed, values, preferred_element_type=jnp.float32
    )
    grad_values = jnp.einsum(
        "bhlm,blhe->bmhe", probs_low, grad_mixed, preferred_element_type=jnp.float32
    )
    (grad_scores_full,) = softmax_back(grad_probs)
    grad_scores = grad_scores_full.astype(jnp.bfloat16)
    grad_queries = (
        jnp.einsum("bhlm,bmhe->blhe", grad_scores, key_part, preferred_element_type=jnp.float32)
        * SCORE_SCALE
    )
    grad_keys = (
        jnp.einsum("bhlm,blhe->bmhe", grad_scores, queries, preferred_element_type=jnp.float32)
        * SCORE_SCALE
    )
    grad_qkv = jnp.stack([grad_queries, grad_keys, grad_values], axis=2)
    grad_qkv = grad_qkv.reshape(row_count, 3 * width).astype(jnp.bfloat16)
    grad_w_qkv = matmul(act_one.T, grad_qkv)
    column_sums = jnp.sum(grad_qkv.astype(jnp.float32), axis=0)
    grad_b_query = column_sums[:width]
    grad_b_value = column_sums[2 * width :]
    grad_norm_one, grad_ln1_gain, grad_ln1_bias = norm_one_back(matmul(grad_qkv, w_qkv.T))
    grad_kept = grad_after + grad_norm_one
    share_w_out = scatter_sum(grad_w_out)
    share_w_qkv = scatter_sum(grad_w_qkv)
    small = scatter_vectors(
        [grad_ln1_gain, grad_ln1_bias, grad_b_query, grad_b_value, grad_b_out, grad_ln2_gain, grad_ln2_bias, grad_b_fc1, grad_b_fc2]
    )
    grad_patches = jnp.einsum(
        "bsp,bsd->bpd",
        table,
        grad_kept.reshape(images, slot_count, width),
        precision=lax.Precision.HIGHEST,
    )
    return (
        layer_out,
        grad_patches,
        small[0],
        small[1],
        share_w_qkv,
        small[2],
        small[3],
        share_w_out,
        small[4],
        small[5],
        small[6],
        share_w_fc1,
        small[7],
        share_w_fc2,
        small[8],
    )


def solution(mesh):
    in_specs = (
        P(("dp", "rep"), None, None),
        P(("dp", "rep"), None),
        P(),
        P(),
        P(),
        P(),
        P(),
        P(),
        P(),
        P(),
        P(),
        P(),
        P(),
        P(),
        P(),
        P(("dp", "rep"), None, None),
    )
    out_specs = (
        P(("dp", "rep"), None, None),
        P(("dp", "rep"), None, None),
        P(("dp", "rep")),
        P(("dp", "rep")),
        P(("dp", "rep"), None),
        P(("dp", "rep")),
        P(("dp", "rep")),
        P(("dp", "rep"), None),
        P(("dp", "rep")),
        P(("dp", "rep")),
        P(("dp", "rep")),
        P(("dp", "rep"), None),
        P(("dp", "rep")),
        P(("dp", "rep"), None),
        P(("dp", "rep")),
    )
    return jax.shard_map(local, mesh=mesh, in_specs=in_specs, out_specs=out_specs, check_vma=False)
```

```python
from functools import partial

import jax
import jax.numpy as jnp
from jax import lax
from jax.experimental import pallas as pl
from jax.experimental.pallas import tpu as pltpu
from jax.sharding import PartitionSpec as P

HEADS = 16
HEAD_DIM = 64
NORM_EPSILON = 1e-06
SCORE_SCALE = 0.125
PAD = 64
GROUP = 256
MIB = 1 << 20
NT = (((1,), (1,)), ((), ()))


def select_parts(keep, slot_count):
    slot_ids = jnp.arange(slot_count, dtype=jnp.int32)
    ranks = jnp.cumsum(keep, axis=1) - 1
    table = (ranks[:, None, :] == slot_ids[None, :, None]) & (keep[:, None, :] == 1)
    counts = jnp.sum(keep, axis=1)
    valid_slots = (slot_ids[None, :] < counts[:, None]).astype(jnp.float32)
    return (table.astype(jnp.float32), valid_slots)


def matmul(left, right):
    return jnp.dot(left, right, preferred_element_type=jnp.float32)


def matmul_nt(left, right):
    return lax.dot_general(left, right, NT, preferred_element_type=jnp.float32)


def normed_rows(v):
    centred = v - jnp.mean(v, axis=-1, keepdims=True)
    scale = lax.rsqrt(jnp.mean(centred * centred, axis=-1, keepdims=True) + NORM_EPSILON)
    return centred * scale, scale


def head_sums(v, heads):
    high = v.astype(jnp.bfloat16)
    rest = (v - high.astype(jnp.float32)).astype(jnp.bfloat16)
    return matmul(high, heads) + matmul(rest, heads)


def spread_heads(v, heads):
    return jnp.concatenate([v] * 4, axis=0) * heads


def forward_kernel(
    patches, cotangent, select, keys_valid, slot_rows, heads,
    ln1_gain, ln1_bias, b_query, b_value, b_out, ln2_gain, ln2_bias, w_qkv, w_out,
    kept_out, act1_t_out, qkv_out, probs_out, mixed_t_out, after_out, act2_out, act2_t_out, top_out,
    act1, mixed, kept,
):
    images = keys_valid.shape[0]
    width = patches.shape[1]
    kept[...] = matmul(select[...], patches[...])
    kept_out[...] = kept[...].astype(jnp.bfloat16)
    unit, _ = normed_rows(kept[...])
    act1[...] = (unit * ln1_gain[...] + ln1_bias[...]).astype(jnp.bfloat16)
    top_out[...] = matmul(slot_rows[...], cotangent[...]).astype(jnp.bfloat16)
    act1_t_out[...] = act1[...].T
    qkv_out[0] = (matmul(act1[...], w_qkv[:, :width]) + b_query[...]).astype(jnp.bfloat16)
    qkv_out[1] = matmul(act1[...], w_qkv[:, width : 2 * width]).astype(jnp.bfloat16)
    qkv_out[2] = (matmul(act1[...], w_qkv[:, 2 * width :]) + b_value[...]).astype(jnp.bfloat16)

    def attend(i, carry):
        rows = pl.ds(pl.multiple_of(i * PAD, PAD), PAD)
        seen = keys_valid[i] > 0
        head_of = lax.broadcasted_iota(jnp.int32, (PAD, GROUP), 1) // HEAD_DIM
        for g in range(width // GROUP):
            lanes = slice(g * GROUP, (g + 1) * GROUP)
            keys = spread_heads(qkv_out[1, rows, lanes], heads[...])
            scores = matmul_nt(qkv_out[0, rows, lanes], keys) * SCORE_SCALE
            scores = jnp.where(seen, scores, -1000000000.0)
            top = jnp.zeros_like(scores)
            for h in range(4):
                own = jnp.max(jnp.where(head_of == h, scores, -3e38), axis=1, keepdims=True)
                top = jnp.where(head_of == h, own, top)
            raised = jnp.exp(scores - top)
            probs = (raised / head_sums(raised, heads[...])).astype(jnp.bfloat16)
            probs_out[rows, lanes] = probs
            values = spread_heads(qkv_out[2, rows, lanes], heads[...])
            mixed[rows, lanes] = matmul(probs, values).astype(jnp.bfloat16)
        return carry

    lax.fori_loop(0, images, attend, 0, unroll=True)
    mixed_t_out[...] = mixed[...].T
    after = kept[...] + (matmul(mixed[...], w_out[...]) + b_out[...])
    after_out[...] = after
    unit, _ = normed_rows(after)
    act2 = (unit * ln2_gain[...] + ln2_bias[...]).astype(jnp.bfloat16)
    act2_out[...] = act2
    act2_t_out[...] = act2.T


def forward(patches, cotangent, select, keys_valid, slot_rows, heads, vectors, w_qkv, w_out):
    width = patches.shape[1]
    rows, images = select.shape[0], keys_valid.shape[0]
    step = 4
    block = step * PAD
    half = lambda *shape: jax.ShapeDtypeStruct(shape, jnp.bfloat16)
    whole = lambda a: pl.BlockSpec(a.shape, lambda g: (0,) * a.ndim, pipeline_mode=pl.Buffered(1))
    by_rows = lambda columns: pl.BlockSpec((block, columns), lambda g: (g, 0))
    by_columns = pl.BlockSpec((width, block), lambda g: (0, g))
    return pl.pallas_call(
        forward_kernel,
        grid=(images // step,),
        in_specs=[
            whole(patches), whole(cotangent), by_rows(select.shape[1]), pl.BlockSpec((step, 1, GROUP), lambda g: (g, 0, 0)),
            by_rows(select.shape[1]), whole(heads), *[whole(v) for v in vectors], whole(w_qkv), whole(w_out),
        ],
        out_specs=[
            by_rows(width), by_columns, pl.BlockSpec((3, block, width), lambda g: (0, g, 0)), by_rows(width), by_columns,
            by_rows(width), by_rows(width), by_columns, by_rows(width),
        ],
        out_shape=[
            half(rows, width), half(width, rows), half(3, rows, width), half(rows, width), half(width, rows),
            jax.ShapeDtypeStruct((rows, width), jnp.float32), half(rows, width), half(width, rows), half(rows, width),
        ],
        scratch_shapes=[
            pltpu.VMEM((block, width), jnp.bfloat16), pltpu.VMEM((block, width), jnp.bfloat16),
            pltpu.VMEM((block, width), jnp.float32),
        ],
        compiler_params=pltpu.CompilerParams(vmem_limit_bytes=56 * MIB),
        name="forward",
    )(patches, cotangent, select, keys_valid, slot_rows, heads, *vectors, w_qkv, w_out)


TILE = 256
HALF = 512
RING = 8
LAG = 5
MESH = pl.DeviceIdType.MESH


def gelu_parts(x):
    cdf = 0.5 * (1.0 + lax.erf(x * 0.7071067811865476))
    slope = cdf + x * (0.3989422804014327 * jnp.exp(-0.5 * (x * x)))
    return x * cdf, slope


def norm_back(grad, gain, unit, scale):
    e = grad * gain
    return scale * (e - jnp.mean(e, axis=-1, keepdims=True) - unit * jnp.mean(e * unit, axis=-1, keepdims=True))


def column_sum(v):
    return jnp.sum(v, axis=0, keepdims=True)


def fold_heads(v, head_of):
    out = v[:HEAD_DIM]
    for h in range(1, 4):
        out = jnp.where(head_of == h, v[h * PAD : (h + 1) * PAD], out)
    return out


def backward_kernel(
    act2_h, act2_t_h, top_h, after_h, act1_t_h, kept_h, qkv_h, probs_h, mixed_t_h, w_fc1_h, w_fc2_h, w_out_h, w_qkv_h,
    patch_back_h, slot_back_h, slot_valid, heads, b_fc1, ln1_gain, ln2_gain, b_fc2,
    layer_h, patches_h, fc1_share, fc2_share, out_share, qkv_share, vectors_out,
    pool, wide, ring, core_in, first_in, second_in, last_out, last_in, gather_in, vectors, vectors_in,
    load_sem, core_sem, first_sem, second_sem, last_sem, gather_send, gather_sem, vector_sem,
):
    dp, rep = lax.axis_index("dp"), lax.axis_index("rep")
    z, x, y, core = dp // 2, lax.rem(dp, 2), rep // 2, lax.rem(rep, 2)
    place = lambda z, x, y, core: (z * 2 + x, y * 2 + core)
    core_peer = place(z, x, y, 1 - core)
    x_peer, y_peer = place(z, 1 - x, y, core), place(z, x, 1 - y, core)
    z_peers = [place(lax.rem(z + k, 4), x, y, core) for k in range(1, 4)]
    own = ((x, y), (y, x))
    peers = ((x_peer, y_peer), (y_peer, x_peer))
    width = pool.shape[1]

    barrier = pltpu.get_barrier_semaphore()
    for peer in (core_peer, x_peer, y_peer, *z_peers):
        pl.semaphore_signal(barrier, inc=1, device_id=peer, device_id_type=MESH)

    started = {}

    def load(name, source, target):
        copy = pltpu.make_async_copy(source, target, load_sem.at[len(started)])
        copy.start()
        started[name] = copy

    def loaded(*names):
        for name in names:
            started[name].wait()

    def load_chunk(j):
        columns = slice(j * width, (j + 1) * width)
        load(f"w1_{j}", w_fc1_h.at[:, columns], pool.at[3 + j % 2])
        load(f"w2_{j}", w_fc2_h.at[columns, :], pool.at[5 + j % 2])

    load("act2", act2_h, pool.at[0])
    load_chunk(0)
    load("top", top_h, pool.at[2])
    load("act2_t", act2_t_h, pool.at[1])
    vectors[...] = jnp.zeros_like(vectors)
    pl.semaphore_wait(barrier, 6)

    units = []
    for j in range(4):
        units += [("fc2", j, h) for h in range(2)] + [("fc1", j, h) for h in range(2)]
    units += [("out", 0, h) for h in range(2)]
    units += [("qkv", k, h) for k in range(3) for h in range(2)]
    share_of = {"fc1": fc1_share, "out": out_share, "qkv": qkv_share}
    even = [u for u, unit in enumerate(units) if unit[0] != "fc2"]
    finished, ticked = set(), [-1]

    def remote(source, target, send, receive, peer):
        return pltpu.make_async_remote_copy(
            src_ref=source, dst_ref=target, send_sem=send, recv_sem=receive, device_id=peer, device_id_type=MESH
        )

    def core_copy(u):
        s = u % 2
        return remote(ring.at[RING + s], core_in.at[s], core_sem.at[0, s], core_sem.at[1, s], core_peer)

    def first_copies(u):
        s = u % 4
        return [
            remote(
                ring.at[u % RING, half, 1 - own[half][0]], first_in.at[s, half],
                first_sem.at[0, s, half], first_sem.at[1, s, half], peers[half][0],
            )
            for half in range(2)
        ]

    def second_copies(u):
        s = u % 4
        return [
            remote(
                ring.at[u % RING, half, own[half][0], 1 - own[half][1]], second_in.at[s, half],
                second_sem.at[0, s, half], second_sem.at[1, s, half], peers[half][1],
            )
            for half in range(2)
        ]

    def last_copies(u):
        s, t = u % 4, even.index(u) % 8
        return [
            remote(
                last_out.at[s, lax.rem(z + k, 4)], last_in.at[t, k - 1],
                last_sem.at[0, t, k - 1], last_sem.at[1, t, k - 1], z_peers[k - 1],
            )
            for k in range(1, 4)
        ]

    def gather_copy(u, step):
        _, j, h = units[u]
        return remote(
            last_out.at[u % 4], gather_in.at[h, step], gather_send.at[h], gather_sem.at[h, step], place(j, x, y, core)
        )

    def core_finish(u):
        if u < 0 or u in finished:
            return
        finished.add(u)
        core_copy(u).wait()
        for half in range(2):
            for i in range(2):
                ring[u % RING, half, i] += core_in[u % 2, half, i]

    def tick():
        t = ticked[0] = ticked[0] + 1
        if t < len(units):
            core_finish(t)
            for copy in first_copies(t):
                copy.start()
        if 0 <= t - 1 < len(units):
            u = t - 1
            for half, (copy, onward) in enumerate(zip(first_copies(u), second_copies(u))):
                copy.wait()
                i = own[half][0]
                ring[u % RING, half, i] += first_in[u % 4, half]
                onward.start()
        if 0 <= t - 2 < len(units):
            u = t - 2
            for half, copy in enumerate(second_copies(u)):
                copy.wait()
                i, j = own[half]
                for q in range(4):
                    last_out[u % 4, q, half] = ring[u % RING, half, i, j, q] + second_in[u % 4, half, q]
            if units[u][0] != "fc2":
                for copy in last_copies(u):
                    copy.start()
            else:
                home = units[u][1]

                @pl.when(z != home)
                def _():
                    gather_copy(u, lax.rem(home - z + 4, 4) - 1).start()

        if 0 <= t - LAG < len(units):
            u = t - LAG
            kind, j, h = units[u]
            columns = slice(h * HALF, (h + 1) * HALF)
            if kind != "fc2":
                for copy in last_copies(u):
                    copy.wait()
                s, at = even.index(u) % 8, j * width + h * HALF
                for half in range(2):
                    total = last_out[u % 4, z, half]
                    for k in range(3):
                        total = total + last_in[s, k, half]
                    share_of[kind][half * 16 : (half + 1) * 16, at : at + HALF] = total
            else:

                @pl.when(z != j)
                def _():
                    gather_copy(u, lax.rem(j - z + 4, 4) - 1).wait_send()

                @pl.when(z == j)
                def _():
                    for k in range(3):
                        gather_copy(u, k).wait_recv()
                    for q in range(4):
                        for half in range(2):
                            total = last_out[u % 4, q, half]
                            for k in range(3):
                                total = total + gather_in[h, k, q, half]
                            at = q * 32 + half * 16
                            fc2_share[at : at + 16, columns] = total

    def produce(u, left, right):
        kind, _, h = units[u]
        assert u - RING + 2 <= ticked[0]
        columns = slice(h * HALF, (h + 1) * HALF)

        def part(owner, slot):
            if kind == "fc2":
                rows = [left[pl.ds(pl.multiple_of(b * 256 + owner * 128, 128), 128), :] for b in range(4)]
            else:
                rows = [left[pl.ds(pl.multiple_of(b * 64 + owner * 32, 32), 32), :] for b in range(16)]
            product = matmul(jnp.concatenate(rows, axis=0), right[:, columns])
            for b in range(16):
                if kind == "fc2":
                    i, j, q = b // 8, b // 4 % 2, b % 4
                else:
                    q, i, j = b // 4, b // 2 % 2, b % 2
                ring[slot, 0, i, j, q] = product[b * 32 : b * 32 + 16]
                ring[slot, 1, j, i, q] = product[b * 32 + 16 : b * 32 + 32]

        part(1 - core, RING + u % 2)
        core_finish(u - 1)
        core_copy(u).start()
        part(core, u % RING)

    def row_loop(body, count=4):
        def step(r, carry):
            body(pl.ds(pl.multiple_of(r * TILE, TILE), TILE))
            return carry

        lax.fori_loop(0, count, step, 0)

    def chunk_forward(j):
        w1, w2 = pool.at[3 + j % 2], pool.at[5 + j % 2]

        def body(rows):
            total = None
            for c in range(2):
                columns = slice(c * HALF, (c + 1) * HALF)
                hidden = slice(j * width + c * HALF, j * width + (c + 1) * HALF)
                value, slope = gelu_parts(matmul(pool[0, rows, :], w1[:, columns]) + b_fc1[:, hidden])
                value = value.astype(jnp.bfloat16)
                wide[2, rows, columns] = slope
                pool[7, columns, rows] = value.T
                branch = matmul(value, w2[columns, :])
                total = branch if total is None else total + branch
            if j == 0:
                wide[1, rows, :] = total
                vectors[7:8, :] += column_sum(pool[2, rows, :].astype(jnp.float32))
            else:
                wide[1, rows, :] += total

        row_loop(body)

    def chunk_backward(j):
        w1, w2 = pool.at[3 + j % 2], pool.at[5 + j % 2]

        def body(rows):
            total = None
            for c in range(2):
                columns = slice(c * HALF, (c + 1) * HALF)
                grad = matmul_nt(pool[2, rows, :], w2[columns, :]) * wide[2, rows, columns]
                grad = grad.astype(jnp.bfloat16)
                pool[8, rows, columns] = grad
                vectors[8 + j : 9 + j, columns] += column_sum(grad.astype(jnp.float32))
                back = matmul_nt(grad, w1[:, columns])
                total = back if total is None else total + back
            if j == 0:
                wide[0, rows, :] = total
            else:
                wide[0, rows, :] += total

        row_loop(body)

    for j in range(4):
        if j == 0:
            loaded("act2", "w1_0", "w2_0", "top", "act2_t")
        else:
            loaded(f"w1_{j}", f"w2_{j}")
        if j < 3:
            load_chunk(j + 1)
        chunk_forward(j)
        if j > 0:
            tick()
        produce(4 * j, pool.at[7], pool.at[2])
        if j == 0:
            tick()
        produce(4 * j + 1, pool.at[7], pool.at[2])
        chunk_backward(j)
        tick()
        produce(4 * j + 2, pool.at[1], pool.at[8])
        produce(4 * j + 3, pool.at[1], pool.at[8])
        if j == 3:
            load("after", after_h, wide.at[2])
            load("w_out", w_out_h, pool.at[3])
            load("mixed_t", mixed_t_h, pool.at[4])
            for k in range(3):
                load(f"qkv_{k}", qkv_h.at[k], pool.at[6 + k])
            load("probs", probs_h, pool.at[1])
        tick()

    loaded("after", "w_out")

    def middle(rows):
        after = wide[2, rows, :]
        unit, scale = normed_rows(after)
        grad = wide[0, rows, :]
        vectors[5:6, :] += column_sum(grad * unit)
        vectors[6:7, :] += column_sum(grad)
        grad = pool[2, rows, :].astype(jnp.float32) + norm_back(grad, ln2_gain[...], unit, scale)
        wide[0, rows, :] = grad
        pool[2, rows, :] = ((after + (wide[1, rows, :] + b_fc2[...])) * slot_valid[rows, :]).astype(jnp.bfloat16)
        branch = grad.astype(jnp.bfloat16)
        pool[0, rows, :] = branch
        vectors[4:5, :] += column_sum(branch.astype(jnp.float32))
        pool[5, rows, :] = matmul_nt(branch, pool[3]).astype(jnp.bfloat16)

    row_loop(middle)
    loaded("mixed_t")
    tick()
    produce(16, pool.at[4], pool.at[0])
    produce(17, pool.at[4], pool.at[0])
    tick()
    load("slot_back", slot_back_h, pool.at[3, : slot_back_h.shape[0]])
    loaded("qkv_0", "qkv_1", "qkv_2", "probs")

    def attend_back(i, carry):
        rows = pl.ds(pl.multiple_of(i * PAD, PAD), PAD)
        head_of = lax.broadcasted_iota(jnp.int32, (PAD, GROUP), 1) // HEAD_DIM
        for g in range(width // GROUP):
            lanes = slice(g * GROUP, (g + 1) * GROUP)
            grad_mixed, low_probs = pool[5, rows, lanes], pool[1, rows, lanes]
            queries = pool[6, rows, lanes]
            keys = spread_heads(pool[7, rows, lanes], heads[...])
            values = spread_heads(pool[8, rows, lanes], heads[...])
            probs = low_probs.astype(jnp.float32)
            grad_probs = matmul_nt(grad_mixed, values)
            grad_scores = probs * (grad_probs - head_sums(probs * grad_probs, heads[...]))
            grad_scores = grad_scores.astype(jnp.bfloat16)
            grad_queries = matmul(grad_scores, keys) * SCORE_SCALE
            grad_keys = fold_heads(matmul(grad_scores.T, queries), head_of) * SCORE_SCALE
            grad_values = fold_heads(matmul(low_probs.T, grad_mixed), head_of)
            pool[6, rows, lanes] = grad_queries.astype(jnp.bfloat16)
            pool[7, rows, lanes] = grad_keys.astype(jnp.bfloat16)
            pool[8, rows, lanes] = grad_values.astype(jnp.bfloat16)
        return carry

    images = width // PAD
    for part in range(4):
        lax.fori_loop(part * images // 4, (part + 1) * images // 4, attend_back, 0)
        if part == 0:
            load("act1_t", act1_t_h, pool.at[0])
        tick()
    for k, slot in enumerate((4, 5, 1)):
        load(f"w_qkv_{k}", w_qkv_h.at[:, k * width : (k + 1) * width], pool.at[slot])

    loaded("act1_t")
    for k in range(3):
        produce(18 + 2 * k, pool.at[0], pool.at[6 + k])
        produce(19 + 2 * k, pool.at[0], pool.at[6 + k])
        tick()

    loaded("slot_back")
    slots = slot_back_h.shape[0]
    pool[9, :slots, :] = matmul(pool[3, :slots, :], pool[2]).astype(jnp.bfloat16)
    load("layer", pool.at[9, :slots], layer_h)
    load("kept", kept_h, pool.at[2])
    load("patch_back", patch_back_h, pool.at[3, :slots])
    loaded("w_qkv_0", "w_qkv_1", "w_qkv_2", "kept")

    def first(rows):
        grads = [pool[6 + k, rows, :] for k in range(3)]
        vectors[2:3, :] += column_sum(grads[0].astype(jnp.float32))
        vectors[3:4, :] += column_sum(grads[2].astype(jnp.float32))
        grad = matmul_nt(grads[0], pool[4]) + matmul_nt(grads[1], pool[5]) + matmul_nt(grads[2], pool[1])
        unit, scale = normed_rows(pool[2, rows, :].astype(jnp.float32))
        vectors[0:1, :] += column_sum(grad * unit)
        vectors[1:2, :] += column_sum(grad)
        grad = wide[0, rows, :] + norm_back(grad, ln1_gain[...], unit, scale)
        for k in range(3):
            piece = grad.astype(jnp.bfloat16)
            pool[6 + k, rows, :] = piece
            grad = grad - piece.astype(jnp.float32)

    row_loop(first)
    tick()

    def vector_copies(stage):
        peers_of = {0: [core_peer], 1: [x_peer], 2: [y_peer], 3: z_peers}[stage]
        return [
            remote(vectors, vectors_in.at[stage + k], vector_sem.at[0, stage + k], vector_sem.at[1, stage + k], peer)
            for k, peer in enumerate(peers_of)
        ]

    def vector_stage(stage):
        if stage > 0:
            copies = vector_copies(stage - 1)
            for copy in copies:
                copy.wait()
            total = vectors[...]
            for k in range(len(copies)):
                total = total + vectors_in[stage - 1 + k]
            if stage == 4:
                vectors_out[...] = total
                return
            vectors[...] = total
        for copy in vector_copies(stage):
            copy.start()

    vector_stage(0)
    loaded("patch_back")
    block = 160
    for r in range(slots // block):
        rows = slice(r * block, (r + 1) * block)
        pieces = [matmul(pool[3, rows, :], pool[6 + k]) for k in (2, 1, 0)]
        wide[1, rows, :] = (pieces[0] + pieces[1]) + pieces[2]
    load("patches", wide.at[1, :slots], patches_h)
    tick()
    vector_stage(1)
    for stage in (2, 3, 4):
        tick()
        vector_stage(stage)
    while ticked[0] < len(units) - 1 + LAG:
        tick()
    loaded("layer", "patches")


def backward(tensors, vectors, back, slot_valid, heads, dp, rep):
    width = tensors[0].shape[1]
    slots = back[0].shape[0]
    any_space, vmem = pl.BlockSpec(memory_space=pl.ANY), pl.BlockSpec(memory_space=pltpu.VMEM)
    shape = jax.ShapeDtypeStruct
    f32, bf16, devices = jnp.float32, jnp.bfloat16, dp * rep
    dma = pltpu.SemaphoreType.DMA
    return pl.pallas_call(
        backward_kernel,
        in_specs=[any_space] * (len(tensors) + 2) + [vmem] * (2 + len(vectors)),
        out_specs=[any_space] * 2 + [vmem] * 5,
        out_shape=[
            shape((slots, width), bf16), shape((slots, width), f32), shape((width // devices, 4 * width), f32),
            shape((4 * width // devices, width), f32), shape((width // devices, width), f32),
            shape((width // devices, 3 * width), f32), shape((16, width), f32),
        ],
        scratch_shapes=[
            pltpu.VMEM((10, width, width), bf16), pltpu.VMEM((3, width, width), f32),
            pltpu.VMEM((RING + 2, 2, 2, 2, 4, 16, HALF), f32), pltpu.VMEM((2, 2, 2, 2, 4, 16, HALF), f32),
            pltpu.VMEM((4, 2, 2, 4, 16, HALF), f32), pltpu.VMEM((4, 2, 4, 16, HALF), f32),
            pltpu.VMEM((4, 4, 2, 16, HALF), f32), pltpu.VMEM((8, 3, 2, 16, HALF), f32),
            pltpu.VMEM((2, 3, 4, 2, 16, HALF), f32), pltpu.VMEM((16, width), f32), pltpu.VMEM((6, 16, width), f32),
            dma((32,)), dma((2, 2)), dma((2, 4, 2)), dma((2, 4, 2)), dma((2, 8, 3)), dma((2,)), dma((2, 3)), dma((2, 6)),
        ],
        compiler_params=pltpu.CompilerParams(collective_id=0, has_side_effects=True, vmem_limit_bytes=63 * MIB),
        name="backward",
    )(*tensors, *back, slot_valid, heads, *vectors)


def local_kernels(
    patches, keep, ln1_gain, ln1_bias, w_qkv, b_query, b_value, w_out, b_out, ln2_gain, ln2_bias, w_fc1, b_fc1, w_fc2,
    b_fc2, cotangent,
):
    dp, rep = lax.axis_size("dp"), lax.axis_size("rep")
    images, slots, width = patches.shape
    rows = images * slots
    table, valid = select_parts(keep, slots)
    table = jnp.pad(table, ((0, 0), (0, PAD - slots), (0, 0)))
    valid = jnp.pad(valid, ((0, 0), (0, PAD - slots)))
    same_image = jnp.eye(images)
    bf16 = jnp.bfloat16
    select = (table[:, :, :, None] * same_image[:, None, None, :]).reshape(images * PAD, rows).astype(bf16)
    select_back = (jnp.moveaxis(table, 2, 0)[:, None, :, :] * same_image[None, :, :, None]).reshape(rows, images * PAD)
    place = jnp.eye(PAD, slots)
    slot_rows = valid[:, :, None, None] * place[None, :, :, None] * same_image[:, None, None, :]
    slot_rows = slot_rows.reshape(images * PAD, rows).astype(bf16)
    slot_back = (place.T[:, None, None, :] * same_image[None, :, :, None]).reshape(rows, images * PAD).astype(bf16)
    keys_valid = jnp.tile(valid, (1, GROUP // PAD))[:, None, :]
    lane = jnp.arange(GROUP) // HEAD_DIM
    heads = (lane[:, None] == lane[None, :]).astype(bf16)
    flat = lambda a: jnp.swapaxes(a, 0, 1).reshape(rows, width)
    row = lambda v: v.reshape(1, -1)
    kept, act1_t, qkv, probs, mixed_t, after, act2, act2_t, top = forward(
        flat(patches), flat(cotangent), select, keys_valid, slot_rows, heads,
        [row(v) for v in (ln1_gain, ln1_bias, b_query, b_value, b_out, ln2_gain, ln2_bias)], w_qkv, w_out,
    )
    layer, grad_patches, fc1_share, fc2_share, out_share, qkv_share, vectors = backward(
        [act2, act2_t, top, after, act1_t, kept, qkv, probs, mixed_t, w_fc1, w_fc2, w_out, w_qkv],
        [row(v) for v in (b_fc1, ln1_gain, ln2_gain, b_fc2)],
        [select_back.astype(bf16), slot_back], valid.reshape(images * PAD, 1), heads, dp, rep,
    )
    device = lax.axis_index("dp") * rep + lax.axis_index("rep")
    share = width // (dp * rep)
    mine = lax.dynamic_slice(vectors[:8], (0, device * share), (8, share))
    hidden = lax.dynamic_slice(vectors[8:12].reshape(-1), (device * 4 * share,), (4 * share,))
    unflat = lambda a: jnp.swapaxes(a.reshape(slots, images, width), 0, 1)
    return (
        unflat(layer), unflat(grad_patches), mine[0], mine[1], qkv_share, mine[2], mine[3], out_share, mine[4], mine[5],
        mine[6], fc1_share, hidden, fc2_share, mine[7],
    )


def normalize(v):
    centred = v - jnp.mean(v, axis=-1, keepdims=True)
    return centred * lax.rsqrt(jnp.mean(centred * centred, axis=-1, keepdims=True) + NORM_EPSILON)


def affine_norm(v, gain, shift):
    return normalize(v) * gain + shift


def exchange(parts, axis, stride, count):
    size = lax.axis_size(axis)
    index = lax.axis_index(axis)
    place = (index // stride) % count
    total = lax.dynamic_index_in_dim(parts, place, 0, keepdims=False)
    for step in range(1, count):
        pairs = []
        for source in range(size):
            own = (source // stride) % count
            target = source + (((own + step) % count) - own) * stride
            pairs.append((source, target))
        sent = lax.dynamic_index_in_dim(parts, (place + step) % count, 0, keepdims=False)
        total = total + lax.ppermute(sent, axis, pairs)
    return total


def scatter_sum(grad):
    rows, columns = grad.shape
    dp, rep = lax.axis_size("dp"), lax.axis_size("rep")
    z, y = dp // 2, rep // 2
    share = rows // (dp * rep)
    parts = grad.reshape(z, 2, y, 2, share, columns)
    parts = exchange(jnp.moveaxis(parts, 3, 0), "rep", 1, 2)
    half = columns // 2
    x_first, y_first = parts[..., :half], parts[..., half:]
    x_first = exchange(jnp.moveaxis(x_first, 1, 0), "dp", 1, 2)
    y_first = exchange(jnp.moveaxis(y_first, 2, 0), "rep", 2, y)
    x_first = exchange(jnp.moveaxis(x_first, 1, 0), "rep", 2, y)
    y_first = exchange(jnp.moveaxis(y_first, 1, 0), "dp", 1, 2)
    both = jnp.concatenate([x_first, y_first], axis=-1)
    return exchange(both, "dp", 2, z)


def scatter_vectors(vectors):
    joined = jnp.concatenate([v.reshape(lax.axis_size("dp") * lax.axis_size("rep"), -1) for v in vectors], axis=1)
    total = lax.psum_scatter(joined, ("dp", "rep"), scatter_dimension=0, tiled=True)[0]
    out, start = [], 0
    for v in vectors:
        length = v.shape[0] // (lax.axis_size("dp") * lax.axis_size("rep"))
        out.append(total[start : start + length])
        start += length
    return out


def local_permutes(
    patches,
    keep,
    ln1_gain,
    ln1_bias,
    w_qkv,
    b_query,
    b_value,
    w_out,
    b_out,
    ln2_gain,
    ln2_bias,
    w_fc1,
    b_fc1,
    w_fc2,
    b_fc2,
    cotangent,
):
    images, slot_count, width = patches.shape
    row_count = images * slot_count
    table, valid_slots = select_parts(keep, slot_count)
    kept = jnp.einsum(
        "bsp,bpd->bsd", table.astype(jnp.bfloat16), patches, preferred_element_type=jnp.float32
    ).reshape(row_count, width)
    normed_one, norm_one_back = jax.vjp(affine_norm, kept, ln1_gain, ln1_bias)
    act_one = normed_one.astype(jnp.bfloat16)
    bias_all = jnp.concatenate([b_query, jnp.zeros_like(b_query), b_value])
    qkv = (matmul(act_one, w_qkv) + bias_all).astype(jnp.bfloat16)
    qkv = qkv.reshape(images, slot_count, 3, HEADS, HEAD_DIM)
    queries, key_part, values = (qkv[:, :, 0], qkv[:, :, 1], qkv[:, :, 2])
    scores = (
        jnp.einsum("blhe,bmhe->bhlm", queries, key_part, preferred_element_type=jnp.float32)
        * SCORE_SCALE
    )
    scores = jnp.where(valid_slots[:, None, None, :] > 0, scores, -1000000000.0)
    attn_probs, softmax_back = jax.vjp(partial(jax.nn.softmax, axis=-1), scores)
    probs_low = attn_probs.astype(jnp.bfloat16)
    mixed_heads = jnp.einsum(
        "bhlm,bmhe->blhe", probs_low, values, preferred_element_type=jnp.float32
    )
    mixed_heads = mixed_heads.reshape(row_count, width).astype(jnp.bfloat16)
    after_attn = kept + (matmul(mixed_heads, w_out) + b_out)
    normed_two, norm_two_back = jax.vjp(affine_norm, after_attn, ln2_gain, ln2_bias)
    act_two = normed_two.astype(jnp.bfloat16)
    pre_gelu = matmul(act_two, w_fc1) + b_fc1
    gelu_full, gelu_back = jax.vjp(partial(jax.nn.gelu, approximate=False), pre_gelu)
    gelu_out = gelu_full.astype(jnp.bfloat16)
    mlp_out = matmul(gelu_out, w_fc2) + b_fc2
    row_mask = valid_slots.reshape(row_count, 1)
    layer_out = ((after_attn + mlp_out) * row_mask).astype(jnp.bfloat16)
    layer_out = layer_out.reshape(images, slot_count, width)
    grad_out = cotangent.astype(jnp.float32).reshape(row_count, width) * row_mask
    grad_top = grad_out.astype(jnp.bfloat16)
    grad_w_fc2 = matmul(gelu_out.T, grad_top)
    grad_b_fc2 = jnp.sum(grad_top.astype(jnp.float32), axis=0)
    (grad_pre_full,) = gelu_back(matmul(grad_top, w_fc2.T))
    grad_pre = grad_pre_full.astype(jnp.bfloat16)
    grad_w_fc1 = matmul(act_two.T, grad_pre)
    grad_b_fc1 = jnp.sum(grad_pre.astype(jnp.float32), axis=0)
    grad_norm_two, grad_ln2_gain, grad_ln2_bias = norm_two_back(matmul(grad_pre, w_fc1.T))
    grad_after = grad_out + grad_norm_two
    share_w_fc2 = scatter_sum(grad_w_fc2)
    share_w_fc1 = scatter_sum(grad_w_fc1)
    grad_branch = grad_after.astype(jnp.bfloat16)
    grad_w_out = matmul(mixed_heads.T, grad_branch)
    grad_b_out = jnp.sum(grad_branch.astype(jnp.float32), axis=0)
    grad_mixed = matmul(grad_branch, w_out.T).astype(jnp.bfloat16)
    grad_mixed = grad_mixed.reshape(images, slot_count, HEADS, HEAD_DIM)
    grad_probs = jnp.einsum(
        "blhe,bmhe->bhlm", grad_mixed, values, preferred_element_type=jnp.float32
    )
    grad_values = jnp.einsum(
        "bhlm,blhe->bmhe", probs_low, grad_mixed, preferred_element_type=jnp.float32
    )
    (grad_scores_full,) = softmax_back(grad_probs)
    grad_scores = grad_scores_full.astype(jnp.bfloat16)
    grad_queries = (
        jnp.einsum("bhlm,bmhe->blhe", grad_scores, key_part, preferred_element_type=jnp.float32)
        * SCORE_SCALE
    )
    grad_keys = (
        jnp.einsum("bhlm,blhe->bmhe", grad_scores, queries, preferred_element_type=jnp.float32)
        * SCORE_SCALE
    )
    grad_qkv = jnp.stack([grad_queries, grad_keys, grad_values], axis=2)
    grad_qkv = grad_qkv.reshape(row_count, 3 * width).astype(jnp.bfloat16)
    grad_w_qkv = matmul(act_one.T, grad_qkv)
    column_sums = jnp.sum(grad_qkv.astype(jnp.float32), axis=0)
    grad_b_query = column_sums[:width]
    grad_b_value = column_sums[2 * width :]
    grad_norm_one, grad_ln1_gain, grad_ln1_bias = norm_one_back(matmul(grad_qkv, w_qkv.T))
    grad_kept = grad_after + grad_norm_one
    share_w_out = scatter_sum(grad_w_out)
    share_w_qkv = scatter_sum(grad_w_qkv)
    small = scatter_vectors(
        [grad_ln1_gain, grad_ln1_bias, grad_b_query, grad_b_value, grad_b_out, grad_ln2_gain, grad_ln2_bias, grad_b_fc1, grad_b_fc2]
    )
    grad_patches = jnp.einsum(
        "bsp,bsd->bpd",
        table,
        grad_kept.reshape(images, slot_count, width),
        precision=lax.Precision.HIGHEST,
    )
    return (
        layer_out,
        grad_patches,
        small[0],
        small[1],
        share_w_qkv,
        small[2],
        small[3],
        share_w_out,
        small[4],
        small[5],
        small[6],
        share_w_fc1,
        small[7],
        share_w_fc2,
        small[8],
    )


def solution(mesh):
    in_specs = (
        P(("dp", "rep"), None, None),
        P(("dp", "rep"), None),
        P(),
        P(),
        P(),
        P(),
        P(),
        P(),
        P(),
        P(),
        P(),
        P(),
        P(),
        P(),
        P(),
        P(("dp", "rep"), None, None),
    )
    out_specs = (
        P(("dp", "rep"), None, None),
        P(("dp", "rep"), None, None),
        P(("dp", "rep")),
        P(("dp", "rep")),
        P(("dp", "rep"), None),
        P(("dp", "rep")),
        P(("dp", "rep")),
        P(("dp", "rep"), None),
        P(("dp", "rep")),
        P(("dp", "rep")),
        P(("dp", "rep")),
        P(("dp", "rep"), None),
        P(("dp", "rep")),
        P(("dp", "rep"), None),
        P(("dp", "rep")),
    )
    fits = mesh.shape["dp"] == 8 and mesh.shape["rep"] == 4
    local = local_kernels if fits else local_permutes
    return jax.shard_map(local, mesh=mesh, in_specs=in_specs, out_specs=out_specs, check_vma=False)
```

```python
from functools import partial

import jax
import jax.numpy as jnp
from jax import lax
from jax.experimental import pallas as pl
from jax.experimental.pallas import tpu as pltpu
from jax.sharding import PartitionSpec as P

HEADS = 16
HEAD_DIM = 64
NORM_EPSILON = 1e-06
SCORE_SCALE = 0.125
PAD = 64
GROUP = 256
MIB = 1 << 20
NT = (((1,), (1,)), ((), ()))


def select_parts(keep, slot_count):
    slot_ids = jnp.arange(slot_count, dtype=jnp.int32)
    ranks = jnp.cumsum(keep, axis=1) - 1
    table = (ranks[:, None, :] == slot_ids[None, :, None]) & (keep[:, None, :] == 1)
    counts = jnp.sum(keep, axis=1)
    valid_slots = (slot_ids[None, :] < counts[:, None]).astype(jnp.float32)
    return (table.astype(jnp.float32), valid_slots)


def matmul(left, right):
    return jnp.dot(left, right, preferred_element_type=jnp.float32)


def matmul_nt(left, right):
    return lax.dot_general(left, right, NT, preferred_element_type=jnp.float32)


def normed_rows(v):
    centred = v - jnp.mean(v, axis=-1, keepdims=True)
    scale = lax.rsqrt(jnp.mean(centred * centred, axis=-1, keepdims=True) + NORM_EPSILON)
    return centred * scale, scale


def head_mask():
    row = lax.broadcasted_iota(jnp.int32, (GROUP, GROUP), 0) // HEAD_DIM
    lane = lax.broadcasted_iota(jnp.int32, (GROUP, GROUP), 1) // HEAD_DIM
    return jnp.where(row == lane, 1.0, 0.0).astype(jnp.bfloat16)


def spread_heads(v, heads):
    return jnp.concatenate([v] * 4, axis=0) * heads


def fold_heads(v, head_of):
    out = v[:PAD]
    for h in range(1, 4):
        out = jnp.where(head_of == h, v[h * PAD : (h + 1) * PAD], out)
    return out


def forward_kernel(
    counts, patches, cotangent, keys, ln1_gain, ln1_bias, b_query, b_value, b_out, ln2_gain, ln2_bias,
    w_qkv, w_out, kept_out, act1_t_out, qkv_out, probs_out, mixed_t_out, after_out, act2_out, act2_t_out, top_out,
    act1, mixed, kept, heads,
):
    width = patches.shape[1]
    block = kept.shape[0]
    images = block // PAD
    step = pl.program_id(0)
    heads[...] = head_mask()

    def select(which):
        row = lax.broadcasted_iota(jnp.int32, (block, patches.shape[0]), 0) + step * block
        return jnp.where(row == keys[which : which + 1, :], 1.0, 0.0).astype(jnp.bfloat16)

    kept[...] = matmul(select(0), patches[...])
    kept_out[...] = kept[...].astype(jnp.bfloat16)
    unit, _ = normed_rows(kept[...])
    act1[...] = (unit * ln1_gain[...] + ln1_bias[...]).astype(jnp.bfloat16)
    top_out[...] = matmul(select(1), cotangent[...]).astype(jnp.bfloat16)
    act1_t_out[...] = act1[...].T
    qkv_out[0] = (matmul(act1[...], w_qkv[:, :width]) + b_query[...]).astype(jnp.bfloat16)
    qkv_out[1] = matmul(act1[...], w_qkv[:, width : 2 * width]).astype(jnp.bfloat16)
    qkv_out[2] = (matmul(act1[...], w_qkv[:, 2 * width :]) + b_value[...]).astype(jnp.bfloat16)

    def attend(i, carry):
        rows = pl.ds(pl.multiple_of(i * PAD, PAD), PAD)
        row = lax.broadcasted_iota(jnp.int32, (PAD, GROUP), 0)
        head_of = lax.broadcasted_iota(jnp.int32, (PAD, GROUP), 1) // HEAD_DIM
        seen = row < counts[step * images + i]
        for g in range(width // GROUP):
            lanes = slice(g * GROUP, (g + 1) * GROUP)
            queries = spread_heads(qkv_out[0, rows, lanes], heads[...])
            scores = matmul_nt(qkv_out[1, rows, lanes], queries) * SCORE_SCALE
            scores = jnp.where(seen, scores, -1000000000.0)
            raised = jnp.exp(scores - jnp.max(scores, axis=0, keepdims=True))
            probs = (raised * (1.0 / jnp.sum(raised, axis=0, keepdims=True))).astype(jnp.bfloat16)
            probs_out[rows, lanes] = probs
            mixed[rows, lanes] = fold_heads(matmul(probs.T, qkv_out[2, rows, lanes]), head_of).astype(jnp.bfloat16)
        return carry

    lax.fori_loop(0, images, attend, 0, unroll=True)
    mixed_t_out[...] = mixed[...].T
    after = kept[...] + (matmul(mixed[...], w_out[...]) + b_out[...])
    after_out[...] = after
    unit, _ = normed_rows(after)
    act2 = (unit * ln2_gain[...] + ln2_bias[...]).astype(jnp.bfloat16)
    act2_out[...] = act2
    act2_t_out[...] = act2.T


def forward(counts, patches, cotangent, keys, vectors, w_qkv, w_out):
    width = patches.shape[1]
    images = counts.shape[0]
    step = 4
    rows, block = images * PAD, step * PAD
    half = lambda *shape: jax.ShapeDtypeStruct(shape, jnp.bfloat16)
    whole = lambda a: pl.BlockSpec(a.shape, lambda g: (0,) * a.ndim, pipeline_mode=pl.Buffered(1))
    by_rows = pl.BlockSpec((block, width), lambda g: (g, 0))
    by_columns = pl.BlockSpec((width, block), lambda g: (0, g))
    return pl.pallas_call(
        forward_kernel,
        grid=(images // step,),
        in_specs=[
            pl.BlockSpec(memory_space=pltpu.SMEM), whole(patches), whole(cotangent), whole(keys),
            *[whole(v) for v in vectors], whole(w_qkv), whole(w_out),
        ],
        out_specs=[
            by_rows, by_columns, pl.BlockSpec((3, block, width), lambda g: (0, g, 0)), by_rows, by_columns,
            by_rows, by_rows, by_columns, by_rows,
        ],
        out_shape=[
            half(rows, width), half(width, rows), half(3, rows, width), half(rows, width), half(width, rows),
            jax.ShapeDtypeStruct((rows, width), jnp.float32), half(rows, width), half(width, rows), half(rows, width),
        ],
        scratch_shapes=[
            pltpu.VMEM((block, width), jnp.bfloat16), pltpu.VMEM((block, width), jnp.bfloat16),
            pltpu.VMEM((block, width), jnp.float32), pltpu.VMEM((GROUP, GROUP), jnp.bfloat16),
        ],
        compiler_params=pltpu.CompilerParams(vmem_limit_bytes=56 * MIB),
        name="forward",
    )(counts, patches, cotangent, keys, *vectors, w_qkv, w_out)


TILE = 256
HALF = 512
RING = 11
SENDS, TAKES = 3, 4
STAGES = 4
FIRSTS, LATERS = 4, 8
PLAN = (
    (), (), (), (), ((0, 0), (1, 0)), (), (), ((0, 1),), ((2, 0),), ((1, 1), (3, 0)), ((0, 2),), (), ((2, 1), (4,
    0)), ((0, 3), (1, 2)), (), ((2, 2), (3, 1), (5, 0)), (), ((0, 4), (2, 3), (4, 1), (6, 0)), (), ((1, 3),), ((4,
    2), (5, 1), (3, 2), (7, 0)), ((2, 4), (6, 1), (8, 0)), ((1, 4), (4, 3), (5, 2)), ((3, 3),), (), ((6, 2), (7, 1),
    (9, 0)), (), ((4, 4), (5, 3)), ((3, 4), (6, 3), (8, 1), (10, 0)), ((7, 2), (8, 2), (9, 1), (11, 0)), ((5, 4),),
    ((6, 4),), ((10, 1), (7, 3), (12, 0)), ((8, 3), (9, 2)), (), (), ((7, 4), (10, 2), (11, 1), (13, 0)), ((8, 4),
    (9, 3), (10, 3), (12, 1), (14, 0)), ((11, 2), (13, 1), (15, 0)), ((9, 4), (12, 2)), ((10, 4),), ((14, 1), (16,
    0)), ((11, 3),), ((12, 3),), ((13, 2), (14, 2), (15, 1), (17, 0), (11, 4)), ((16, 1), (18, 0), (12, 4)), ((14,
    3),), ((13, 3), (17, 1), (19, 0)), ((15, 2), (18, 1), (20, 0)), ((14, 4), (16, 2), (15, 3), (19, 1), (21, 0)),
    ((13, 4), (20, 1), (22, 0), (16, 3)), ((17, 2), (21, 1), (23, 0), (18, 2)), ((15, 4), (22, 1), (17, 3), (19,
    2)), ((23, 1), (18, 3), (19, 3), (20, 2)), ((16, 4), (20, 3), (21, 2), (21, 3), (22, 2), (17, 4), (22, 3), (23,
    2), (18, 4), (19, 4), (23, 3), (20, 4), (21, 4), (22, 4), (23, 4)),
)
MESH = pl.DeviceIdType.MESH


def gelu_parts(x):
    cdf = 0.5 * (1.0 + lax.erf(x * 0.7071067811865476))
    slope = cdf + x * (0.3989422804014327 * jnp.exp(-0.5 * (x * x)))
    return x * cdf, slope


def norm_back(grad, gain, unit, scale):
    e = grad * gain
    return scale * (e - jnp.mean(e, axis=-1, keepdims=True) - unit * jnp.mean(e * unit, axis=-1, keepdims=True))


def column_sum(v):
    return jnp.sum(v, axis=0, keepdims=True)


def backward_kernel(
    act2_h, act2_t_h, top_h, after_h, act1_t_h, kept_h, qkv_h, probs_h, mixed_t_h, w_fc1_h, w_fc2_h, w_out_h, w_qkv_h,
    keys, b_fc1, ln1_gain, ln2_gain, b_fc2,
    layer_h, patches_h, fc1_share, fc2_share, out_share, qkv_share, vectors_out,
    pool, wide, ring, core_in, first_in, second_in, third_in, fourth_in, home_in, vectors, vectors_in, heads,
    load_sem, core_sem, stage_sem, home_sem, vector_sem,
):
    dp, rep = lax.axis_index("dp"), lax.axis_index("rep")
    far, near = dp // 4, lax.rem(dp // 2, 2)
    x, y, core = lax.rem(dp, 2), rep // 2, lax.rem(rep, 2)
    place = lambda far, near, x, y, core: (far * 4 + near * 2 + x, y * 2 + core)
    axes = {
        "c": (core, place(far, near, x, y, 1 - core)),
        "x": (x, place(far, near, 1 - x, y, core)),
        "y": (y, place(far, near, x, 1 - y, core)),
        "near": (near, place(far, 1 - near, x, y, core)),
        "far": (far, place(1 - far, near, x, y, core)),
    }
    spread_orders = (("x", "near", "y", "far"), ("y", "near", "x", "far"))
    home_orders = (("x", "y", "near", "far"), ("y", "x", "near", "far"))
    width = pool.shape[1]

    barrier = pltpu.get_barrier_semaphore()
    for _, peer in axes.values():
        pl.semaphore_signal(barrier, inc=1, device_id=peer, device_id_type=MESH)

    started = {}

    def load(name, source, target):
        copy = pltpu.make_async_copy(source, target, load_sem.at[len(started)])
        copy.start()
        started[name] = copy

    def loaded(*names):
        for name in names:
            started[name].wait()

    def load_chunk(j):
        columns = slice(j * width, (j + 1) * width)
        load(f"w1_{j}", w_fc1_h.at[:, columns], pool.at[3 + j % 2])
        load(f"w2_{j}", w_fc2_h.at[columns, :], pool.at[5 + j % 2])

    load("act2", act2_h, pool.at[0])
    load_chunk(0)
    load("top", top_h, pool.at[2])
    load("act2_t", act2_t_h, pool.at[1])
    vectors[...] = jnp.zeros_like(vectors)
    heads[...] = head_mask()
    pl.semaphore_wait(barrier, len(axes))

    units = []
    for j in range(4):
        units += [("fc2", j, h) for h in range(2)] + [("fc1", j, h) for h in range(2)]
    units += [("out", 0, h) for h in range(2)]
    units += [("qkv", k, h) for k in range(3) for h in range(2)]
    share_of = {"fc1": fc1_share, "out": out_share, "qkv": qkv_share}
    finished, delivered, pumped = set(), set(), []

    def remote(source, target, send, receive, peer):
        return pltpu.make_async_remote_copy(
            src_ref=source, dst_ref=target, send_sem=send, recv_sem=receive, device_id=peer, device_id_type=MESH
        )

    def core_copy(u):
        s, t = u % SENDS, u % TAKES
        return remote(ring.at[RING + s], core_in.at[t], core_sem.at[0, t], core_sem.at[1, t], axes["c"][1])

    def orders_of(u):
        return home_orders if units[u][0] == "fc2" else spread_orders

    def kept(u, half, stage):
        return (u % RING, half, *(axes[name][0] for name in orders_of(u)[half][:stage]))

    def landing(u, half, stage):
        if stage == 0:
            return first_in, (u % FIRSTS, half)
        return (second_in, third_in, fourth_in)[stage - 1], (u % LATERS, half)

    def stage_copy(u, half, stage):
        index, peer = axes[orders_of(u)[half][stage]]
        target, at = landing(u, half, stage)
        slot = stage * LATERS + at[0]
        return remote(
            ring.at[(*kept(u, half, stage), 1 - index)], target.at[at],
            stage_sem.at[0, slot, half], stage_sem.at[1, slot, half], peer,
        )

    def home_copy(u, half, stage):
        _, j, h = units[u]
        slot = h if stage == 2 else 2 + h
        return remote(
            ring.at[kept(u, half, 2)], home_in.at[slot, half], home_sem.at[0, slot, half], home_sem.at[1, slot, half],
            axes["near" if stage == 2 else "far"][1],
        )

    def home_roles(u, stage):
        j = units[u][1]
        if stage == 2:
            return near != j % 2, near == j % 2
        return (near == j % 2) & (far != j // 2), (near == j % 2) & (far == j // 2)

    def stage_start(u, half, stage):
        if units[u][0] == "fc2" and stage >= 2:

            @pl.when(home_roles(u, stage)[0])
            def _():
                home_copy(u, half, stage).start()
        else:
            stage_copy(u, half, stage).start()

    def stage_finish(u, half, stage):
        if units[u][0] == "fc2" and stage >= 2:
            sends, takes = home_roles(u, stage)
            copy = home_copy(u, half, stage)

            @pl.when(sends)
            def _():
                copy.wait_send()

            @pl.when(takes)
            def _():
                copy.wait_recv()
                j, h = units[u][1:]
                slot = h if stage == 2 else 2 + h
                ring[kept(u, half, 2)] += home_in[slot, half]
        else:
            stage_copy(u, half, stage).wait()
            source, at = landing(u, half, stage)
            ring[kept(u, half, stage + 1)] += source[at]

    def deliver(u):
        kind, j, h = units[u]
        if kind == "fc2":

            @pl.when((near == j % 2) & (far == j // 2))
            def _():
                for half in range(2):
                    for q in range(4):
                        at = q * 32 + half * 16
                        fc2_share[at : at + 16, h * HALF : (h + 1) * HALF] = ring[(*kept(u, half, 2), q // 2, q % 2)]
        else:
            at = j * width + h * HALF
            for half in range(2):
                share_of[kind][half * 16 : (half + 1) * 16, at : at + HALF] = ring[kept(u, half, 4)]

    def core_finish(u):
        if u < 0 or u in finished:
            return
        finished.add(u)
        core_copy(u).wait()
        for half in range(2):
            for i in range(2):
                ring[u % RING, half, i] += core_in[u % TAKES, half, i]

    def pump():
        for u, k in PLAN[len(pumped)]:
            if k == 0:
                core_finish(u)
            for half in range(2):
                if k > 0:
                    stage_finish(u, half, k - 1)
                if k < STAGES:
                    stage_start(u, half, k)
            if k == STAGES:
                deliver(u)
                delivered.add(u)
        pumped.append(True)

    def produce(u, left, right):
        kind, _, h = units[u]
        assert u < RING or u - RING in delivered
        columns = slice(h * HALF, (h + 1) * HALF)

        def part(owner, slot):
            if kind == "fc2":
                rows = [left[pl.ds(pl.multiple_of(b * 256 + owner * 128, 128), 128), :] for b in range(4)]
            else:
                rows = [left[pl.ds(pl.multiple_of(b * 64 + owner * 32, 32), 32), :] for b in range(16)]
            product = matmul(jnp.concatenate(rows, axis=0), right[:, columns])
            for b in range(16):
                if kind == "fc2":
                    names = {"x": b // 8, "y": b // 4 % 2, "near": b // 2 % 2, "far": b % 2}
                else:
                    names = {"far": b // 8, "near": b // 4 % 2, "x": b // 2 % 2, "y": b % 2}
                for half, order in enumerate(orders_of(u)):
                    at = b * 32 + half * 16
                    ring[(slot, half, *(names[name] for name in order))] = product[at : at + 16]

        core_finish(u - TAKES // 2)
        part(1 - core, RING + u % SENDS)
        core_copy(u).start()
        part(core, u % RING)
        pump()

    def row_loop(body):
        def step(r, carry):
            body(pl.ds(pl.multiple_of(r * TILE, TILE), TILE))
            return carry

        parts = width // TILE // 2
        for part in range(2):
            lax.fori_loop(part * parts, (part + 1) * parts, step, 0)
            pump()

    def chunk_forward(j):
        w1 = pool.at[3 + j % 2]

        def body(rows):
            for c in range(2):
                columns = slice(c * HALF, (c + 1) * HALF)
                hidden = slice(j * width + c * HALF, j * width + (c + 1) * HALF)
                value, slope = gelu_parts(matmul(pool[0, rows, :], w1[:, columns]) + b_fc1[:, hidden])
                value = value.astype(jnp.bfloat16)
                wide[2, rows, columns] = slope
                pool[8, rows, columns] = value
                pool[7, columns, rows] = value.T

        row_loop(body)

    def chunk_backward(j):
        w1, w2 = pool.at[3 + j % 2], pool.at[5 + j % 2]

        def body(rows):
            branch = matmul(pool[8, rows, :], w2[...])
            if j == 0:
                wide[1, rows, :] = branch
                vectors[7:8, :] += column_sum(pool[2, rows, :].astype(jnp.float32))
            else:
                wide[1, rows, :] += branch
            total = None
            for c in range(2):
                columns = slice(c * HALF, (c + 1) * HALF)
                grad = matmul_nt(pool[2, rows, :], w2[columns, :]) * wide[2, rows, columns]
                grad = grad.astype(jnp.bfloat16)
                pool[8, rows, columns] = grad
                vectors[8 + j : 9 + j, columns] += column_sum(grad.astype(jnp.float32))
                back = matmul_nt(grad, w1[:, columns])
                total = back if total is None else total + back
            if j == 0:
                wide[0, rows, :] = total
            else:
                wide[0, rows, :] += total

        row_loop(body)

    for j in range(4):
        loaded(*(("act2", "w1_0") if j == 0 else (f"w1_{j}",)))
        if j < 3:
            load_chunk(j + 1)
        else:
            load("w_out", w_out_h, pool.at[3])
            load("mixed_t", mixed_t_h, pool.at[5])
        chunk_forward(j)
        if j == 0:
            loaded("top")
        produce(4 * j, pool.at[7], pool.at[2])
        produce(4 * j + 1, pool.at[7], pool.at[2])
        if j == 0:
            loaded("act2_t")
        loaded(f"w2_{j}")
        chunk_backward(j)
        if j == 3:
            load("after", after_h, wide.at[2])
            for k in range(2):
                load(f"qkv_{k}", qkv_h.at[k], pool.at[6 + k])
        produce(4 * j + 2, pool.at[1], pool.at[8])
        produce(4 * j + 3, pool.at[1], pool.at[8])
        if j == 3:
            load("qkv_2", qkv_h.at[2], pool.at[8])
            load("probs", probs_h, pool.at[1])

    loaded("after", "w_out")

    def middle(rows):
        after = wide[2, rows, :]
        unit, scale = normed_rows(after)
        grad = wide[0, rows, :]
        vectors[5:6, :] += column_sum(grad * unit)
        vectors[6:7, :] += column_sum(grad)
        grad = pool[2, rows, :].astype(jnp.float32) + norm_back(grad, ln2_gain[...], unit, scale)
        wide[0, rows, :] = grad
        pool[2, rows, :] = (after + (wide[1, rows, :] + b_fc2[...])).astype(jnp.bfloat16)
        branch = grad.astype(jnp.bfloat16)
        pool[0, rows, :] = branch
        vectors[4:5, :] += column_sum(branch.astype(jnp.float32))
        pool[4, rows, :] = matmul_nt(branch, pool[3]).astype(jnp.bfloat16)

    row_loop(middle)
    loaded("mixed_t")
    load("w_qkv_0", w_qkv_h.at[:, :width], pool.at[3])
    produce(16, pool.at[5], pool.at[0])
    produce(17, pool.at[5], pool.at[0])
    load("w_qkv_1", w_qkv_h.at[:, width : 2 * width], pool.at[5])
    load("act1_t", act1_t_h, pool.at[0])
    loaded("qkv_0", "qkv_1", "qkv_2", "probs")

    def attend_back(i, carry):
        rows = pl.ds(pl.multiple_of(i * PAD, PAD), PAD)
        head_of = lax.broadcasted_iota(jnp.int32, (PAD, GROUP), 1) // HEAD_DIM
        for g in range(width // GROUP):
            lanes = slice(g * GROUP, (g + 1) * GROUP)
            queries = spread_heads(pool[6, rows, lanes], heads[...])
            keys, values = pool[7, rows, lanes], pool[8, rows, lanes]
            grad_mixed = spread_heads(pool[4, rows, lanes], heads[...])
            low_probs = pool[1, rows, lanes]
            probs = low_probs.astype(jnp.float32)
            grad_probs = matmul_nt(values, grad_mixed)
            grad_scores = probs * (grad_probs - column_sum(probs * grad_probs))
            grad_scores = grad_scores.astype(jnp.bfloat16)
            grad_queries = fold_heads(matmul(grad_scores.T, keys), head_of) * SCORE_SCALE
            grad_keys = matmul(grad_scores, queries) * SCORE_SCALE
            grad_values = matmul(low_probs, grad_mixed)
            pool[6, rows, lanes] = grad_queries.astype(jnp.bfloat16)
            pool[7, rows, lanes] = grad_keys.astype(jnp.bfloat16)
            pool[8, rows, lanes] = grad_values.astype(jnp.bfloat16)
        return carry

    images = width // PAD
    for part in range(4):
        lax.fori_loop(part * images // 4, (part + 1) * images // 4, attend_back, 0)
        pump()
    load("w_qkv_2", w_qkv_h.at[:, 2 * width :], pool.at[4])

    slots, block = layer_h.shape[0], 160

    def select_rows(r, column):
        rows = slice(r * block, (r + 1) * block)
        lane = lax.broadcasted_iota(jnp.int32, (block, width), 1)
        return rows, jnp.where(lane == keys[rows, column : column + 1], 1.0, 0.0).astype(jnp.bfloat16)

    for r in range(slots // block):
        rows, select = select_rows(r, 1)
        pool[1, rows, :] = matmul(select, pool[2]).astype(jnp.bfloat16)
    load("layer", pool.at[1, :slots], layer_h)
    load("kept", kept_h, pool.at[2])
    pump()

    loaded("act1_t")
    for k in range(3):
        produce(18 + 2 * k, pool.at[0], pool.at[6 + k])
        produce(19 + 2 * k, pool.at[0], pool.at[6 + k])

    loaded("w_qkv_0", "w_qkv_1", "w_qkv_2", "kept")

    def first(rows):
        grads = [pool[6 + k, rows, :] for k in range(3)]
        vectors[2:3, :] += column_sum(grads[0].astype(jnp.float32))
        vectors[3:4, :] += column_sum(grads[2].astype(jnp.float32))
        grad = matmul_nt(grads[0], pool[3]) + matmul_nt(grads[1], pool[5]) + matmul_nt(grads[2], pool[4])
        unit, scale = normed_rows(pool[2, rows, :].astype(jnp.float32))
        vectors[0:1, :] += column_sum(grad * unit)
        vectors[1:2, :] += column_sum(grad)
        grad = wide[0, rows, :] + norm_back(grad, ln1_gain[...], unit, scale)
        for k in range(3):
            piece = grad.astype(jnp.bfloat16)
            pool[6 + k, rows, :] = piece
            grad = grad - piece.astype(jnp.float32)

    row_loop(first)

    def vector_copy(stage):
        peer = axes[("c", "x", "y", "near", "far")[stage]][1]
        return remote(vectors, vectors_in.at[stage], vector_sem.at[0, stage], vector_sem.at[1, stage], peer)

    def vector_stage(stage):
        if stage > 0:
            vector_copy(stage - 1).wait()
            total = vectors[...] + vectors_in[stage - 1]
            if stage == 5:
                vectors_out[...] = total
                return
            vectors[...] = total
        vector_copy(stage).start()

    vector_stage(0)
    for r in range(slots // block):
        rows, select = select_rows(r, 0)
        pieces = [matmul(select, pool[6 + k]) for k in (2, 1, 0)]
        wide[1, rows, :] = (pieces[0] + pieces[1]) + pieces[2]
    load("patches", wide.at[1, :slots], patches_h)
    pump()
    for stage in (1, 2, 3, 4, 5):
        vector_stage(stage)
        pump()
    assert len(delivered) == len(units)
    loaded("layer", "patches")


def backward(tensors, vectors, keys, dp, rep):
    width = tensors[0].shape[1]
    slots = keys.shape[0]
    any_space, vmem = pl.BlockSpec(memory_space=pl.ANY), pl.BlockSpec(memory_space=pltpu.VMEM)
    shape = jax.ShapeDtypeStruct
    f32, bf16, devices = jnp.float32, jnp.bfloat16, dp * rep
    dma = pltpu.SemaphoreType.DMA
    piece = (16, HALF)
    return pl.pallas_call(
        backward_kernel,
        in_specs=[any_space] * len(tensors) + [vmem] * (1 + len(vectors)),
        out_specs=[any_space] * 2 + [vmem] * 5,
        out_shape=[
            shape((slots, width), bf16), shape((slots, width), f32), shape((width // devices, 4 * width), f32),
            shape((4 * width // devices, width), f32), shape((width // devices, width), f32),
            shape((width // devices, 3 * width), f32), shape((16, width), f32),
        ],
        scratch_shapes=[
            pltpu.VMEM((9, width, width), bf16), pltpu.VMEM((3, width, width), f32),
            pltpu.VMEM((RING + SENDS, 2, 2, 2, 2, 2, *piece), f32), pltpu.VMEM((TAKES, 2, 2, 2, 2, 2, *piece), f32),
            pltpu.VMEM((FIRSTS, 2, 2, 2, 2, *piece), f32), pltpu.VMEM((LATERS, 2, 2, 2, *piece), f32),
            pltpu.VMEM((LATERS, 2, 2, *piece), f32), pltpu.VMEM((LATERS, 2, *piece), f32),
            pltpu.VMEM((4, 2, 2, 2, *piece), f32), pltpu.VMEM((16, width), f32), pltpu.VMEM((5, 16, width), f32),
            pltpu.VMEM((GROUP, GROUP), bf16),
            dma((32,)), dma((2, TAKES)), dma((2, 4 * LATERS, 2)), dma((2, 4, 2)), dma((2, 5)),
        ],
        compiler_params=pltpu.CompilerParams(collective_id=0, has_side_effects=True, vmem_limit_bytes=63 * MIB),
        name="backward",
    )(*tensors, keys, *vectors)


def local_kernels(
    patches, keep, ln1_gain, ln1_bias, w_qkv, b_query, b_value, w_out, b_out, ln2_gain, ln2_bias, w_fc1, b_fc1, w_fc2,
    b_fc2, cotangent,
):
    dp, rep = lax.axis_size("dp"), lax.axis_size("rep")
    images, slots, width = patches.shape
    rows = images * slots
    kept = keep.T
    image = jnp.arange(images, dtype=jnp.int32) * PAD
    ids = jnp.arange(slots, dtype=jnp.int32)[:, None]
    upto = (ids >= ids.T).astype(jnp.float32)
    ranks = matmul(upto, kept.astype(jnp.float32)).astype(jnp.int32)
    counts = ranks[-1]
    keys = jnp.stack([
        jnp.where(kept == 1, image + ranks - 1, -1), jnp.where(ids < counts, image + ids, -1)
    ]).reshape(2, rows)
    flat = lambda a: jnp.swapaxes(a, 0, 1).reshape(rows, width)
    row = lambda v: v.reshape(1, -1)
    kept, act1_t, qkv, probs, mixed_t, after, act2, act2_t, top = forward(
        counts, flat(patches), flat(cotangent), keys,
        [row(v) for v in (ln1_gain, ln1_bias, b_query, b_value, b_out, ln2_gain, ln2_bias)], w_qkv, w_out,
    )
    layer, grad_patches, fc1_share, fc2_share, out_share, qkv_share, vectors = backward(
        [act2, act2_t, top, after, act1_t, kept, qkv, probs, mixed_t, w_fc1, w_fc2, w_out, w_qkv],
        [row(v) for v in (b_fc1, ln1_gain, ln2_gain, b_fc2)], keys.T, dp, rep,
    )
    device = lax.axis_index("dp") * rep + lax.axis_index("rep")
    share = width // (dp * rep)
    mine = lax.dynamic_slice(vectors[:8], (0, device * share), (8, share))
    hidden = lax.dynamic_slice(vectors[8:12].reshape(-1), (device * 4 * share,), (4 * share,))
    unflat = lambda a: jnp.swapaxes(a.reshape(slots, images, width), 0, 1)
    return (
        unflat(layer), unflat(grad_patches), mine[0], mine[1], qkv_share, mine[2], mine[3], out_share, mine[4], mine[5],
        mine[6], fc1_share, hidden, fc2_share, mine[7],
    )


def normalize(v):
    centred = v - jnp.mean(v, axis=-1, keepdims=True)
    return centred * lax.rsqrt(jnp.mean(centred * centred, axis=-1, keepdims=True) + NORM_EPSILON)


def affine_norm(v, gain, shift):
    return normalize(v) * gain + shift


def exchange(parts, axis, stride, count):
    size = lax.axis_size(axis)
    index = lax.axis_index(axis)
    place = (index // stride) % count
    total = lax.dynamic_index_in_dim(parts, place, 0, keepdims=False)
    for step in range(1, count):
        pairs = []
        for source in range(size):
            own = (source // stride) % count
            target = source + (((own + step) % count) - own) * stride
            pairs.append((source, target))
        sent = lax.dynamic_index_in_dim(parts, (place + step) % count, 0, keepdims=False)
        total = total + lax.ppermute(sent, axis, pairs)
    return total


def scatter_sum(grad):
    rows, columns = grad.shape
    dp, rep = lax.axis_size("dp"), lax.axis_size("rep")
    z, y = dp // 2, rep // 2
    share = rows // (dp * rep)
    parts = grad.reshape(z, 2, y, 2, share, columns)
    parts = exchange(jnp.moveaxis(parts, 3, 0), "rep", 1, 2)
    half = columns // 2
    x_first, y_first = parts[..., :half], parts[..., half:]
    x_first = exchange(jnp.moveaxis(x_first, 1, 0), "dp", 1, 2)
    y_first = exchange(jnp.moveaxis(y_first, 2, 0), "rep", 2, y)
    x_first = exchange(jnp.moveaxis(x_first, 1, 0), "rep", 2, y)
    y_first = exchange(jnp.moveaxis(y_first, 1, 0), "dp", 1, 2)
    both = jnp.concatenate([x_first, y_first], axis=-1)
    return exchange(both, "dp", 2, z)


def scatter_vectors(vectors):
    joined = jnp.concatenate([v.reshape(lax.axis_size("dp") * lax.axis_size("rep"), -1) for v in vectors], axis=1)
    total = lax.psum_scatter(joined, ("dp", "rep"), scatter_dimension=0, tiled=True)[0]
    out, start = [], 0
    for v in vectors:
        length = v.shape[0] // (lax.axis_size("dp") * lax.axis_size("rep"))
        out.append(total[start : start + length])
        start += length
    return out


def local_permutes(
    patches,
    keep,
    ln1_gain,
    ln1_bias,
    w_qkv,
    b_query,
    b_value,
    w_out,
    b_out,
    ln2_gain,
    ln2_bias,
    w_fc1,
    b_fc1,
    w_fc2,
    b_fc2,
    cotangent,
):
    images, slot_count, width = patches.shape
    row_count = images * slot_count
    table, valid_slots = select_parts(keep, slot_count)
    kept = jnp.einsum(
        "bsp,bpd->bsd", table.astype(jnp.bfloat16), patches, preferred_element_type=jnp.float32
    ).reshape(row_count, width)
    normed_one, norm_one_back = jax.vjp(affine_norm, kept, ln1_gain, ln1_bias)
    act_one = normed_one.astype(jnp.bfloat16)
    bias_all = jnp.concatenate([b_query, jnp.zeros_like(b_query), b_value])
    qkv = (matmul(act_one, w_qkv) + bias_all).astype(jnp.bfloat16)
    qkv = qkv.reshape(images, slot_count, 3, HEADS, HEAD_DIM)
    queries, key_part, values = (qkv[:, :, 0], qkv[:, :, 1], qkv[:, :, 2])
    scores = (
        jnp.einsum("blhe,bmhe->bhlm", queries, key_part, preferred_element_type=jnp.float32)
        * SCORE_SCALE
    )
    scores = jnp.where(valid_slots[:, None, None, :] > 0, scores, -1000000000.0)
    attn_probs, softmax_back = jax.vjp(partial(jax.nn.softmax, axis=-1), scores)
    probs_low = attn_probs.astype(jnp.bfloat16)
    mixed_heads = jnp.einsum(
        "bhlm,bmhe->blhe", probs_low, values, preferred_element_type=jnp.float32
    )
    mixed_heads = mixed_heads.reshape(row_count, width).astype(jnp.bfloat16)
    after_attn = kept + (matmul(mixed_heads, w_out) + b_out)
    normed_two, norm_two_back = jax.vjp(affine_norm, after_attn, ln2_gain, ln2_bias)
    act_two = normed_two.astype(jnp.bfloat16)
    pre_gelu = matmul(act_two, w_fc1) + b_fc1
    gelu_full, gelu_back = jax.vjp(partial(jax.nn.gelu, approximate=False), pre_gelu)
    gelu_out = gelu_full.astype(jnp.bfloat16)
    mlp_out = matmul(gelu_out, w_fc2) + b_fc2
    row_mask = valid_slots.reshape(row_count, 1)
    layer_out = ((after_attn + mlp_out) * row_mask).astype(jnp.bfloat16)
    layer_out = layer_out.reshape(images, slot_count, width)
    grad_out = cotangent.astype(jnp.float32).reshape(row_count, width) * row_mask
    grad_top = grad_out.astype(jnp.bfloat16)
    grad_w_fc2 = matmul(gelu_out.T, grad_top)
    grad_b_fc2 = jnp.sum(grad_top.astype(jnp.float32), axis=0)
    (grad_pre_full,) = gelu_back(matmul(grad_top, w_fc2.T))
    grad_pre = grad_pre_full.astype(jnp.bfloat16)
    grad_w_fc1 = matmul(act_two.T, grad_pre)
    grad_b_fc1 = jnp.sum(grad_pre.astype(jnp.float32), axis=0)
    grad_norm_two, grad_ln2_gain, grad_ln2_bias = norm_two_back(matmul(grad_pre, w_fc1.T))
    grad_after = grad_out + grad_norm_two
    share_w_fc2 = scatter_sum(grad_w_fc2)
    share_w_fc1 = scatter_sum(grad_w_fc1)
    grad_branch = grad_after.astype(jnp.bfloat16)
    grad_w_out = matmul(mixed_heads.T, grad_branch)
    grad_b_out = jnp.sum(grad_branch.astype(jnp.float32), axis=0)
    grad_mixed = matmul(grad_branch, w_out.T).astype(jnp.bfloat16)
    grad_mixed = grad_mixed.reshape(images, slot_count, HEADS, HEAD_DIM)
    grad_probs = jnp.einsum(
        "blhe,bmhe->bhlm", grad_mixed, values, preferred_element_type=jnp.float32
    )
    grad_values = jnp.einsum(
        "bhlm,blhe->bmhe", probs_low, grad_mixed, preferred_element_type=jnp.float32
    )
    (grad_scores_full,) = softmax_back(grad_probs)
    grad_scores = grad_scores_full.astype(jnp.bfloat16)
    grad_queries = (
        jnp.einsum("bhlm,bmhe->blhe", grad_scores, key_part, preferred_element_type=jnp.float32)
        * SCORE_SCALE
    )
    grad_keys = (
        jnp.einsum("bhlm,blhe->bmhe", grad_scores, queries, preferred_element_type=jnp.float32)
        * SCORE_SCALE
    )
    grad_qkv = jnp.stack([grad_queries, grad_keys, grad_values], axis=2)
    grad_qkv = grad_qkv.reshape(row_count, 3 * width).astype(jnp.bfloat16)
    grad_w_qkv = matmul(act_one.T, grad_qkv)
    column_sums = jnp.sum(grad_qkv.astype(jnp.float32), axis=0)
    grad_b_query = column_sums[:width]
    grad_b_value = column_sums[2 * width :]
    grad_norm_one, grad_ln1_gain, grad_ln1_bias = norm_one_back(matmul(grad_qkv, w_qkv.T))
    grad_kept = grad_after + grad_norm_one
    share_w_out = scatter_sum(grad_w_out)
    share_w_qkv = scatter_sum(grad_w_qkv)
    small = scatter_vectors(
        [grad_ln1_gain, grad_ln1_bias, grad_b_query, grad_b_value, grad_b_out, grad_ln2_gain, grad_ln2_bias, grad_b_fc1, grad_b_fc2]
    )
    grad_patches = jnp.einsum(
        "bsp,bsd->bpd",
        table,
        grad_kept.reshape(images, slot_count, width),
        precision=lax.Precision.HIGHEST,
    )
    return (
        layer_out,
        grad_patches,
        small[0],
        small[1],
        share_w_qkv,
        small[2],
        small[3],
        share_w_out,
        small[4],
        small[5],
        small[6],
        share_w_fc1,
        small[7],
        share_w_fc2,
        small[8],
    )


def solution(mesh):
    in_specs = (
        P(("dp", "rep"), None, None),
        P(("dp", "rep"), None),
        P(),
        P(),
        P(),
        P(),
        P(),
        P(),
        P(),
        P(),
        P(),
        P(),
        P(),
        P(),
        P(),
        P(("dp", "rep"), None, None),
    )
    out_specs = (
        P(("dp", "rep"), None, None),
        P(("dp", "rep"), None, None),
        P(("dp", "rep")),
        P(("dp", "rep")),
        P(("dp", "rep"), None),
        P(("dp", "rep")),
        P(("dp", "rep")),
        P(("dp", "rep"), None),
        P(("dp", "rep")),
        P(("dp", "rep")),
        P(("dp", "rep")),
        P(("dp", "rep"), None),
        P(("dp", "rep")),
        P(("dp", "rep"), None),
        P(("dp", "rep")),
    )
    fits = mesh.shape["dp"] == 8 and mesh.shape["rep"] == 4
    local = local_kernels if fits else local_permutes
    return jax.shard_map(local, mesh=mesh, in_specs=in_specs, out_specs=out_specs, check_vma=False)
```

```python
from functools import partial

import jax
import jax.numpy as jnp
from jax import lax
from jax.experimental import pallas as pl
from jax.experimental.pallas import tpu as pltpu
from jax.sharding import PartitionSpec as P

HEADS = 16
HEAD_DIM = 64
NORM_EPSILON = 1e-06
SCORE_SCALE = 0.125
PAD = 64
GROUP = 256
MIB = 1 << 20
NT = (((1,), (1,)), ((), ()))


def select_parts(keep, slot_count):
    slot_ids = jnp.arange(slot_count, dtype=jnp.int32)
    ranks = jnp.cumsum(keep, axis=1) - 1
    table = (ranks[:, None, :] == slot_ids[None, :, None]) & (keep[:, None, :] == 1)
    counts = jnp.sum(keep, axis=1)
    valid_slots = (slot_ids[None, :] < counts[:, None]).astype(jnp.float32)
    return (table.astype(jnp.float32), valid_slots)


def matmul(left, right):
    return jnp.dot(left, right, preferred_element_type=jnp.float32)


def matmul_nt(left, right):
    return lax.dot_general(left, right, NT, preferred_element_type=jnp.float32)


def normed_rows(v):
    centred = v - jnp.mean(v, axis=-1, keepdims=True)
    scale = lax.rsqrt(jnp.mean(centred * centred, axis=-1, keepdims=True) + NORM_EPSILON)
    return centred * scale, scale


def head_mask():
    row = lax.broadcasted_iota(jnp.int32, (GROUP, GROUP), 0) // HEAD_DIM
    lane = lax.broadcasted_iota(jnp.int32, (GROUP, GROUP), 1) // HEAD_DIM
    return jnp.where(row == lane, 1.0, 0.0).astype(jnp.bfloat16)


def spread_heads(v, heads):
    return jnp.concatenate([v] * 4, axis=0) * heads


def fold_heads(v, head_of):
    out = v[:PAD]
    for h in range(1, 4):
        out = jnp.where(head_of == h, v[h * PAD : (h + 1) * PAD], out)
    return out


TILE = 256
HALF = 512
RING = 11
SENDS, TAKES = 3, 4
STAGES = 4
FIRSTS, LATERS = 6, 8
PLAN = (
    (), (), (), (), ((0, 0), (1, 0)), (), (), ((0, 1),), ((2, 0), (3, 0)), ((1, 1),), (), ((0, 2),), ((4, 0), (2,
    1)), ((1, 2), (3, 1)), (), ((0, 3), (5, 0)), ((4, 1), (6, 0)), ((1, 3), (2, 2), (3, 2)), (), (), ((0, 4), (5,
    1), (8, 0)), ((3, 3), (4, 2), (9, 0)), ((5, 2),), (), ((6, 1), (7, 0)), ((4, 3), (8, 1), (1, 4)), ((9, 1), (2,
    3), (5, 3), (3, 4), (10, 0), (6, 2), (8, 2), (9, 2), (7, 1), (11, 0), (10, 1), (6, 3), (7, 2), (4, 4), (12, 0),
    (2, 4)), (), ((5, 4), (7, 3), (11, 1), (13, 0)), ((12, 1), (8, 3)), (), (), ((9, 3), (13, 1), (14, 0)), ((8, 4),
    (12, 2)), ((13, 2), (10, 2), (15, 0), (6, 4)), ((7, 4), (9, 4)), ((10, 3), (14, 1)), ((11, 2), (12, 3), (16, 0),
    (15, 1)), ((10, 4), (11, 3), (13, 3), (14, 2), (17, 0)), ((12, 4),), ((16, 1),), (), (), ((11, 4), (15, 2), (17,
    1), (18, 0)), ((16, 2),), ((15, 3), (19, 0)), ((13, 4),), ((14, 3), (18, 1), (20, 0)), ((17, 2), (19, 1)), ((24,
    0), (14, 4), (15, 4), (16, 3), (20, 1), (24, 1), (17, 3)), ((18, 2), (19, 2), (21, 0), (16, 4), (17, 4), (20,
    2), (24, 2), (19, 3), (18, 3), (22, 0), (20, 3), (19, 4), (18, 4), (21, 1), (24, 3), (23, 0), (20, 4), (22, 1),
    (21, 2), (24, 4), (23, 1), (21, 3), (22, 2), (24, 5), (23, 2), (21, 4), (22, 3), (23, 3), (22, 4), (23, 4)),
)
WAYS = (0, 0, 3, 2, 0, 0, 2, 2, 0, 0, 1, 1, 0, 0, 3, 1, 3, 1, 1, 3, 3, 1, 1, 3)
ORDERS = (
    (("x", "y"), ("y", "x")),
    (("x", "near", "y", "far"), ("y", "near", "x", "far")),
    (("near", "x", "y", "far"), ("near", "y", "x", "far")),
    (("x", "y", "near", "far"), ("y", "x", "near", "far")),
)
MESH = pl.DeviceIdType.MESH


def gelu_parts(x):
    cdf = 0.5 * (1.0 + lax.erf(x * 0.7071067811865476))
    slope = cdf + x * (0.3989422804014327 * jnp.exp(-0.5 * (x * x)))
    return x * cdf, slope


def norm_back(grad, gain, unit, scale):
    e = grad * gain
    return scale * (e - jnp.mean(e, axis=-1, keepdims=True) - unit * jnp.mean(e * unit, axis=-1, keepdims=True))


def column_sum(v):
    return jnp.sum(v, axis=0, keepdims=True)


class Slots:
    def __init__(self, refs):
        self.refs = refs
        self.at = self.View(refs)

    class View:
        def __init__(self, refs):
            self.refs = refs

        def __getitem__(self, key):
            if isinstance(key, tuple):
                return self.refs[key[0]].at[key[1:]]
            return self.refs[key]

    def __getitem__(self, key):
        return self.refs[key[0]][key[1:]] if isinstance(key, tuple) else self.refs[key][...]

    def __setitem__(self, key, value):
        self.refs[key[0]][key[1:]] = value


def layer_kernel(
    counts, patches_in, cotangent_in, w_qkv_h, w_out_h, w_fc1_h, w_fc2_h,
    keys_row, keys, ln1_gain, ln1_bias, b_query, b_value, b_out, ln2_gain, ln2_bias, b_fc1, b_fc2,
    layer_h, patches_h, fc1_share, fc2_share, out_share, qkv_share, vectors_out,
    act1_t_h, qkv_h, probs_h, mixed_t_h, kept_h, after_h,
    pool, wide, ring, core_in, first_in, second_in, third_in, fourth_in, home_in, vectors, vectors_in, heads,
    load_sem, core_sem, stage_sem, home_sem, vector_sem,
):
    pool, wide = Slots(pool), Slots(wide)
    width = ln1_gain.shape[1]
    dp, rep = lax.axis_index("dp"), lax.axis_index("rep")
    far, near = dp // 4, lax.rem(dp // 2, 2)
    x, y, core = lax.rem(dp, 2), rep // 2, lax.rem(rep, 2)
    place = lambda far, near, x, y, core: (far * 4 + near * 2 + x, y * 2 + core)
    axes = {
        "c": (core, place(far, near, x, y, 1 - core)),
        "x": (x, place(far, near, 1 - x, y, core)),
        "y": (y, place(far, near, x, 1 - y, core)),
        "near": (near, place(far, 1 - near, x, y, core)),
        "far": (far, place(1 - far, near, x, y, core)),
    }

    barrier = pltpu.get_barrier_semaphore()
    for _, peer in axes.values():
        pl.semaphore_signal(barrier, inc=1, device_id=peer, device_id_type=MESH)

    started = {}

    def load(name, source, target):
        copy = pltpu.make_async_copy(source, target, load_sem.at[len(started)])
        copy.start()
        started[name] = copy

    def loaded(*names):
        for name in names:
            started[name].wait()

    def load_chunk(j):
        columns = slice(j * width, (j + 1) * width)
        load(f"w1_{j}", w_fc1_h.at[:, columns], pool.at[W1[j % 2]])
        load(f"w2_{j}", w_fc2_h.at[columns, :], pool.at[W2[j % 2]])

    W1, W2 = (3, 1), (5, 6)
    slots = patches_in.shape[0]
    images = width // PAD
    load("cotangent", cotangent_in, pool.at[8, :slots])
    load("patches_in", patches_in, pool.at[7, :slots])
    for k in range(3):
        load(f"w_in_{k}", w_qkv_h.at[:, k * width : (k + 1) * width], pool.at[4 + k])
    load("w_out_in", w_out_h, pool.at[1])
    load("w1_0", w_fc1_h.at[:, :width], pool.at[W1[0]])
    vectors[...] = jnp.zeros_like(vectors)
    heads[...] = head_mask()

    def tile_loop(body, tile=TILE):
        def step(r, carry):
            body(pl.ds(pl.multiple_of(r * tile, tile), tile), r * tile)
            return carry

        lax.fori_loop(0, width // tile, step, 0)

    def select(which, start):
        row = lax.broadcasted_iota(jnp.int32, (TILE, slots), 0) + start
        return jnp.where(row == keys_row[which : which + 1, :], 1.0, 0.0).astype(jnp.bfloat16)

    def open_top(rows, start):
        pool[2, rows, :] = matmul(select(1, start), pool[8, :slots, :]).astype(jnp.bfloat16)

    def open_kept(rows, start):
        kept_rows = matmul(select(0, start), pool[7, :slots, :])
        wide[0, rows, :] = kept_rows
        unit, _ = normed_rows(kept_rows)
        act1 = (unit * ln1_gain[...] + ln1_bias[...]).astype(jnp.bfloat16)
        pool[8, rows, :] = act1
        pool[0, :, rows] = act1.T

    def project(source, target, bias):
        def body(rows, start):
            out = matmul(pool[8, rows, :], pool[source])
            pool[target, rows, :] = (out if bias is None else out + bias[...]).astype(jnp.bfloat16)

        tile_loop(body, 2 * TILE)

    loaded("cotangent")
    tile_loop(open_top)
    loaded("patches_in")
    tile_loop(open_kept)
    load("kept_out", wide.at[0], kept_h)
    load("act1_t_out", pool.at[0], act1_t_h)
    for k, (target, bias) in enumerate(((7, b_query), (4, None), (5, b_value))):
        loaded(f"w_in_{k}")
        project(4 + k, target, bias)
        load(f"qkv_out_{k}", pool.at[target], qkv_h.at[k])

    def attend(i, carry):
        rows = pl.ds(pl.multiple_of(i * PAD, PAD), PAD)
        row = lax.broadcasted_iota(jnp.int32, (PAD, GROUP), 0)
        head_of = lax.broadcasted_iota(jnp.int32, (PAD, GROUP), 1) // HEAD_DIM
        seen = row < counts[i]
        for g in range(width // GROUP):
            lanes = slice(g * GROUP, (g + 1) * GROUP)
            queries = spread_heads(pool[7, rows, lanes], heads[...])
            scores = matmul_nt(pool[4, rows, lanes], queries) * SCORE_SCALE
            scores = jnp.where(seen, scores, -1000000000.0)
            raised = jnp.exp(scores - jnp.max(scores, axis=0, keepdims=True))
            probs = (raised * (1.0 / jnp.sum(raised, axis=0, keepdims=True))).astype(jnp.bfloat16)
            pool[6, rows, lanes] = probs
            pool[8, rows, lanes] = fold_heads(matmul(probs.T, pool[5, rows, lanes]), head_of).astype(jnp.bfloat16)
        return carry

    lax.fori_loop(0, images, attend, 0, unroll=4)
    load("probs_out", pool.at[6], probs_h)
    loaded("w_out_in", "act1_t_out", "qkv_out_0", "qkv_out_1", "qkv_out_2")

    def close_attention(rows, start):
        mixed = pool[8, rows, :]
        pool[7, :, rows] = mixed.T
        after = wide[0, rows, :] + (matmul(mixed, pool[1]) + b_out[...])
        wide[1, rows, :] = after
        unit, _ = normed_rows(after)
        act2 = (unit * ln2_gain[...] + ln2_bias[...]).astype(jnp.bfloat16)
        pool[0, rows, :] = act2
        pool[4, :, rows] = act2.T

    tile_loop(close_attention)
    load("mixed_t_out", pool.at[7], mixed_t_h)
    load("after_out", wide.at[1], after_h)
    load("w2_0", w_fc2_h.at[:width, :], pool.at[W2[0]])
    pl.semaphore_wait(barrier, len(axes))

    units = []
    for j in range(4):
        units += [("fc2", j, h) for h in range(2)] + [("fc1", j, h) for h in range(2)]
    units += [("out", 0, h) for h in range(2)]
    units += [("qkv", k, h) for k in range(3) for h in range(2)]
    share_of = {"fc1": fc1_share, "out": out_share, "qkv": qkv_share}
    finished, delivered, pumped = set(), set(), []

    def remote(source, target, send, receive, peer):
        return pltpu.make_async_remote_copy(
            src_ref=source, dst_ref=target, send_sem=send, recv_sem=receive, device_id=peer, device_id_type=MESH
        )

    def core_copy(u):
        s, t = u % SENDS, u % TAKES
        return remote(ring.at[RING + s], core_in.at[t], core_sem.at[0, t], core_sem.at[1, t], axes["c"][1])

    def orders_of(u):
        assert (WAYS[u] == 0) == (units[u][0] == "fc2")
        return ORDERS[WAYS[u]]

    def kept(u, half, stage):
        return (u % RING, half, *(axes[name][0] for name in orders_of(u)[half][:stage]))

    def landing(u, half, stage):
        if stage == 0:
            return first_in, (u % FIRSTS, half)
        return (second_in, third_in, fourth_in)[stage - 1], (u % LATERS, half)

    def stage_copy(u, half, stage):
        index, peer = axes[orders_of(u)[half][stage]]
        target, at = landing(u, half, stage)
        slot = stage * LATERS + at[0]
        return remote(
            ring.at[(*kept(u, half, stage), 1 - index)], target.at[at],
            stage_sem.at[0, slot, half], stage_sem.at[1, slot, half], peer,
        )

    def home_copy(u, half, stage):
        _, j, h = units[u]
        slot = h if stage == 2 else 2 + h
        return remote(
            ring.at[kept(u, half, 2)], home_in.at[slot, half], home_sem.at[0, slot, half], home_sem.at[1, slot, half],
            axes["near" if stage == 2 else "far"][1],
        )

    def home_roles(u, stage):
        j = units[u][1]
        if stage == 2:
            return near != j % 2, near == j % 2
        return (near == j % 2) & (far != j // 2), (near == j % 2) & (far == j // 2)

    def stage_start(u, half, stage):
        if units[u][0] == "fc2" and stage >= 2:

            @pl.when(home_roles(u, stage)[0])
            def _():
                home_copy(u, half, stage).start()
        else:
            stage_copy(u, half, stage).start()

    def stage_finish(u, half, stage):
        if units[u][0] == "fc2" and stage >= 2:
            sends, takes = home_roles(u, stage)
            copy = home_copy(u, half, stage)

            @pl.when(sends)
            def _():
                copy.wait_send()

            @pl.when(takes)
            def _():
                copy.wait_recv()
                j, h = units[u][1:]
                slot = h if stage == 2 else 2 + h
                ring[kept(u, half, 2)] += home_in[slot, half]
        else:
            stage_copy(u, half, stage).wait()
            source, at = landing(u, half, stage)
            ring[kept(u, half, stage + 1)] += source[at]

    def deliver(u):
        kind, j, h = units[u]
        if kind == "fc2":

            @pl.when((near == j % 2) & (far == j // 2))
            def _():
                for half in range(2):
                    for q in range(4):
                        at = q * 32 + half * 16
                        fc2_share[at : at + 16, h * HALF : (h + 1) * HALF] = ring[(*kept(u, half, 2), q // 2, q % 2)]
        else:
            at = j * width + h * HALF
            for half in range(2):
                share_of[kind][half * 16 : (half + 1) * 16, at : at + HALF] = ring[kept(u, half, 4)]

    def core_finish(u):
        if u < 0 or u in finished:
            return
        finished.add(u)
        core_copy(u).wait()
        for half in range(2):
            for i in range(2):
                ring[u % RING, half, i] += core_in[u % TAKES, half, i]

    def vector_copy(stage):
        peer = axes[("c", "x", "y", "near", "far")[stage]][1]
        return remote(vectors, vectors_in.at[stage], vector_sem.at[0, stage], vector_sem.at[1, stage], peer)

    def vector_stage(stage):
        if stage > 0:
            vector_copy(stage - 1).wait()
            total = vectors[...] + vectors_in[stage - 1]
            if stage == 5:
                vectors_out[...] = total
                return
            vectors[...] = total
        vector_copy(stage).start()

    def pump():
        for u, k in PLAN[len(pumped)]:
            if u == len(units):
                vector_stage(k)
                continue
            if k == 0:
                for v in range(u + 1):
                    core_finish(v)
            for half in range(2):
                if k > 0:
                    stage_finish(u, half, k - 1)
                if k < STAGES:
                    stage_start(u, half, k)
            if k == STAGES:
                deliver(u)
                delivered.add(u)
        pumped.append(True)

    def produce(u, left, right):
        kind, _, h = units[u]
        assert u < RING or u - RING in delivered
        columns = slice(h * HALF, (h + 1) * HALF)

        def part(owner, slot):
            if kind == "fc2":
                rows = [left[pl.ds(pl.multiple_of(b * 256 + owner * 128, 128), 128), :] for b in range(4)]
            else:
                rows = [left[pl.ds(pl.multiple_of(b * 64 + owner * 32, 32), 32), :] for b in range(16)]
            product = matmul(jnp.concatenate(rows, axis=0), right[:, columns])
            for b in range(16):
                if kind == "fc2":
                    names = {"x": b // 8, "y": b // 4 % 2, "near": b // 2 % 2, "far": b % 2}
                else:
                    names = {"far": b // 8, "near": b // 4 % 2, "x": b // 2 % 2, "y": b % 2}
                for half, order in enumerate(orders_of(u)):
                    at = b * 32 + half * 16
                    order = (*order, "near", "far")[:4]
                    ring[(slot, half, *(names[name] for name in order))] = product[at : at + 16]

        core_finish(u - TAKES // 2)
        part(1 - core, RING + u % SENDS)
        core_copy(u).start()
        part(core, u % RING)
        pump()

    def row_loop(body):
        def step(r, carry):
            body(pl.ds(pl.multiple_of(r * TILE, TILE), TILE))
            return carry

        parts = width // TILE // 2
        for part in range(2):
            lax.fori_loop(part * parts, (part + 1) * parts, step, 0)
            pump()

    def chunk_forward(j):
        w1 = pool.at[W1[j % 2]]

        def body(rows):
            for c in range(2):
                columns = slice(c * HALF, (c + 1) * HALF)
                hidden = slice(j * width + c * HALF, j * width + (c + 1) * HALF)
                value, slope = gelu_parts(matmul(pool[0, rows, :], w1[:, columns]) + b_fc1[:, hidden])
                value = value.astype(jnp.bfloat16)
                wide[2, rows, columns] = slope
                pool[8, rows, columns] = value
                pool[7, columns, rows] = value.T

        row_loop(body)

    def chunk_backward(j):
        w1, w2 = pool.at[W1[j % 2]], pool.at[W2[j % 2]]

        def body(rows):
            branch = matmul(pool[8, rows, :], w2[...])
            if j == 0:
                wide[1, rows, :] = branch
                vectors[7:8, :] += column_sum(pool[2, rows, :].astype(jnp.float32))
            else:
                wide[1, rows, :] += branch
            total = None
            for c in range(2):
                columns = slice(c * HALF, (c + 1) * HALF)
                grad = matmul_nt(pool[2, rows, :], w2[columns, :]) * wide[2, rows, columns]
                grad = grad.astype(jnp.bfloat16)
                pool[8, rows, columns] = grad
                vectors[8 + j : 9 + j, columns] += column_sum(grad.astype(jnp.float32))
                back = matmul_nt(grad, w1[:, columns])
                total = back if total is None else total + back
            if j == 0:
                wide[0, rows, :] = total
            else:
                wide[0, rows, :] += total

        row_loop(body)

    for j in range(4):
        loaded(f"w1_{j}")
        if j == 0:
            loaded("mixed_t_out", "probs_out")
        if j < 3:
            load_chunk(j + 1)
        else:
            load("w_out", w_out_h, pool.at[3])
            load("mixed_t", mixed_t_h, pool.at[5])
        chunk_forward(j)
        produce(4 * j, pool.at[7], pool.at[2])
        produce(4 * j + 1, pool.at[7], pool.at[2])
        if j == 0:
            loaded("kept_out", "after_out")
        loaded(f"w2_{j}")
        chunk_backward(j)
        if j == 3:
            load("after", after_h, wide.at[2])
            for k in range(2):
                load(f"qkv_{k}", qkv_h.at[k], pool.at[6 + k])
            load("probs", probs_h, pool.at[1])
        produce(4 * j + 2, pool.at[4], pool.at[8])
        produce(4 * j + 3, pool.at[4], pool.at[8])
        if j == 3:
            load("qkv_2", qkv_h.at[2], pool.at[8])

    loaded("after", "w_out")

    def middle(rows):
        after = wide[2, rows, :]
        unit, scale = normed_rows(after)
        grad = wide[0, rows, :]
        vectors[5:6, :] += column_sum(grad * unit)
        vectors[6:7, :] += column_sum(grad)
        grad = pool[2, rows, :].astype(jnp.float32) + norm_back(grad, ln2_gain[...], unit, scale)
        wide[0, rows, :] = grad
        pool[2, rows, :] = (after + (wide[1, rows, :] + b_fc2[...])).astype(jnp.bfloat16)
        branch = grad.astype(jnp.bfloat16)
        pool[0, rows, :] = branch
        vectors[4:5, :] += column_sum(branch.astype(jnp.float32))
        pool[4, rows, :] = matmul_nt(branch, pool[3]).astype(jnp.bfloat16)

    row_loop(middle)
    loaded("mixed_t")
    load("w_qkv_0", w_qkv_h.at[:, :width], pool.at[3])
    load("kept", kept_h, wide.at[1])
    produce(16, pool.at[5], pool.at[0])
    produce(17, pool.at[5], pool.at[0])
    load("w_qkv_1", w_qkv_h.at[:, width : 2 * width], pool.at[5])
    load("act1_t", act1_t_h, pool.at[0])
    loaded("qkv_0", "qkv_1", "qkv_2", "probs")

    def attend_back(i, carry):
        rows = pl.ds(pl.multiple_of(i * PAD, PAD), PAD)
        head_of = lax.broadcasted_iota(jnp.int32, (PAD, GROUP), 1) // HEAD_DIM
        for g in range(width // GROUP):
            lanes = slice(g * GROUP, (g + 1) * GROUP)
            queries = spread_heads(pool[6, rows, lanes], heads[...])
            keys, values = pool[7, rows, lanes], pool[8, rows, lanes]
            grad_mixed = spread_heads(pool[4, rows, lanes], heads[...])
            low_probs = pool[1, rows, lanes]
            probs = low_probs.astype(jnp.float32)
            grad_probs = matmul_nt(values, grad_mixed)
            grad_scores = probs * (grad_probs - column_sum(probs * grad_probs))
            grad_scores = grad_scores.astype(jnp.bfloat16)
            grad_queries = fold_heads(matmul(grad_scores.T, keys), head_of) * SCORE_SCALE
            grad_keys = matmul(grad_scores, queries) * SCORE_SCALE
            grad_values = matmul(low_probs, grad_mixed)
            pool[6, rows, lanes] = grad_queries.astype(jnp.bfloat16)
            pool[7, rows, lanes] = grad_keys.astype(jnp.bfloat16)
            pool[8, rows, lanes] = grad_values.astype(jnp.bfloat16)
        return carry

    for part in range(4):
        lax.fori_loop(part * images // 4, (part + 1) * images // 4, attend_back, 0, unroll=2)
        pump()
    load("w_qkv_2", w_qkv_h.at[:, 2 * width :], pool.at[4])

    block = 160

    def select_rows(r, column):
        rows = slice(r * block, (r + 1) * block)
        lane = lax.broadcasted_iota(jnp.int32, (block, width), 1)
        return rows, jnp.where(lane == keys[rows, column : column + 1], 1.0, 0.0).astype(jnp.bfloat16)

    for r in range(slots // block):
        rows, select = select_rows(r, 1)
        pool[1, rows, :] = matmul(select, pool[2]).astype(jnp.bfloat16)
    load("layer", pool.at[1, :slots], layer_h)
    pump()

    loaded("act1_t")
    for k in range(3):
        produce(18 + 2 * k, pool.at[0], pool.at[6 + k])
        produce(19 + 2 * k, pool.at[0], pool.at[6 + k])

    loaded("w_qkv_0", "w_qkv_1", "w_qkv_2", "kept")

    def first(rows):
        grads = [pool[6 + k, rows, :] for k in range(3)]
        vectors[2:3, :] += column_sum(grads[0].astype(jnp.float32))
        vectors[3:4, :] += column_sum(grads[2].astype(jnp.float32))
        grad = matmul_nt(grads[0], pool[3]) + matmul_nt(grads[1], pool[5]) + matmul_nt(grads[2], pool[4])
        unit, scale = normed_rows(wide[1, rows, :])
        vectors[0:1, :] += column_sum(grad * unit)
        vectors[1:2, :] += column_sum(grad)
        grad = wide[0, rows, :] + norm_back(grad, ln1_gain[...], unit, scale)
        for k in range(3):
            piece = grad.astype(jnp.bfloat16)
            pool[6 + k, rows, :] = piece
            grad = grad - piece.astype(jnp.float32)

    row_loop(first)

    for r in range(slots // block):
        rows, select = select_rows(r, 0)
        pieces = [matmul(select, pool[6 + k]) for k in (2, 1, 0)]
        wide[2, rows, :] = (pieces[0] + pieces[1]) + pieces[2]
    load("patches", wide.at[2, :slots], patches_h)
    pump()
    pump()
    assert len(delivered) == len(units)
    loaded("layer", "patches")


def layer(counts, tensors, keys, vectors, dp, rep):
    slots, width = tensors[0].shape
    any_space, vmem = pl.BlockSpec(memory_space=pl.ANY), pl.BlockSpec(memory_space=pltpu.VMEM)
    shape = jax.ShapeDtypeStruct
    f32, bf16, devices = jnp.float32, jnp.bfloat16, dp * rep
    dma = pltpu.SemaphoreType.DMA
    piece = (16, HALF)
    square = (width, width)
    return pl.pallas_call(
        layer_kernel,
        in_specs=[pl.BlockSpec(memory_space=pltpu.SMEM)] + [any_space] * len(tensors) + [vmem] * (2 + len(vectors)),
        out_specs=[any_space] * 2 + [vmem] * 5 + [any_space] * 6,
        out_shape=[
            shape((slots, width), bf16), shape((slots, width), f32), shape((width // devices, 4 * width), f32),
            shape((4 * width // devices, width), f32), shape((width // devices, width), f32),
            shape((width // devices, 3 * width), f32), shape((16, width), f32),
            shape(square, bf16), shape((3, *square), bf16), shape(square, bf16), shape(square, bf16), shape(square, f32),
            shape(square, f32),
        ],
        scratch_shapes=[
            [pltpu.VMEM(square, bf16)] * 9, [pltpu.VMEM(square, f32)] * 3,
            pltpu.VMEM((RING + SENDS, 2, 2, 2, 2, 2, *piece), f32), pltpu.VMEM((TAKES, 2, 2, 2, 2, 2, *piece), f32),
            pltpu.VMEM((FIRSTS, 2, 2, 2, 2, *piece), f32), pltpu.VMEM((LATERS, 2, 2, 2, *piece), f32),
            pltpu.VMEM((LATERS, 2, 2, *piece), f32), pltpu.VMEM((LATERS, 2, *piece), f32),
            pltpu.VMEM((4, 2, 2, 2, *piece), f32), pltpu.VMEM((16, width), f32), pltpu.VMEM((5, 16, width), f32),
            pltpu.VMEM((GROUP, GROUP), bf16),
            dma((48,)), dma((2, TAKES)), dma((2, 4 * LATERS, 2)), dma((2, 4, 2)), dma((2, 5)),
        ],
        compiler_params=pltpu.CompilerParams(collective_id=0, has_side_effects=True, vmem_limit_bytes=63 * MIB),
        name="layer",
    )(counts, *tensors, *keys, *vectors)[:7]


def local_kernels(
    patches, keep, ln1_gain, ln1_bias, w_qkv, b_query, b_value, w_out, b_out, ln2_gain, ln2_bias, w_fc1, b_fc1, w_fc2,
    b_fc2, cotangent,
):
    dp, rep = lax.axis_size("dp"), lax.axis_size("rep")
    images, slots, width = patches.shape
    rows = images * slots
    kept = keep.T
    image = jnp.arange(images, dtype=jnp.int32) * PAD
    ids = jnp.arange(slots, dtype=jnp.int32)[:, None]
    upto = (ids >= ids.T).astype(jnp.float32)
    ranks = matmul(upto, kept.astype(jnp.float32)).astype(jnp.int32)
    counts = ranks[-1]
    keys = jnp.stack([
        jnp.where(kept == 1, image + ranks - 1, -1), jnp.where(ids < counts, image + ids, -1)
    ]).reshape(2, rows)
    flat = lambda a: jnp.swapaxes(a, 0, 1).reshape(rows, width)
    row = lambda v: v.reshape(1, -1)
    layer_rows, grad_patches, fc1_share, fc2_share, out_share, qkv_share, vectors = layer(
        counts, [flat(patches), flat(cotangent), w_qkv, w_out, w_fc1, w_fc2], [keys, keys.T],
        [row(v) for v in (ln1_gain, ln1_bias, b_query, b_value, b_out, ln2_gain, ln2_bias, b_fc1, b_fc2)], dp, rep,
    )
    device = lax.axis_index("dp") * rep + lax.axis_index("rep")
    share = width // (dp * rep)
    mine = lax.dynamic_slice(vectors[:8], (0, device * share), (8, share))
    hidden = lax.dynamic_slice(vectors[8:12].reshape(-1), (device * 4 * share,), (4 * share,))
    unflat = lambda a: jnp.swapaxes(a.reshape(slots, images, width), 0, 1)
    return (
        unflat(layer_rows), unflat(grad_patches), mine[0], mine[1], qkv_share, mine[2], mine[3], out_share, mine[4], mine[5],
        mine[6], fc1_share, hidden, fc2_share, mine[7],
    )


def normalize(v):
    centred = v - jnp.mean(v, axis=-1, keepdims=True)
    return centred * lax.rsqrt(jnp.mean(centred * centred, axis=-1, keepdims=True) + NORM_EPSILON)


def affine_norm(v, gain, shift):
    return normalize(v) * gain + shift


def exchange(parts, axis, stride, count):
    size = lax.axis_size(axis)
    index = lax.axis_index(axis)
    place = (index // stride) % count
    total = lax.dynamic_index_in_dim(parts, place, 0, keepdims=False)
    for step in range(1, count):
        pairs = []
        for source in range(size):
            own = (source // stride) % count
            target = source + (((own + step) % count) - own) * stride
            pairs.append((source, target))
        sent = lax.dynamic_index_in_dim(parts, (place + step) % count, 0, keepdims=False)
        total = total + lax.ppermute(sent, axis, pairs)
    return total


def scatter_sum(grad):
    rows, columns = grad.shape
    dp, rep = lax.axis_size("dp"), lax.axis_size("rep")
    z, y = dp // 2, rep // 2
    share = rows // (dp * rep)
    parts = grad.reshape(z, 2, y, 2, share, columns)
    parts = exchange(jnp.moveaxis(parts, 3, 0), "rep", 1, 2)
    half = columns // 2
    x_first, y_first = parts[..., :half], parts[..., half:]
    x_first = exchange(jnp.moveaxis(x_first, 1, 0), "dp", 1, 2)
    y_first = exchange(jnp.moveaxis(y_first, 2, 0), "rep", 2, y)
    x_first = exchange(jnp.moveaxis(x_first, 1, 0), "rep", 2, y)
    y_first = exchange(jnp.moveaxis(y_first, 1, 0), "dp", 1, 2)
    both = jnp.concatenate([x_first, y_first], axis=-1)
    return exchange(both, "dp", 2, z)


def scatter_vectors(vectors):
    joined = jnp.concatenate([v.reshape(lax.axis_size("dp") * lax.axis_size("rep"), -1) for v in vectors], axis=1)
    total = lax.psum_scatter(joined, ("dp", "rep"), scatter_dimension=0, tiled=True)[0]
    out, start = [], 0
    for v in vectors:
        length = v.shape[0] // (lax.axis_size("dp") * lax.axis_size("rep"))
        out.append(total[start : start + length])
        start += length
    return out


def local_permutes(
    patches,
    keep,
    ln1_gain,
    ln1_bias,
    w_qkv,
    b_query,
    b_value,
    w_out,
    b_out,
    ln2_gain,
    ln2_bias,
    w_fc1,
    b_fc1,
    w_fc2,
    b_fc2,
    cotangent,
):
    images, slot_count, width = patches.shape
    row_count = images * slot_count
    table, valid_slots = select_parts(keep, slot_count)
    kept = jnp.einsum(
        "bsp,bpd->bsd", table.astype(jnp.bfloat16), patches, preferred_element_type=jnp.float32
    ).reshape(row_count, width)
    normed_one, norm_one_back = jax.vjp(affine_norm, kept, ln1_gain, ln1_bias)
    act_one = normed_one.astype(jnp.bfloat16)
    bias_all = jnp.concatenate([b_query, jnp.zeros_like(b_query), b_value])
    qkv = (matmul(act_one, w_qkv) + bias_all).astype(jnp.bfloat16)
    qkv = qkv.reshape(images, slot_count, 3, HEADS, HEAD_DIM)
    queries, key_part, values = (qkv[:, :, 0], qkv[:, :, 1], qkv[:, :, 2])
    scores = (
        jnp.einsum("blhe,bmhe->bhlm", queries, key_part, preferred_element_type=jnp.float32)
        * SCORE_SCALE
    )
    scores = jnp.where(valid_slots[:, None, None, :] > 0, scores, -1000000000.0)
    attn_probs, softmax_back = jax.vjp(partial(jax.nn.softmax, axis=-1), scores)
    probs_low = attn_probs.astype(jnp.bfloat16)
    mixed_heads = jnp.einsum(
        "bhlm,bmhe->blhe", probs_low, values, preferred_element_type=jnp.float32
    )
    mixed_heads = mixed_heads.reshape(row_count, width).astype(jnp.bfloat16)
    after_attn = kept + (matmul(mixed_heads, w_out) + b_out)
    normed_two, norm_two_back = jax.vjp(affine_norm, after_attn, ln2_gain, ln2_bias)
    act_two = normed_two.astype(jnp.bfloat16)
    pre_gelu = matmul(act_two, w_fc1) + b_fc1
    gelu_full, gelu_back = jax.vjp(partial(jax.nn.gelu, approximate=False), pre_gelu)
    gelu_out = gelu_full.astype(jnp.bfloat16)
    mlp_out = matmul(gelu_out, w_fc2) + b_fc2
    row_mask = valid_slots.reshape(row_count, 1)
    layer_out = ((after_attn + mlp_out) * row_mask).astype(jnp.bfloat16)
    layer_out = layer_out.reshape(images, slot_count, width)
    grad_out = cotangent.astype(jnp.float32).reshape(row_count, width) * row_mask
    grad_top = grad_out.astype(jnp.bfloat16)
    grad_w_fc2 = matmul(gelu_out.T, grad_top)
    grad_b_fc2 = jnp.sum(grad_top.astype(jnp.float32), axis=0)
    (grad_pre_full,) = gelu_back(matmul(grad_top, w_fc2.T))
    grad_pre = grad_pre_full.astype(jnp.bfloat16)
    grad_w_fc1 = matmul(act_two.T, grad_pre)
    grad_b_fc1 = jnp.sum(grad_pre.astype(jnp.float32), axis=0)
    grad_norm_two, grad_ln2_gain, grad_ln2_bias = norm_two_back(matmul(grad_pre, w_fc1.T))
    grad_after = grad_out + grad_norm_two
    share_w_fc2 = scatter_sum(grad_w_fc2)
    share_w_fc1 = scatter_sum(grad_w_fc1)
    grad_branch = grad_after.astype(jnp.bfloat16)
    grad_w_out = matmul(mixed_heads.T, grad_branch)
    grad_b_out = jnp.sum(grad_branch.astype(jnp.float32), axis=0)
    grad_mixed = matmul(grad_branch, w_out.T).astype(jnp.bfloat16)
    grad_mixed = grad_mixed.reshape(images, slot_count, HEADS, HEAD_DIM)
    grad_probs = jnp.einsum(
        "blhe,bmhe->bhlm", grad_mixed, values, preferred_element_type=jnp.float32
    )
    grad_values = jnp.einsum(
        "bhlm,blhe->bmhe", probs_low, grad_mixed, preferred_element_type=jnp.float32
    )
    (grad_scores_full,) = softmax_back(grad_probs)
    grad_scores = grad_scores_full.astype(jnp.bfloat16)
    grad_queries = (
        jnp.einsum("bhlm,bmhe->blhe", grad_scores, key_part, preferred_element_type=jnp.float32)
        * SCORE_SCALE
    )
    grad_keys = (
        jnp.einsum("bhlm,blhe->bmhe", grad_scores, queries, preferred_element_type=jnp.float32)
        * SCORE_SCALE
    )
    grad_qkv = jnp.stack([grad_queries, grad_keys, grad_values], axis=2)
    grad_qkv = grad_qkv.reshape(row_count, 3 * width).astype(jnp.bfloat16)
    grad_w_qkv = matmul(act_one.T, grad_qkv)
    column_sums = jnp.sum(grad_qkv.astype(jnp.float32), axis=0)
    grad_b_query = column_sums[:width]
    grad_b_value = column_sums[2 * width :]
    grad_norm_one, grad_ln1_gain, grad_ln1_bias = norm_one_back(matmul(grad_qkv, w_qkv.T))
    grad_kept = grad_after + grad_norm_one
    share_w_out = scatter_sum(grad_w_out)
    share_w_qkv = scatter_sum(grad_w_qkv)
    small = scatter_vectors(
        [grad_ln1_gain, grad_ln1_bias, grad_b_query, grad_b_value, grad_b_out, grad_ln2_gain, grad_ln2_bias, grad_b_fc1, grad_b_fc2]
    )
    grad_patches = jnp.einsum(
        "bsp,bsd->bpd",
        table,
        grad_kept.reshape(images, slot_count, width),
        precision=lax.Precision.HIGHEST,
    )
    return (
        layer_out,
        grad_patches,
        small[0],
        small[1],
        share_w_qkv,
        small[2],
        small[3],
        share_w_out,
        small[4],
        small[5],
        small[6],
        share_w_fc1,
        small[7],
        share_w_fc2,
        small[8],
    )


def solution(mesh):
    in_specs = (
        P(("dp", "rep"), None, None),
        P(("dp", "rep"), None),
        P(),
        P(),
        P(),
        P(),
        P(),
        P(),
        P(),
        P(),
        P(),
        P(),
        P(),
        P(),
        P(),
        P(("dp", "rep"), None, None),
    )
    out_specs = (
        P(("dp", "rep"), None, None),
        P(("dp", "rep"), None, None),
        P(("dp", "rep")),
        P(("dp", "rep")),
        P(("dp", "rep"), None),
        P(("dp", "rep")),
        P(("dp", "rep")),
        P(("dp", "rep"), None),
        P(("dp", "rep")),
        P(("dp", "rep")),
        P(("dp", "rep")),
        P(("dp", "rep"), None),
        P(("dp", "rep")),
        P(("dp", "rep"), None),
        P(("dp", "rep")),
    )
    fits = mesh.shape["dp"] == 8 and mesh.shape["rep"] == 4
    local = local_kernels if fits else local_permutes
    return jax.shard_map(local, mesh=mesh, in_specs=in_specs, out_specs=out_specs, check_vma=False)
```

```python
from functools import partial

import jax
import jax.numpy as jnp
from jax import lax
from jax.experimental import pallas as pl
from jax.experimental.pallas import tpu as pltpu
from jax.sharding import PartitionSpec as P

HEADS = 16
HEAD_DIM = 64
NORM_EPSILON = 1e-06
SCORE_SCALE = 0.125
PAD = 64
GROUP = 256
MIB = 1 << 20
NT = (((1,), (1,)), ((), ()))


def select_parts(keep, slot_count):
    slot_ids = jnp.arange(slot_count, dtype=jnp.int32)
    ranks = jnp.cumsum(keep, axis=1) - 1
    table = (ranks[:, None, :] == slot_ids[None, :, None]) & (keep[:, None, :] == 1)
    counts = jnp.sum(keep, axis=1)
    valid_slots = (slot_ids[None, :] < counts[:, None]).astype(jnp.float32)
    return (table.astype(jnp.float32), valid_slots)


def matmul(left, right):
    return jnp.dot(left, right, preferred_element_type=jnp.float32)


def matmul_nt(left, right):
    return lax.dot_general(left, right, NT, preferred_element_type=jnp.float32)


def normed_rows(v):
    centred = v - jnp.mean(v, axis=-1, keepdims=True)
    scale = lax.rsqrt(jnp.mean(centred * centred, axis=-1, keepdims=True) + NORM_EPSILON)
    return centred * scale, scale


def head_mask():
    row = lax.broadcasted_iota(jnp.int32, (GROUP, GROUP), 0) // HEAD_DIM
    lane = lax.broadcasted_iota(jnp.int32, (GROUP, GROUP), 1) // HEAD_DIM
    return jnp.where(row == lane, 1.0, 0.0).astype(jnp.bfloat16)


def spread_heads(v, heads):
    return jnp.concatenate([v] * 4, axis=0) * heads


def fold_heads(v, head_of):
    out = v[:PAD]
    for h in range(1, 4):
        out = jnp.where(head_of == h, v[h * PAD : (h + 1) * PAD], out)
    return out


TILE = 256
HALF = 512
RING = 11
SENDS, TAKES = 3, 4
STAGES = 4
FIRSTS, LATERS = 5, 8
PLAN = (
    (), (), (), (), ((0, 0),), ((1, 0),), (), ((0, 1),), (), ((2, 0), (1, 1), (3, 0)), (), (), ((0, 2), (4, 0)),
    ((1, 2), (2, 1), (5, 0)), ((3, 1),), (), (), ((0, 3), (4, 1)), (), (), ((1, 3), (3, 2), (5, 1)), ((3, 3), (2,
    2), (4, 2), (6, 0)), ((5, 2), (2, 3), (7, 0), (0, 4)), (), ((4, 3),), ((1, 4), (6, 1), (8, 0)), ((3, 4), (5, 3),
    (7, 1), (2, 4), (9, 0)), (), ((4, 4), (8, 1)), ((6, 2), (11, 0)), ((9, 1),), ((10, 0),), ((5, 4), (6, 3), (8,
    2)), ((12, 0),), ((7, 2), (11, 1), (9, 2), (12, 1), (13, 0), (7, 3), (10, 1), (6, 4)), ((12, 2),), ((8, 3), (13,
    1), (14, 0)), ((12, 3), (10, 2), (11, 2), (13, 2)), ((8, 4), (15, 0)), ((7, 4), (12, 4), (9, 3), (10, 3), (11,
    3), (14, 1)), ((16, 0),), ((13, 3),), ((15, 1), (14, 2), (17, 0), (9, 4)), ((10, 4),), ((11, 4),), ((16, 1),),
    (), ((13, 4), (17, 1), (18, 0)), ((15, 2), (16, 2), (19, 0)), ((24, 0), (14, 3), (15, 3), (18, 1), (24, 1), (20,
    0)), ((17, 2), (19, 1), (16, 3), (24, 2), (14, 4), (15, 4), (20, 1), (17, 3), (18, 2), (16, 4), (19, 2), (17,
    4), (24, 3), (21, 0), (20, 2), (19, 3), (18, 3), (22, 0), (24, 4), (20, 3), (19, 4), (21, 1), (23, 0), (18, 4),
    (24, 5), (20, 4), (22, 1), (21, 2), (23, 1), (21, 3), (22, 2), (23, 2), (21, 4), (22, 3), (23, 3), (22, 4), (23,
    4)),
)
WAYS = (0, 0, 1, 2, 0, 0, 1, 1, 0, 0, 2, 1, 0, 0, 3, 1, 3, 1, 1, 3, 3, 1, 1, 3)
ORDERS = (
    (("x", "y"), ("y", "x")),
    (("x", "near", "y", "far"), ("y", "near", "x", "far")),
    (("near", "x", "y", "far"), ("near", "y", "x", "far")),
    (("x", "y", "near", "far"), ("y", "x", "near", "far")),
)
MESH = pl.DeviceIdType.MESH


def gelu_parts(x):
    cdf = 0.5 * (1.0 + lax.erf(x * 0.7071067811865476))
    slope = cdf + x * (0.3989422804014327 * jnp.exp(-0.5 * (x * x)))
    return x * cdf, slope


def norm_back(grad, gain, unit, scale):
    e = grad * gain
    return scale * (e - jnp.mean(e, axis=-1, keepdims=True) - unit * jnp.mean(e * unit, axis=-1, keepdims=True))


def column_sum(v):
    return jnp.sum(v, axis=0, keepdims=True)


class Slots:
    def __init__(self, refs):
        self.refs = refs
        self.at = self.View(refs)

    class View:
        def __init__(self, refs):
            self.refs = refs

        def __getitem__(self, key):
            if isinstance(key, tuple):
                return self.refs[key[0]].at[key[1:]]
            return self.refs[key]

    def __getitem__(self, key):
        return self.refs[key[0]][key[1:]] if isinstance(key, tuple) else self.refs[key][...]

    def __setitem__(self, key, value):
        self.refs[key[0]][key[1:]] = value


def layer_kernel(
    counts, patches_in, cotangent_in, w_qkv_h, w_out_h, w_fc1_h, w_fc2_h,
    keys_row, ln1_gain, ln1_bias, b_query, b_value, b_out, ln2_gain, ln2_bias, b_fc1, b_fc2,
    layer_h, patches_h, fc1_share, fc2_share, out_share, qkv_share, small_share, hidden_share,
    act1_t_h, qkv_h, probs_h, mixed_t_h, kept_h, after_h,
    pool, wide, ring, core_in, first_in, second_in, third_in, fourth_in, home_in, vectors, vectors_in, heads, keys,
    load_sem, core_sem, stage_sem, home_sem, vector_sem,
):
    pool, wide = Slots(pool), Slots(wide)
    width = ln1_gain.shape[1]
    dp, rep = lax.axis_index("dp"), lax.axis_index("rep")
    far, near = dp // 4, lax.rem(dp // 2, 2)
    x, y, core = lax.rem(dp, 2), rep // 2, lax.rem(rep, 2)
    place = lambda far, near, x, y, core: (far * 4 + near * 2 + x, y * 2 + core)
    axes = {
        "c": (core, place(far, near, x, y, 1 - core)),
        "x": (x, place(far, near, 1 - x, y, core)),
        "y": (y, place(far, near, x, 1 - y, core)),
        "near": (near, place(far, 1 - near, x, y, core)),
        "far": (far, place(1 - far, near, x, y, core)),
    }

    barrier = pltpu.get_barrier_semaphore()
    for _, peer in axes.values():
        pl.semaphore_signal(barrier, inc=1, device_id=peer, device_id_type=MESH)

    started = {}

    def load(name, source, target):
        copy = pltpu.make_async_copy(source, target, load_sem.at[len(started)])
        copy.start()
        started[name] = copy

    def loaded(*names):
        for name in names:
            started[name].wait()

    def load_chunk(j):
        columns = slice(j * width, (j + 1) * width)
        load(f"w1_{j}", w_fc1_h.at[:, columns], pool.at[W1[j % 2]])
        load(f"w2_{j}", w_fc2_h.at[columns, :], pool.at[W2[j % 2]])

    W1, W2 = (3, 1), (5, 6)
    slots = patches_in.shape[0]
    images = width // PAD
    load("cotangent", cotangent_in, pool.at[8, :slots])
    load("patches_in", patches_in, pool.at[7, :slots])
    for k in range(3):
        load(f"w_in_{k}", w_qkv_h.at[:, k * width : (k + 1) * width], pool.at[4 + k])
    load("w_out_in", w_out_h, pool.at[1])
    load("w1_0", w_fc1_h.at[:, :width], pool.at[W1[0]])
    vectors[...] = jnp.zeros_like(vectors)
    heads[...] = head_mask()
    keys[...] = keys_row[...].T

    def tile_loop(body):
        for start in range(0, width, TILE):
            body(slice(start, start + TILE), start)

    def select(which, start):
        row = lax.broadcasted_iota(jnp.int32, (TILE, slots), 0) + start
        return jnp.where(row.astype(jnp.float32) == keys_row[which : which + 1, :], 1.0, 0.0).astype(jnp.bfloat16)

    def open_top(rows, start):
        pool[2, rows, :] = matmul(select(1, start), pool[8, :slots, :]).astype(jnp.bfloat16)

    def open_kept(rows, start):
        kept_rows = matmul(select(0, start), pool[7, :slots, :])
        wide[0, rows, :] = kept_rows
        unit, _ = normed_rows(kept_rows)
        act1 = (unit * ln1_gain[...] + ln1_bias[...]).astype(jnp.bfloat16)
        pool[8, rows, :] = act1
        pool[0, :, rows] = act1.T

    def project(source, target, bias):
        def body(rows, start):
            out = matmul(pool[8, rows, :], pool[source])
            pool[target, rows, :] = (out if bias is None else out + bias[...]).astype(jnp.bfloat16)

        tile_loop(body)

    loaded("cotangent")
    tile_loop(open_top)
    loaded("patches_in")
    tile_loop(open_kept)
    load("kept_out", wide.at[0], kept_h)
    load("act1_t_out", pool.at[0], act1_t_h)
    for k, (target, bias) in enumerate(((7, b_query), (4, None), (5, b_value))):
        loaded(f"w_in_{k}")
        project(4 + k, target, bias)
        load(f"qkv_out_{k}", pool.at[target], qkv_h.at[k])

    def attend(i, carry):
        rows = pl.ds(pl.multiple_of(i * PAD, PAD), PAD)
        row = lax.broadcasted_iota(jnp.int32, (PAD, GROUP), 0)
        head_of = lax.broadcasted_iota(jnp.int32, (PAD, GROUP), 1) // HEAD_DIM
        seen = row < counts[i]
        for g in range(width // GROUP):
            lanes = slice(g * GROUP, (g + 1) * GROUP)
            queries = spread_heads(pool[7, rows, lanes], heads[...])
            scores = matmul_nt(pool[4, rows, lanes], queries) * SCORE_SCALE
            scores = jnp.where(seen, scores, -1000000000.0)
            raised = jnp.exp(scores - jnp.max(scores, axis=0, keepdims=True))
            probs = (raised * (1.0 / jnp.sum(raised, axis=0, keepdims=True))).astype(jnp.bfloat16)
            pool[6, rows, lanes] = probs
            pool[8, rows, lanes] = fold_heads(matmul(probs.T, pool[5, rows, lanes]), head_of).astype(jnp.bfloat16)
        return carry

    lax.fori_loop(0, images, attend, 0, unroll=4)
    load("probs_out", pool.at[6], probs_h)
    loaded("w_out_in", "act1_t_out", "qkv_out_0", "qkv_out_1", "qkv_out_2")

    def close_attention(rows, start):
        mixed = pool[8, rows, :]
        pool[7, :, rows] = mixed.T
        after = wide[0, rows, :] + (matmul(mixed, pool[1]) + b_out[...])
        wide[1, rows, :] = after
        unit, _ = normed_rows(after)
        act2 = (unit * ln2_gain[...] + ln2_bias[...]).astype(jnp.bfloat16)
        pool[0, rows, :] = act2
        pool[4, :, rows] = act2.T

    tile_loop(close_attention)
    load("mixed_t_out", pool.at[7], mixed_t_h)
    load("after_out", wide.at[1], after_h)
    load("w2_0", w_fc2_h.at[:width, :], pool.at[W2[0]])
    pl.semaphore_wait(barrier, len(axes))

    units = []
    for j in range(4):
        units += [("fc2", j, h) for h in range(2)] + [("fc1", j, h) for h in range(2)]
    units += [("out", 0, h) for h in range(2)]
    units += [("qkv", k, h) for k in range(3) for h in range(2)]
    share_of = {"fc1": fc1_share, "out": out_share, "qkv": qkv_share}
    finished, delivered, pumped = set(), set(), []

    def remote(source, target, send, receive, peer):
        return pltpu.make_async_remote_copy(
            src_ref=source, dst_ref=target, send_sem=send, recv_sem=receive, device_id=peer, device_id_type=MESH
        )

    def core_copy(u):
        s, t = u % SENDS, u % TAKES
        return remote(ring.at[RING + s], core_in.at[t], core_sem.at[0, t], core_sem.at[1, t], axes["c"][1])

    def orders_of(u):
        assert (WAYS[u] == 0) == (units[u][0] == "fc2")
        return ORDERS[WAYS[u]]

    def kept(u, half, stage):
        return (u % RING, half, *(axes[name][0] for name in orders_of(u)[half][:stage]))

    def landing(u, half, stage):
        if stage == 0:
            return first_in, (u % FIRSTS, half)
        return (second_in, third_in, fourth_in)[stage - 1], (u % LATERS, half)

    def stage_copy(u, half, stage):
        index, peer = axes[orders_of(u)[half][stage]]
        target, at = landing(u, half, stage)
        slot = stage * LATERS + at[0]
        return remote(
            ring.at[(*kept(u, half, stage), 1 - index)], target.at[at],
            stage_sem.at[0, slot, half], stage_sem.at[1, slot, half], peer,
        )

    def home_copy(u, half, stage):
        _, j, h = units[u]
        slot = h if stage == 2 else 2 + h
        return remote(
            ring.at[kept(u, half, 2)], home_in.at[slot, half], home_sem.at[0, slot, half], home_sem.at[1, slot, half],
            axes["near" if stage == 2 else "far"][1],
        )

    def home_roles(u, stage):
        j = units[u][1]
        if stage == 2:
            return near != j % 2, near == j % 2
        return (near == j % 2) & (far != j // 2), (near == j % 2) & (far == j // 2)

    def stage_start(u, half, stage):
        if units[u][0] == "fc2" and stage >= 2:

            @pl.when(home_roles(u, stage)[0])
            def _():
                home_copy(u, half, stage).start()
        else:
            stage_copy(u, half, stage).start()

    def stage_finish(u, half, stage):
        if units[u][0] == "fc2" and stage >= 2:
            sends, takes = home_roles(u, stage)
            copy = home_copy(u, half, stage)

            @pl.when(sends)
            def _():
                copy.wait_send()

            @pl.when(takes)
            def _():
                copy.wait_recv()
                j, h = units[u][1:]
                slot = h if stage == 2 else 2 + h
                ring[kept(u, half, 2)] += home_in[slot, half]
        else:
            stage_copy(u, half, stage).wait()
            source, at = landing(u, half, stage)
            ring[kept(u, half, stage + 1)] += source[at]

    def deliver(u):
        kind, j, h = units[u]
        if kind == "fc2":

            @pl.when((near == j % 2) & (far == j // 2))
            def _():
                for half in range(2):
                    for q in range(4):
                        at = q * 32 + half * 16
                        fc2_share[at : at + 16, h * HALF : (h + 1) * HALF] = ring[(*kept(u, half, 2), q // 2, q % 2)]
        else:
            at = j * width + h * HALF
            for half in range(2):
                share_of[kind][half * 16 : (half + 1) * 16, at : at + HALF] = ring[kept(u, half, 4)]

    def core_finish(u):
        if u < 0 or u in finished:
            return
        finished.add(u)
        core_copy(u).wait()
        for half in range(2):
            for i in range(2):
                ring[u % RING, half, i] += core_in[u % TAKES, half, i]

    def vector_copy(stage):
        peer = axes[("c", "x", "y", "near", "far")[stage]][1]
        return remote(vectors, vectors_in.at[stage], vector_sem.at[0, stage], vector_sem.at[1, stage], peer)

    def vector_stage(stage):
        if stage > 0:
            vector_copy(stage - 1).wait()
            total = vectors[...] + vectors_in[stage - 1]
            vectors[...] = total
            if stage == 5:
                device = dp * 4 + rep
                block = pl.ds(pl.multiple_of(device // 4 * 128, 128), 128)
                small_share[...] = pltpu.roll(vectors[:8, block], lax.rem(128 - lax.rem(device, 4) * 32, 128), 1)
                block = pl.ds(pl.multiple_of(lax.rem(device, 8) * 128, 128), 128)
                rows = vectors[8:16, block]
                own = lax.broadcasted_iota(jnp.int32, rows.shape, 0) == device // 8
                hidden_share[...] = column_sum(jnp.where(own, rows, 0.0))
                return
        vector_copy(stage).start()

    def pump():
        for u, k in PLAN[len(pumped)]:
            if u == len(units):
                vector_stage(k)
                continue
            if k == 0:
                for v in range(u + 1):
                    core_finish(v)
            for half in range(2):
                if k > 0:
                    stage_finish(u, half, k - 1)
                if k < STAGES:
                    stage_start(u, half, k)
            if k == STAGES:
                deliver(u)
                delivered.add(u)
        pumped.append(True)

    def produce(u, left, right):
        kind, _, h = units[u]
        assert u < RING or u - RING in delivered
        columns = slice(h * HALF, (h + 1) * HALF)

        def part(owner, slot):
            if kind == "fc2":
                rows = [left[pl.ds(pl.multiple_of(b * 256 + owner * 128, 128), 128), :] for b in range(4)]
            else:
                rows = [left[pl.ds(pl.multiple_of(b * 64 + owner * 32, 32), 32), :] for b in range(16)]
            product = matmul(jnp.concatenate(rows, axis=0), right[:, columns])
            for b in range(16):
                if kind == "fc2":
                    names = {"x": b // 8, "y": b // 4 % 2, "near": b // 2 % 2, "far": b % 2}
                else:
                    names = {"far": b // 8, "near": b // 4 % 2, "x": b // 2 % 2, "y": b % 2}
                for half, order in enumerate(orders_of(u)):
                    at = b * 32 + half * 16
                    order = (*order, "near", "far")[:4]
                    ring[(slot, half, *(names[name] for name in order))] = product[at : at + 16]

        core_finish(u - TAKES // 2)
        part(1 - core, RING + u % SENDS)
        core_copy(u).start()
        part(core, u % RING)
        pump()

    def row_loop(body, unroll=False):
        def step(r, carry):
            body(pl.ds(pl.multiple_of(r * TILE, TILE), TILE))
            return carry

        parts = width // TILE // 2
        for part in range(2):
            lax.fori_loop(part * parts, (part + 1) * parts, step, 0, unroll=unroll)
            pump()

    def chunk_forward(j):
        w1 = pool.at[W1[j % 2]]

        def body(rows):
            for c in range(2):
                columns = slice(c * HALF, (c + 1) * HALF)
                hidden = slice(j * width + c * HALF, j * width + (c + 1) * HALF)
                value, slope = gelu_parts(matmul(pool[0, rows, :], w1[:, columns]) + b_fc1[:, hidden])
                value = value.astype(jnp.bfloat16)
                wide[2, rows, columns] = slope
                pool[8, rows, columns] = value
                pool[7, columns, rows] = value.T

        row_loop(body, unroll=True)

    def chunk_backward(j):
        w1, w2 = pool.at[W1[j % 2]], pool.at[W2[j % 2]]

        def body(rows):
            branch = matmul(pool[8, rows, :], w2[...])
            if j == 0:
                wide[1, rows, :] = branch
                vectors[7:8, :] += column_sum(pool[2, rows, :].astype(jnp.float32))
            else:
                wide[1, rows, :] += branch
            total = None
            for c in range(2):
                columns = slice(c * HALF, (c + 1) * HALF)
                grad = matmul_nt(pool[2, rows, :], w2[columns, :]) * wide[2, rows, columns]
                grad = grad.astype(jnp.bfloat16)
                pool[8, rows, columns] = grad
                vectors[8 + j : 9 + j, columns] += column_sum(grad.astype(jnp.float32))
                back = matmul_nt(grad, w1[:, columns])
                total = back if total is None else total + back
            if j == 0:
                wide[0, rows, :] = total
            else:
                wide[0, rows, :] += total

        row_loop(body)

    for j in range(4):
        loaded(f"w1_{j}")
        if j == 0:
            loaded("mixed_t_out", "probs_out")
        if j < 3:
            load_chunk(j + 1)
        else:
            load("w_out", w_out_h, pool.at[3])
            load("mixed_t", mixed_t_h, pool.at[5])
        chunk_forward(j)
        produce(4 * j, pool.at[7], pool.at[2])
        produce(4 * j + 1, pool.at[7], pool.at[2])
        if j == 0:
            loaded("kept_out", "after_out")
        loaded(f"w2_{j}")
        chunk_backward(j)
        if j == 3:
            load("after", after_h, wide.at[2])
            for k in range(2):
                load(f"qkv_{k}", qkv_h.at[k], pool.at[6 + k])
            load("probs", probs_h, pool.at[1])
        produce(4 * j + 2, pool.at[4], pool.at[8])
        produce(4 * j + 3, pool.at[4], pool.at[8])
        if j == 3:
            load("qkv_2", qkv_h.at[2], pool.at[8])

    loaded("after", "w_out")

    def middle(rows):
        after = wide[2, rows, :]
        unit, scale = normed_rows(after)
        grad = wide[0, rows, :]
        vectors[5:6, :] += column_sum(grad * unit)
        vectors[6:7, :] += column_sum(grad)
        grad = pool[2, rows, :].astype(jnp.float32) + norm_back(grad, ln2_gain[...], unit, scale)
        wide[0, rows, :] = grad
        pool[2, rows, :] = (after + (wide[1, rows, :] + b_fc2[...])).astype(jnp.bfloat16)
        branch = grad.astype(jnp.bfloat16)
        pool[0, rows, :] = branch
        vectors[4:5, :] += column_sum(branch.astype(jnp.float32))
        pool[4, rows, :] = matmul_nt(branch, pool[3]).astype(jnp.bfloat16)

    row_loop(middle)
    loaded("mixed_t")
    load("w_qkv_0", w_qkv_h.at[:, :width], pool.at[3])
    load("kept", kept_h, wide.at[1])
    produce(16, pool.at[5], pool.at[0])
    produce(17, pool.at[5], pool.at[0])
    load("w_qkv_1", w_qkv_h.at[:, width : 2 * width], pool.at[5])
    load("act1_t", act1_t_h, pool.at[0])
    loaded("qkv_0", "qkv_1", "qkv_2", "probs")

    def attend_back(i, carry):
        rows = pl.ds(pl.multiple_of(i * PAD, PAD), PAD)
        head_of = lax.broadcasted_iota(jnp.int32, (PAD, GROUP), 1) // HEAD_DIM
        for g in range(width // GROUP):
            lanes = slice(g * GROUP, (g + 1) * GROUP)
            queries = spread_heads(pool[6, rows, lanes], heads[...])
            keys, values = pool[7, rows, lanes], pool[8, rows, lanes]
            grad_mixed = spread_heads(pool[4, rows, lanes], heads[...])
            low_probs = pool[1, rows, lanes]
            probs = low_probs.astype(jnp.float32)
            grad_probs = matmul_nt(values, grad_mixed)
            grad_scores = probs * (grad_probs - column_sum(probs * grad_probs))
            grad_scores = grad_scores.astype(jnp.bfloat16)
            grad_queries = fold_heads(matmul(grad_scores.T, keys), head_of) * SCORE_SCALE
            grad_keys = matmul(grad_scores, queries) * SCORE_SCALE
            grad_values = matmul(low_probs, grad_mixed)
            pool[6, rows, lanes] = grad_queries.astype(jnp.bfloat16)
            pool[7, rows, lanes] = grad_keys.astype(jnp.bfloat16)
            pool[8, rows, lanes] = grad_values.astype(jnp.bfloat16)
        return carry

    for part in range(4):
        lax.fori_loop(part * images // 4, (part + 1) * images // 4, attend_back, 0, unroll=2)
        pump()
    load("w_qkv_2", w_qkv_h.at[:, 2 * width :], pool.at[4])

    block = 160

    def select_rows(r, column):
        rows = slice(r * block, (r + 1) * block)
        lane = lax.broadcasted_iota(jnp.int32, (block, width), 1)
        return rows, jnp.where(lane.astype(jnp.float32) == keys[rows, column : column + 1], 1.0, 0.0).astype(jnp.bfloat16)

    for r in range(slots // block):
        rows, select = select_rows(r, 1)
        pool[1, rows, :] = matmul(select, pool[2]).astype(jnp.bfloat16)
    load("layer", pool.at[1, :slots], layer_h)
    pump()

    loaded("act1_t")
    for k in range(3):
        produce(18 + 2 * k, pool.at[0], pool.at[6 + k])
        produce(19 + 2 * k, pool.at[0], pool.at[6 + k])

    loaded("w_qkv_0", "w_qkv_1", "w_qkv_2", "kept")

    def first(rows):
        grads = [pool[6 + k, rows, :] for k in range(3)]
        vectors[2:3, :] += column_sum(grads[0].astype(jnp.float32))
        vectors[3:4, :] += column_sum(grads[2].astype(jnp.float32))
        grad = matmul_nt(grads[0], pool[3]) + matmul_nt(grads[1], pool[5]) + matmul_nt(grads[2], pool[4])
        unit, scale = normed_rows(wide[1, rows, :])
        vectors[0:1, :] += column_sum(grad * unit)
        vectors[1:2, :] += column_sum(grad)
        grad = wide[0, rows, :] + norm_back(grad, ln1_gain[...], unit, scale)
        for k in range(3):
            piece = grad.astype(jnp.bfloat16)
            pool[6 + k, rows, :] = piece
            grad = grad - piece.astype(jnp.float32)

    row_loop(first)

    for r in range(slots // block):
        rows, select = select_rows(r, 0)
        pieces = [matmul(select, pool[6 + k]) for k in (2, 1, 0)]
        wide[2, rows, :] = (pieces[0] + pieces[1]) + pieces[2]
    load("patches", wide.at[2, :slots], patches_h)
    pump()
    pump()
    assert len(delivered) == len(units)
    loaded("layer", "patches")


def layer(counts, tensors, keys, vectors, dp, rep):
    slots, width = tensors[0].shape
    any_space, vmem = pl.BlockSpec(memory_space=pl.ANY), pl.BlockSpec(memory_space=pltpu.VMEM)
    shape = jax.ShapeDtypeStruct
    f32, bf16, devices = jnp.float32, jnp.bfloat16, dp * rep
    dma = pltpu.SemaphoreType.DMA
    piece = (16, HALF)
    square = (width, width)
    return pl.pallas_call(
        layer_kernel,
        in_specs=[pl.BlockSpec(memory_space=pltpu.SMEM)] + [any_space] * len(tensors) + [vmem] * (1 + len(vectors)),
        out_specs=[any_space] * 2 + [vmem] * 6 + [any_space] * 6,
        out_shape=[
            shape((slots, width), bf16), shape((slots, width), f32), shape((width // devices, 4 * width), f32),
            shape((4 * width // devices, width), f32), shape((width // devices, width), f32),
            shape((width // devices, 3 * width), f32), shape((8, 128), f32), shape((1, 128), f32),
            shape(square, bf16), shape((3, *square), bf16), shape(square, bf16), shape(square, bf16), shape(square, f32),
            shape(square, f32),
        ],
        scratch_shapes=[
            [pltpu.VMEM(square, bf16)] * 9, [pltpu.VMEM(square, f32)] * 3,
            pltpu.VMEM((RING + SENDS, 2, 2, 2, 2, 2, *piece), f32), pltpu.VMEM((TAKES, 2, 2, 2, 2, 2, *piece), f32),
            pltpu.VMEM((FIRSTS, 2, 2, 2, 2, *piece), f32), pltpu.VMEM((LATERS, 2, 2, 2, *piece), f32),
            pltpu.VMEM((LATERS, 2, 2, *piece), f32), pltpu.VMEM((LATERS, 2, *piece), f32),
            pltpu.VMEM((4, 2, 2, 2, *piece), f32), pltpu.VMEM((16, width), f32), pltpu.VMEM((5, 16, width), f32),
            pltpu.VMEM((GROUP, GROUP), bf16), pltpu.VMEM((slots, 8), f32),
            dma((48,)), dma((2, TAKES)), dma((2, 4 * LATERS, 2)), dma((2, 4, 2)), dma((2, 5)),
        ],
        compiler_params=pltpu.CompilerParams(collective_id=0, has_side_effects=True, vmem_limit_bytes=63 * MIB),
        name="layer",
    )(counts, *tensors, keys, *vectors)[:8]


def finish(results):
    count = len(results)
    parts = []
    for k, r in enumerate(results):
        rows = r.shape[0] // (2 if r.size > 600 * 1024 else 1)
        parts += [(k, start, rows) for start in range(0, r.shape[0], rows)]

    def kernel(*refs):
        held, into, out = refs[2 * count : 3 * count], refs[-2], refs[-1]
        arrive = [
            pltpu.make_async_copy(refs[k].at[pl.ds(at, n)], held[k].at[pl.ds(at, n)], into.at[i])
            for i, (k, at, n) in enumerate(parts)
        ]
        leave = [
            pltpu.make_async_copy(held[k].at[pl.ds(at, n)], refs[count + k].at[pl.ds(at, n)], out.at[i])
            for i, (k, at, n) in enumerate(parts)
        ]
        for copy in arrive:
            copy.start()
        for copy, onward in zip(arrive, leave):
            copy.wait()
            onward.start()
        for copy in leave:
            copy.wait()

    any_space = pl.BlockSpec(memory_space=pl.ANY)
    return pl.pallas_call(
        kernel,
        in_specs=[any_space] * count,
        out_specs=[any_space] * count,
        out_shape=[jax.ShapeDtypeStruct(r.shape, r.dtype) for r in results],
        scratch_shapes=[pltpu.VMEM(r.shape, r.dtype) for r in results]
        + [pltpu.SemaphoreType.DMA((len(parts),)), pltpu.SemaphoreType.DMA((len(parts),))],
        compiler_params=pltpu.CompilerParams(vmem_limit_bytes=60 * MIB),
        name="finish",
    )(*results)


def local_kernels(
    patches, keep, ln1_gain, ln1_bias, w_qkv, b_query, b_value, w_out, b_out, ln2_gain, ln2_bias, w_fc1, b_fc1, w_fc2,
    b_fc2, cotangent,
):
    dp, rep = lax.axis_size("dp"), lax.axis_size("rep")
    images, slots, width = patches.shape
    rows = images * slots
    kept = keep.T
    image = jnp.arange(images, dtype=jnp.int32) * PAD
    ids = jnp.arange(slots, dtype=jnp.int32)[:, None]
    upto = (ids >= ids.T).astype(jnp.float32)
    ranks = matmul(upto, kept.astype(jnp.float32)).astype(jnp.int32)
    counts = ranks[-1]
    keys = jnp.stack([
        jnp.where(kept == 1, image + ranks - 1, -1), jnp.where(ids < counts, image + ids, -1)
    ]).reshape(2, rows)
    keys = jnp.pad(keys.astype(jnp.float32), ((0, 6), (0, 0)))
    flat = lambda a: jnp.swapaxes(a, 0, 1).reshape(rows, width)
    row = lambda v: v.reshape(1, -1)
    *shares, small, hidden = layer(
        counts, [flat(patches), flat(cotangent), w_qkv, w_out, w_fc1, w_fc2], keys,
        [row(v) for v in (ln1_gain, ln1_bias, b_query, b_value, b_out, ln2_gain, ln2_bias, b_fc1, b_fc2)], dp, rep,
    )
    layer_rows, grad_patches, fc1_share, fc2_share, out_share, qkv_share = finish(shares)
    mine = small[:, : width // (dp * rep)]
    unflat = lambda a: jnp.swapaxes(a.reshape(slots, images, width), 0, 1)
    return (
        unflat(layer_rows), unflat(grad_patches), mine[0], mine[1], qkv_share, mine[2], mine[3], out_share, mine[4], mine[5],
        mine[6], fc1_share, hidden[0], fc2_share, mine[7],
    )


def normalize(v):
    centred = v - jnp.mean(v, axis=-1, keepdims=True)
    return centred * lax.rsqrt(jnp.mean(centred * centred, axis=-1, keepdims=True) + NORM_EPSILON)


def affine_norm(v, gain, shift):
    return normalize(v) * gain + shift


def exchange(parts, axis, stride, count):
    size = lax.axis_size(axis)
    index = lax.axis_index(axis)
    place = (index // stride) % count
    total = lax.dynamic_index_in_dim(parts, place, 0, keepdims=False)
    for step in range(1, count):
        pairs = []
        for source in range(size):
            own = (source // stride) % count
            target = source + (((own + step) % count) - own) * stride
            pairs.append((source, target))
        sent = lax.dynamic_index_in_dim(parts, (place + step) % count, 0, keepdims=False)
        total = total + lax.ppermute(sent, axis, pairs)
    return total


def scatter_sum(grad):
    rows, columns = grad.shape
    dp, rep = lax.axis_size("dp"), lax.axis_size("rep")
    z, y = dp // 2, rep // 2
    share = rows // (dp * rep)
    parts = grad.reshape(z, 2, y, 2, share, columns)
    parts = exchange(jnp.moveaxis(parts, 3, 0), "rep", 1, 2)
    half = columns // 2
    x_first, y_first = parts[..., :half], parts[..., half:]
    x_first = exchange(jnp.moveaxis(x_first, 1, 0), "dp", 1, 2)
    y_first = exchange(jnp.moveaxis(y_first, 2, 0), "rep", 2, y)
    x_first = exchange(jnp.moveaxis(x_first, 1, 0), "rep", 2, y)
    y_first = exchange(jnp.moveaxis(y_first, 1, 0), "dp", 1, 2)
    both = jnp.concatenate([x_first, y_first], axis=-1)
    return exchange(both, "dp", 2, z)


def scatter_vectors(vectors):
    joined = jnp.concatenate([v.reshape(lax.axis_size("dp") * lax.axis_size("rep"), -1) for v in vectors], axis=1)
    total = lax.psum_scatter(joined, ("dp", "rep"), scatter_dimension=0, tiled=True)[0]
    out, start = [], 0
    for v in vectors:
        length = v.shape[0] // (lax.axis_size("dp") * lax.axis_size("rep"))
        out.append(total[start : start + length])
        start += length
    return out


def local_permutes(
    patches,
    keep,
    ln1_gain,
    ln1_bias,
    w_qkv,
    b_query,
    b_value,
    w_out,
    b_out,
    ln2_gain,
    ln2_bias,
    w_fc1,
    b_fc1,
    w_fc2,
    b_fc2,
    cotangent,
):
    images, slot_count, width = patches.shape
    row_count = images * slot_count
    table, valid_slots = select_parts(keep, slot_count)
    kept = jnp.einsum(
        "bsp,bpd->bsd", table.astype(jnp.bfloat16), patches, preferred_element_type=jnp.float32
    ).reshape(row_count, width)
    normed_one, norm_one_back = jax.vjp(affine_norm, kept, ln1_gain, ln1_bias)
    act_one = normed_one.astype(jnp.bfloat16)
    bias_all = jnp.concatenate([b_query, jnp.zeros_like(b_query), b_value])
    qkv = (matmul(act_one, w_qkv) + bias_all).astype(jnp.bfloat16)
    qkv = qkv.reshape(images, slot_count, 3, HEADS, HEAD_DIM)
    queries, key_part, values = (qkv[:, :, 0], qkv[:, :, 1], qkv[:, :, 2])
    scores = (
        jnp.einsum("blhe,bmhe->bhlm", queries, key_part, preferred_element_type=jnp.float32)
        * SCORE_SCALE
    )
    scores = jnp.where(valid_slots[:, None, None, :] > 0, scores, -1000000000.0)
    attn_probs, softmax_back = jax.vjp(partial(jax.nn.softmax, axis=-1), scores)
    probs_low = attn_probs.astype(jnp.bfloat16)
    mixed_heads = jnp.einsum(
        "bhlm,bmhe->blhe", probs_low, values, preferred_element_type=jnp.float32
    )
    mixed_heads = mixed_heads.reshape(row_count, width).astype(jnp.bfloat16)
    after_attn = kept + (matmul(mixed_heads, w_out) + b_out)
    normed_two, norm_two_back = jax.vjp(affine_norm, after_attn, ln2_gain, ln2_bias)
    act_two = normed_two.astype(jnp.bfloat16)
    pre_gelu = matmul(act_two, w_fc1) + b_fc1
    gelu_full, gelu_back = jax.vjp(partial(jax.nn.gelu, approximate=False), pre_gelu)
    gelu_out = gelu_full.astype(jnp.bfloat16)
    mlp_out = matmul(gelu_out, w_fc2) + b_fc2
    row_mask = valid_slots.reshape(row_count, 1)
    layer_out = ((after_attn + mlp_out) * row_mask).astype(jnp.bfloat16)
    layer_out = layer_out.reshape(images, slot_count, width)
    grad_out = cotangent.astype(jnp.float32).reshape(row_count, width) * row_mask
    grad_top = grad_out.astype(jnp.bfloat16)
    grad_w_fc2 = matmul(gelu_out.T, grad_top)
    grad_b_fc2 = jnp.sum(grad_top.astype(jnp.float32), axis=0)
    (grad_pre_full,) = gelu_back(matmul(grad_top, w_fc2.T))
    grad_pre = grad_pre_full.astype(jnp.bfloat16)
    grad_w_fc1 = matmul(act_two.T, grad_pre)
    grad_b_fc1 = jnp.sum(grad_pre.astype(jnp.float32), axis=0)
    grad_norm_two, grad_ln2_gain, grad_ln2_bias = norm_two_back(matmul(grad_pre, w_fc1.T))
    grad_after = grad_out + grad_norm_two
    share_w_fc2 = scatter_sum(grad_w_fc2)
    share_w_fc1 = scatter_sum(grad_w_fc1)
    grad_branch = grad_after.astype(jnp.bfloat16)
    grad_w_out = matmul(mixed_heads.T, grad_branch)
    grad_b_out = jnp.sum(grad_branch.astype(jnp.float32), axis=0)
    grad_mixed = matmul(grad_branch, w_out.T).astype(jnp.bfloat16)
    grad_mixed = grad_mixed.reshape(images, slot_count, HEADS, HEAD_DIM)
    grad_probs = jnp.einsum(
        "blhe,bmhe->bhlm", grad_mixed, values, preferred_element_type=jnp.float32
    )
    grad_values = jnp.einsum(
        "bhlm,blhe->bmhe", probs_low, grad_mixed, preferred_element_type=jnp.float32
    )
    (grad_scores_full,) = softmax_back(grad_probs)
    grad_scores = grad_scores_full.astype(jnp.bfloat16)
    grad_queries = (
        jnp.einsum("bhlm,bmhe->blhe", grad_scores, key_part, preferred_element_type=jnp.float32)
        * SCORE_SCALE
    )
    grad_keys = (
        jnp.einsum("bhlm,blhe->bmhe", grad_scores, queries, preferred_element_type=jnp.float32)
        * SCORE_SCALE
    )
    grad_qkv = jnp.stack([grad_queries, grad_keys, grad_values], axis=2)
    grad_qkv = grad_qkv.reshape(row_count, 3 * width).astype(jnp.bfloat16)
    grad_w_qkv = matmul(act_one.T, grad_qkv)
    column_sums = jnp.sum(grad_qkv.astype(jnp.float32), axis=0)
    grad_b_query = column_sums[:width]
    grad_b_value = column_sums[2 * width :]
    grad_norm_one, grad_ln1_gain, grad_ln1_bias = norm_one_back(matmul(grad_qkv, w_qkv.T))
    grad_kept = grad_after + grad_norm_one
    share_w_out = scatter_sum(grad_w_out)
    share_w_qkv = scatter_sum(grad_w_qkv)
    small = scatter_vectors(
        [grad_ln1_gain, grad_ln1_bias, grad_b_query, grad_b_value, grad_b_out, grad_ln2_gain, grad_ln2_bias, grad_b_fc1, grad_b_fc2]
    )
    grad_patches = jnp.einsum(
        "bsp,bsd->bpd",
        table,
        grad_kept.reshape(images, slot_count, width),
        precision=lax.Precision.HIGHEST,
    )
    return (
        layer_out,
        grad_patches,
        small[0],
        small[1],
        share_w_qkv,
        small[2],
        small[3],
        share_w_out,
        small[4],
        small[5],
        small[6],
        share_w_fc1,
        small[7],
        share_w_fc2,
        small[8],
    )


def solution(mesh):
    in_specs = (
        P(("dp", "rep"), None, None),
        P(("dp", "rep"), None),
        P(),
        P(),
        P(),
        P(),
        P(),
        P(),
        P(),
        P(),
        P(),
        P(),
        P(),
        P(),
        P(),
        P(("dp", "rep"), None, None),
    )
    out_specs = (
        P(("dp", "rep"), None, None),
        P(("dp", "rep"), None, None),
        P(("dp", "rep")),
        P(("dp", "rep")),
        P(("dp", "rep"), None),
        P(("dp", "rep")),
        P(("dp", "rep")),
        P(("dp", "rep"), None),
        P(("dp", "rep")),
        P(("dp", "rep")),
        P(("dp", "rep")),
        P(("dp", "rep"), None),
        P(("dp", "rep")),
        P(("dp", "rep"), None),
        P(("dp", "rep")),
    )
    fits = mesh.shape["dp"] == 8 and mesh.shape["rep"] == 4
    local = local_kernels if fits else local_permutes
    return jax.shard_map(local, mesh=mesh, in_specs=in_specs, out_specs=out_specs, check_vma=False)
```

```python
from functools import partial

import jax
import jax.numpy as jnp
from jax import lax
from jax.experimental import pallas as pl
from jax.experimental.pallas import tpu as pltpu
from jax.sharding import PartitionSpec as P

HEADS = 16
HEAD_DIM = 64
NORM_EPSILON = 1e-06
SCORE_SCALE = 0.125
PAD = 64
GROUP = 256
MIB = 1 << 20
NT = (((1,), (1,)), ((), ()))


def select_parts(keep, slot_count):
    slot_ids = jnp.arange(slot_count, dtype=jnp.int32)
    ranks = jnp.cumsum(keep, axis=1) - 1
    table = (ranks[:, None, :] == slot_ids[None, :, None]) & (keep[:, None, :] == 1)
    counts = jnp.sum(keep, axis=1)
    valid_slots = (slot_ids[None, :] < counts[:, None]).astype(jnp.float32)
    return (table.astype(jnp.float32), valid_slots)


def matmul(left, right):
    return jnp.dot(left, right, preferred_element_type=jnp.float32)


def matmul_nt(left, right):
    return lax.dot_general(left, right, NT, preferred_element_type=jnp.float32)


def normed_rows(v):
    centred = v - jnp.mean(v, axis=-1, keepdims=True)
    scale = lax.rsqrt(jnp.mean(centred * centred, axis=-1, keepdims=True) + NORM_EPSILON)
    return centred * scale, scale


def head_mask():
    row = lax.broadcasted_iota(jnp.int32, (GROUP, GROUP), 0) // HEAD_DIM
    lane = lax.broadcasted_iota(jnp.int32, (GROUP, GROUP), 1) // HEAD_DIM
    return jnp.where(row == lane, 1.0, 0.0).astype(jnp.bfloat16)


def spread_heads(v, heads):
    return jnp.concatenate([v] * 4, axis=0) * heads


def fold_heads(v, head_of):
    out = v[:PAD]
    for h in range(1, 4):
        out = jnp.where(head_of == h, v[h * PAD : (h + 1) * PAD], out)
    return out


TILE = 256
HALF = 512
RING = 11
SENDS, TAKES = 3, 4
STAGES = 4
FIRSTS, LATERS = 5, 9
PLAN = (
    (), (), (), ((0, 0),), ((1, 0),), ((0, 1),), (), (), ((1, 1), (2, 0)), ((0, 2),), ((1, 2), (3, 0)), (), ((0, 3),
    (2, 1), (4, 0)), ((1, 3),), ((3, 1), (5, 0)), (), (), ((0, 4), (4, 1)), (), ((6, 0),), ((2, 2), (5, 1), (4, 2),
    (7, 0)), ((1, 4), (8, 0)), ((6, 1),), ((2, 3), (4, 3), (3, 2)), ((5, 2),), ((9, 0),), ((8, 1), (3, 3), (7, 1),
    (9, 1), (6, 2), (10, 0), (8, 2), (2, 4)), ((11, 0),), ((4, 4), (5, 3), (7, 2), (6, 3), (9, 2)), ((3, 4), (12,
    0)), ((11, 1),), ((7, 3), (13, 0)), (), ((10, 1), (12, 1), (8, 3), (13, 1), (10, 2), (5, 4), (14, 0)), ((6, 4),
    (8, 4), (12, 2)), (), ((9, 3), (10, 3), (13, 2), (12, 3), (15, 0)), ((11, 2), (14, 1)), ((7, 4), (9, 4), (10,
    4), (11, 3), (15, 1), (16, 0)), ((13, 3), (14, 2)), ((15, 2), (17, 0)), ((12, 4),), ((11, 4),), ((16, 1),), (),
    ((13, 4), (18, 0)), ((17, 1),), ((14, 3), (15, 3), (16, 2), (19, 0)), ((17, 2), (18, 1), (20, 0)), ((24, 0),
    (14, 4), (15, 4), (16, 3), (17, 3), (19, 1), (24, 1)), ((20, 1), (18, 2), (16, 4), (19, 2), (17, 4), (21, 0),
    (24, 2), (19, 3), (20, 2), (18, 3), (19, 4), (22, 0), (20, 3), (18, 4), (21, 1), (20, 4), (24, 3), (23, 0), (22,
    1), (21, 2), (24, 4), (23, 1), (21, 3), (22, 2), (24, 5), (23, 2), (21, 4), (22, 3), (23, 3), (22, 4), (23, 4)),
)
WAYS = (0, 0, 1, 1, 0, 0, 1, 2, 0, 0, 2, 1, 0, 0, 3, 3, 3, 1, 1, 3, 3, 1, 1, 3)
ORDERS = (
    (("x", "y"), ("y", "x")),
    (("x", "near", "y", "far"), ("y", "near", "x", "far")),
    (("near", "x", "y", "far"), ("near", "y", "x", "far")),
    (("x", "y", "near", "far"), ("y", "x", "near", "far")),
)
MESH = pl.DeviceIdType.MESH


def gelu_parts(x):
    cdf = 0.5 * (1.0 + lax.erf(x * 0.7071067811865476))
    slope = cdf + x * (0.3989422804014327 * jnp.exp(-0.5 * (x * x)))
    return x * cdf, slope


def norm_back(grad, gain, unit, scale):
    e = grad * gain
    return scale * (e - jnp.mean(e, axis=-1, keepdims=True) - unit * jnp.mean(e * unit, axis=-1, keepdims=True))


def column_sum(v):
    return jnp.sum(v, axis=0, keepdims=True)


class Slots:
    def __init__(self, refs):
        self.refs = refs
        self.at = self.View(refs)

    class View:
        def __init__(self, refs):
            self.refs = refs

        def __getitem__(self, key):
            if isinstance(key, tuple):
                return self.refs[key[0]].at[key[1:]]
            return self.refs[key]

    def __getitem__(self, key):
        return self.refs[key[0]][key[1:]] if isinstance(key, tuple) else self.refs[key][...]

    def __setitem__(self, key, value):
        self.refs[key[0]][key[1:]] = value


def layer_kernel(
    counts, patches_in, cotangent_in, w_qkv_h, w_out_h, w_fc1_h, w_fc2_h,
    keys_row, ln1_gain, ln1_bias, b_query, b_value, b_out, ln2_gain, ln2_bias, b_fc1, b_fc2,
    layer_h, patches_h, fc1_share, fc2_share, out_share, qkv_share, small_share, hidden_share,
    act1_t_h, qkv_h, probs_h, mixed_t_h, kept_h, after_h,
    pool, wide, ring, core_in, first_in, second_in, third_in, fourth_in, home_in, vectors, vectors_in, heads, keys,
    load_sem, core_sem, stage_sem, home_sem, vector_sem,
):
    pool, wide = Slots(pool), Slots(wide)
    width = ln1_gain.shape[1]
    dp, rep = lax.axis_index("dp"), lax.axis_index("rep")
    far, near = dp // 4, lax.rem(dp // 2, 2)
    x, y, core = lax.rem(dp, 2), rep // 2, lax.rem(rep, 2)
    place = lambda far, near, x, y, core: (far * 4 + near * 2 + x, y * 2 + core)
    axes = {
        "c": (core, place(far, near, x, y, 1 - core)),
        "x": (x, place(far, near, 1 - x, y, core)),
        "y": (y, place(far, near, x, 1 - y, core)),
        "near": (near, place(far, 1 - near, x, y, core)),
        "far": (far, place(1 - far, near, x, y, core)),
    }

    barrier = pltpu.get_barrier_semaphore()
    for _, peer in axes.values():
        pl.semaphore_signal(barrier, inc=1, device_id=peer, device_id_type=MESH)

    started = {}

    def load(name, source, target):
        copy = pltpu.make_async_copy(source, target, load_sem.at[len(started)])
        copy.start()
        started[name] = copy

    def loaded(*names):
        for name in names:
            started[name].wait()

    def load_chunk(j):
        columns = slice(j * width, (j + 1) * width)
        load(f"w1_{j}", w_fc1_h.at[:, columns], pool.at[W1[j % 2]])
        load(f"w2_{j}", w_fc2_h.at[columns, :], pool.at[W2[j % 2]])

    W1, W2 = (3, 1), (5, 6)
    slots = patches_in.shape[0]
    images = width // PAD
    load("cotangent", cotangent_in, pool.at[8, :slots])
    load("patches_in", patches_in, pool.at[7, :slots])
    for k in range(3):
        load(f"w_in_{k}", w_qkv_h.at[:, k * width : (k + 1) * width], pool.at[4 + k])
    load("w_out_in", w_out_h, pool.at[1])
    load("w1_0", w_fc1_h.at[:, :width], pool.at[W1[0]])
    vectors[...] = jnp.zeros_like(vectors)
    heads[...] = head_mask()
    keys[...] = keys_row[...].T

    def tile_loop(body):
        for start in range(0, width, TILE):
            body(slice(start, start + TILE), start)

    def select(which, start):
        row = lax.broadcasted_iota(jnp.int32, (TILE, slots), 0) + start
        return jnp.where(row.astype(jnp.float32) == keys_row[which : which + 1, :], 1.0, 0.0).astype(jnp.bfloat16)

    def open_top(rows, start):
        pool[2, rows, :] = matmul(select(1, start), pool[8, :slots, :]).astype(jnp.bfloat16)

    def open_kept(rows, start):
        kept_rows = matmul(select(0, start), pool[7, :slots, :])
        wide[0, rows, :] = kept_rows
        unit, _ = normed_rows(kept_rows)
        act1 = (unit * ln1_gain[...] + ln1_bias[...]).astype(jnp.bfloat16)
        pool[8, rows, :] = act1
        pool[0, :, rows] = act1.T

    def project(source, target, bias):
        def body(rows, start):
            out = matmul(pool[8, rows, :], pool[source])
            pool[target, rows, :] = (out if bias is None else out + bias[...]).astype(jnp.bfloat16)

        tile_loop(body)

    loaded("cotangent")
    tile_loop(open_top)
    loaded("patches_in")
    tile_loop(open_kept)
    load("kept_out", wide.at[0], kept_h)
    load("act1_t_out", pool.at[0], act1_t_h)
    for k, (target, bias) in enumerate(((7, b_query), (4, None), (5, b_value))):
        loaded(f"w_in_{k}")
        project(4 + k, target, bias)
        load(f"qkv_out_{k}", pool.at[target], qkv_h.at[k])

    def attend(i, carry):
        rows = pl.ds(pl.multiple_of(i * PAD, PAD), PAD)
        row = lax.broadcasted_iota(jnp.int32, (PAD, GROUP), 0)
        head_of = lax.broadcasted_iota(jnp.int32, (PAD, GROUP), 1) // HEAD_DIM
        seen = row < counts[i]
        for g in range(width // GROUP):
            lanes = slice(g * GROUP, (g + 1) * GROUP)
            queries = spread_heads(pool[7, rows, lanes], heads[...])
            scores = matmul_nt(pool[4, rows, lanes], queries) * SCORE_SCALE
            scores = jnp.where(seen, scores, -1000000000.0)
            raised = jnp.exp(scores - jnp.max(scores, axis=0, keepdims=True))
            probs = (raised * (1.0 / jnp.sum(raised, axis=0, keepdims=True))).astype(jnp.bfloat16)
            pool[6, rows, lanes] = probs
            pool[8, rows, lanes] = fold_heads(matmul(probs.T, pool[5, rows, lanes]), head_of).astype(jnp.bfloat16)
        return carry

    lax.fori_loop(0, images, attend, 0, unroll=4)
    load("probs_out", pool.at[6], probs_h)
    loaded("w_out_in", "act1_t_out", "qkv_out_0", "qkv_out_1", "qkv_out_2")

    def close_attention(rows, start):
        mixed = pool[8, rows, :]
        pool[7, :, rows] = mixed.T
        after = wide[0, rows, :] + (matmul(mixed, pool[1]) + b_out[...])
        wide[1, rows, :] = after
        unit, _ = normed_rows(after)
        act2 = (unit * ln2_gain[...] + ln2_bias[...]).astype(jnp.bfloat16)
        pool[0, rows, :] = act2
        pool[4, :, rows] = act2.T

    tile_loop(close_attention)
    load("mixed_t_out", pool.at[7], mixed_t_h)
    load("after_out", wide.at[1], after_h)
    load("w2_0", w_fc2_h.at[:width, :], pool.at[W2[0]])
    pl.semaphore_wait(barrier, len(axes))

    units = []
    for j in range(4):
        units += [("fc2", j, h) for h in range(2)] + [("fc1", j, h) for h in range(2)]
    units += [("out", 0, h) for h in range(2)]
    units += [("qkv", k, h) for k in range(3) for h in range(2)]
    share_of = {"fc1": fc1_share, "out": out_share, "qkv": qkv_share}
    finished, delivered, pumped = set(), set(), []

    def remote(source, target, send, receive, peer):
        return pltpu.make_async_remote_copy(
            src_ref=source, dst_ref=target, send_sem=send, recv_sem=receive, device_id=peer, device_id_type=MESH
        )

    def core_copy(u):
        s, t = u % SENDS, u % TAKES
        return remote(ring.at[RING + s], core_in.at[t], core_sem.at[0, t], core_sem.at[1, t], axes["c"][1])

    def orders_of(u):
        assert (WAYS[u] == 0) == (units[u][0] == "fc2")
        return ORDERS[WAYS[u]]

    def kept(u, half, stage):
        return (u % RING, half, *(axes[name][0] for name in orders_of(u)[half][:stage]))

    def landing(u, half, stage):
        if stage == 0:
            return first_in, (u % FIRSTS, half)
        return (second_in, third_in, fourth_in)[stage - 1], (u % LATERS, half)

    def stage_copy(u, half, stage):
        index, peer = axes[orders_of(u)[half][stage]]
        target, at = landing(u, half, stage)
        slot = stage * LATERS + at[0]
        return remote(
            ring.at[(*kept(u, half, stage), 1 - index)], target.at[at],
            stage_sem.at[0, slot, half], stage_sem.at[1, slot, half], peer,
        )

    def home_copy(u, half, stage):
        _, j, h = units[u]
        slot = h if stage == 2 else 2 + h
        return remote(
            ring.at[kept(u, half, 2)], home_in.at[slot, half], home_sem.at[0, slot, half], home_sem.at[1, slot, half],
            axes["near" if stage == 2 else "far"][1],
        )

    def home_roles(u, stage):
        j = units[u][1]
        if stage == 2:
            return near != j % 2, near == j % 2
        return (near == j % 2) & (far != j // 2), (near == j % 2) & (far == j // 2)

    def stage_start(u, half, stage):
        if units[u][0] == "fc2" and stage >= 2:

            @pl.when(home_roles(u, stage)[0])
            def _():
                home_copy(u, half, stage).start()
        else:
            stage_copy(u, half, stage).start()

    def stage_finish(u, half, stage):
        if units[u][0] == "fc2" and stage >= 2:
            sends, takes = home_roles(u, stage)
            copy = home_copy(u, half, stage)

            @pl.when(sends)
            def _():
                copy.wait_send()

            @pl.when(takes)
            def _():
                copy.wait_recv()
                j, h = units[u][1:]
                slot = h if stage == 2 else 2 + h
                ring[kept(u, half, 2)] += home_in[slot, half]
        else:
            stage_copy(u, half, stage).wait()
            source, at = landing(u, half, stage)
            ring[kept(u, half, stage + 1)] += source[at]

    def deliver(u):
        kind, j, h = units[u]
        if kind == "fc2":

            @pl.when((near == j % 2) & (far == j // 2))
            def _():
                for half in range(2):
                    for q in range(4):
                        at = q * 32 + half * 16
                        fc2_share[at : at + 16, h * HALF : (h + 1) * HALF] = ring[(*kept(u, half, 2), q // 2, q % 2)]
        else:
            at = j * width + h * HALF
            for half in range(2):
                share_of[kind][half * 16 : (half + 1) * 16, at : at + HALF] = ring[kept(u, half, 4)]

    def core_finish(u):
        if u < 0 or u in finished:
            return
        finished.add(u)
        core_copy(u).wait()
        for half in range(2):
            for i in range(2):
                ring[u % RING, half, i] += core_in[u % TAKES, half, i]

    def vector_copy(stage):
        peer = axes[("c", "x", "y", "near", "far")[stage]][1]
        return remote(vectors, vectors_in.at[stage], vector_sem.at[0, stage], vector_sem.at[1, stage], peer)

    def vector_stage(stage):
        if stage > 0:
            vector_copy(stage - 1).wait()
            total = vectors[...] + vectors_in[stage - 1]
            vectors[...] = total
            if stage == 5:
                device = dp * 4 + rep
                block = pl.ds(pl.multiple_of(device // 4 * 128, 128), 128)
                small_share[...] = pltpu.roll(vectors[:8, block], lax.rem(128 - lax.rem(device, 4) * 32, 128), 1)
                block = pl.ds(pl.multiple_of(lax.rem(device, 8) * 128, 128), 128)
                rows = vectors[8:16, block]
                own = lax.broadcasted_iota(jnp.int32, rows.shape, 0) == device // 8
                hidden_share[...] = column_sum(jnp.where(own, rows, 0.0))
                return
        vector_copy(stage).start()

    def pump():
        for u, k in PLAN[len(pumped)]:
            if u == len(units):
                vector_stage(k)
                continue
            if k == 0:
                for v in range(u + 1):
                    core_finish(v)
            for half in range(2):
                if k > 0:
                    stage_finish(u, half, k - 1)
                if k < STAGES:
                    stage_start(u, half, k)
            if k == STAGES:
                deliver(u)
                delivered.add(u)
        pumped.append(True)

    def produce(u, left, right):
        kind, _, h = units[u]
        assert u < RING or u - RING in delivered
        columns = slice(h * HALF, (h + 1) * HALF)

        def part(owner, slot):
            if kind == "fc2":
                rows = [left[pl.ds(pl.multiple_of(b * 256 + owner * 128, 128), 128), :] for b in range(4)]
            else:
                rows = [left[pl.ds(pl.multiple_of(b * 64 + owner * 32, 32), 32), :] for b in range(16)]
            product = matmul(jnp.concatenate(rows, axis=0), right[:, columns])
            for b in range(16):
                if kind == "fc2":
                    names = {"x": b // 8, "y": b // 4 % 2, "near": b // 2 % 2, "far": b % 2}
                else:
                    names = {"far": b // 8, "near": b // 4 % 2, "x": b // 2 % 2, "y": b % 2}
                for half, order in enumerate(orders_of(u)):
                    at = b * 32 + half * 16
                    order = (*order, "near", "far")[:4]
                    ring[(slot, half, *(names[name] for name in order))] = product[at : at + 16]

        core_finish(u - TAKES // 2)
        part(1 - core, RING + u % SENDS)
        core_copy(u).start()
        part(core, u % RING)
        pump()

    def row_loop(body, unroll=False):
        def step(r, carry):
            body(pl.ds(pl.multiple_of(r * TILE, TILE), TILE))
            return carry

        parts = width // TILE // 2
        for part in range(2):
            lax.fori_loop(part * parts, (part + 1) * parts, step, 0, unroll=unroll)
            pump()

    def chunk_forward(j):
        w1 = pool.at[W1[j % 2]]

        def body(rows):
            for c in range(2):
                columns = slice(c * HALF, (c + 1) * HALF)
                hidden = slice(j * width + c * HALF, j * width + (c + 1) * HALF)
                hidden_in = matmul(pool[0, rows, :], w1[:, columns]) + b_fc1[:, hidden]
                value, slope = gelu_parts(hidden_in)
                value = value.astype(jnp.bfloat16)
                wide[2, rows, columns] = hidden_in if j == 0 else slope
                pool[8, rows, columns] = value
                pool[7, columns, rows] = value.T

        row_loop(body, unroll=True)

    def chunk_backward(j):
        w1, w2 = pool.at[W1[j % 2]], pool.at[W2[j % 2]]

        def body(rows):
            branch = matmul(pool[8, rows, :], w2[...])
            if j == 0:
                wide[1, rows, :] = branch
                vectors[7:8, :] += column_sum(pool[2, rows, :].astype(jnp.float32))
            else:
                wide[1, rows, :] += branch
            total = None
            for c in range(2):
                columns = slice(c * HALF, (c + 1) * HALF)
                slope = wide[2, rows, columns]
                if j == 0:
                    slope = gelu_parts(slope)[1]
                grad = matmul_nt(pool[2, rows, :], w2[columns, :]) * slope
                grad = grad.astype(jnp.bfloat16)
                pool[8, rows, columns] = grad
                vectors[8 + j : 9 + j, columns] += column_sum(grad.astype(jnp.float32))
                back = matmul_nt(grad, w1[:, columns])
                total = back if total is None else total + back
            if j == 0:
                wide[0, rows, :] = total
            else:
                wide[0, rows, :] += total

        row_loop(body)

    for j in range(4):
        loaded(f"w1_{j}")
        if j == 0:
            loaded("mixed_t_out", "probs_out")
        if j < 3:
            load_chunk(j + 1)
        else:
            load("w_out", w_out_h, pool.at[3])
            load("mixed_t", mixed_t_h, pool.at[5])
        chunk_forward(j)
        produce(4 * j, pool.at[7], pool.at[2])
        produce(4 * j + 1, pool.at[7], pool.at[2])
        if j == 0:
            loaded("kept_out", "after_out")
        loaded(f"w2_{j}")
        chunk_backward(j)
        if j == 3:
            load("after", after_h, wide.at[2])
            for k in range(2):
                load(f"qkv_{k}", qkv_h.at[k], pool.at[6 + k])
            load("probs", probs_h, pool.at[1])
        produce(4 * j + 2, pool.at[4], pool.at[8])
        produce(4 * j + 3, pool.at[4], pool.at[8])
        if j == 3:
            load("qkv_2", qkv_h.at[2], pool.at[8])

    loaded("after", "w_out")

    def middle(rows):
        after = wide[2, rows, :]
        unit, scale = normed_rows(after)
        grad = wide[0, rows, :]
        vectors[5:6, :] += column_sum(grad * unit)
        vectors[6:7, :] += column_sum(grad)
        grad = pool[2, rows, :].astype(jnp.float32) + norm_back(grad, ln2_gain[...], unit, scale)
        wide[0, rows, :] = grad
        pool[2, rows, :] = (after + (wide[1, rows, :] + b_fc2[...])).astype(jnp.bfloat16)
        branch = grad.astype(jnp.bfloat16)
        pool[0, rows, :] = branch
        vectors[4:5, :] += column_sum(branch.astype(jnp.float32))
        pool[4, rows, :] = matmul_nt(branch, pool[3]).astype(jnp.bfloat16)

    row_loop(middle)
    loaded("mixed_t")
    load("w_qkv_0", w_qkv_h.at[:, :width], pool.at[3])
    load("kept", kept_h, wide.at[1])
    produce(16, pool.at[5], pool.at[0])
    produce(17, pool.at[5], pool.at[0])
    load("w_qkv_1", w_qkv_h.at[:, width : 2 * width], pool.at[5])
    load("act1_t", act1_t_h, pool.at[0])
    loaded("qkv_0", "qkv_1", "qkv_2", "probs")

    def attend_back(i, carry):
        rows = pl.ds(pl.multiple_of(i * PAD, PAD), PAD)
        head_of = lax.broadcasted_iota(jnp.int32, (PAD, GROUP), 1) // HEAD_DIM
        for g in range(width // GROUP):
            lanes = slice(g * GROUP, (g + 1) * GROUP)
            queries = spread_heads(pool[6, rows, lanes], heads[...])
            keys, values = pool[7, rows, lanes], pool[8, rows, lanes]
            grad_mixed = spread_heads(pool[4, rows, lanes], heads[...])
            low_probs = pool[1, rows, lanes]
            probs = low_probs.astype(jnp.float32)
            grad_probs = matmul_nt(values, grad_mixed)
            grad_scores = probs * (grad_probs - column_sum(probs * grad_probs))
            grad_scores = grad_scores.astype(jnp.bfloat16)
            grad_queries = fold_heads(matmul(grad_scores.T, keys), head_of) * SCORE_SCALE
            grad_keys = matmul(grad_scores, queries) * SCORE_SCALE
            grad_values = matmul(low_probs, grad_mixed)
            pool[6, rows, lanes] = grad_queries.astype(jnp.bfloat16)
            pool[7, rows, lanes] = grad_keys.astype(jnp.bfloat16)
            pool[8, rows, lanes] = grad_values.astype(jnp.bfloat16)
        return carry

    for part in range(4):
        lax.fori_loop(part * images // 4, (part + 1) * images // 4, attend_back, 0, unroll=2)
        pump()
    load("w_qkv_2", w_qkv_h.at[:, 2 * width :], pool.at[4])

    block = 160

    def select_rows(r, column):
        rows = slice(r * block, (r + 1) * block)
        lane = lax.broadcasted_iota(jnp.int32, (block, width), 1)
        return rows, jnp.where(lane.astype(jnp.float32) == keys[rows, column : column + 1], 1.0, 0.0).astype(jnp.bfloat16)

    for r in range(slots // block):
        rows, select = select_rows(r, 1)
        pool[1, rows, :] = matmul(select, pool[2]).astype(jnp.bfloat16)
    load("layer", pool.at[1, :slots], layer_h)
    pump()

    loaded("act1_t")
    for k in range(3):
        produce(18 + 2 * k, pool.at[0], pool.at[6 + k])
        produce(19 + 2 * k, pool.at[0], pool.at[6 + k])

    loaded("w_qkv_0", "w_qkv_1", "w_qkv_2", "kept")

    def first(rows):
        grads = [pool[6 + k, rows, :] for k in range(3)]
        vectors[2:3, :] += column_sum(grads[0].astype(jnp.float32))
        vectors[3:4, :] += column_sum(grads[2].astype(jnp.float32))
        grad = matmul_nt(grads[0], pool[3]) + matmul_nt(grads[1], pool[5]) + matmul_nt(grads[2], pool[4])
        unit, scale = normed_rows(wide[1, rows, :])
        vectors[0:1, :] += column_sum(grad * unit)
        vectors[1:2, :] += column_sum(grad)
        grad = wide[0, rows, :] + norm_back(grad, ln1_gain[...], unit, scale)
        for k in range(3):
            piece = grad.astype(jnp.bfloat16)
            pool[6 + k, rows, :] = piece
            grad = grad - piece.astype(jnp.float32)

    row_loop(first)

    for r in range(slots // block):
        rows, select = select_rows(r, 0)
        pieces = [matmul(select, pool[6 + k]) for k in (2, 1, 0)]
        wide[2, rows, :] = (pieces[0] + pieces[1]) + pieces[2]
    load("patches", wide.at[2, :slots], patches_h)
    pump()
    pump()
    assert len(delivered) == len(units)
    loaded("layer", "patches")


def layer(counts, tensors, keys, vectors, dp, rep):
    slots, width = tensors[0].shape
    any_space, vmem = pl.BlockSpec(memory_space=pl.ANY), pl.BlockSpec(memory_space=pltpu.VMEM)
    shape = jax.ShapeDtypeStruct
    f32, bf16, devices = jnp.float32, jnp.bfloat16, dp * rep
    dma = pltpu.SemaphoreType.DMA
    piece = (16, HALF)
    square = (width, width)
    return pl.pallas_call(
        layer_kernel,
        in_specs=[pl.BlockSpec(memory_space=pltpu.SMEM)] + [any_space] * len(tensors) + [vmem] * (1 + len(vectors)),
        out_specs=[any_space] * 2 + [vmem] * 6 + [any_space] * 6,
        out_shape=[
            shape((slots, width), bf16), shape((slots, width), f32), shape((width // devices, 4 * width), f32),
            shape((4 * width // devices, width), f32), shape((width // devices, width), f32),
            shape((width // devices, 3 * width), f32), shape((8, 128), f32), shape((1, 128), f32),
            shape(square, bf16), shape((3, *square), bf16), shape(square, bf16), shape(square, bf16), shape(square, f32),
            shape(square, f32),
        ],
        scratch_shapes=[
            [pltpu.VMEM(square, bf16)] * 9, [pltpu.VMEM(square, f32)] * 3,
            pltpu.VMEM((RING + SENDS, 2, 2, 2, 2, 2, *piece), f32), pltpu.VMEM((TAKES, 2, 2, 2, 2, 2, *piece), f32),
            pltpu.VMEM((FIRSTS, 2, 2, 2, 2, *piece), f32), pltpu.VMEM((LATERS, 2, 2, 2, *piece), f32),
            pltpu.VMEM((LATERS, 2, 2, *piece), f32), pltpu.VMEM((LATERS, 2, *piece), f32),
            pltpu.VMEM((4, 2, 2, 2, *piece), f32), pltpu.VMEM((16, width), f32), pltpu.VMEM((5, 16, width), f32),
            pltpu.VMEM((GROUP, GROUP), bf16), pltpu.VMEM((slots, 8), f32),
            dma((48,)), dma((2, TAKES)), dma((2, 4 * LATERS, 2)), dma((2, 4, 2)), dma((2, 5)),
        ],
        compiler_params=pltpu.CompilerParams(collective_id=0, has_side_effects=True, vmem_limit_bytes=63 * MIB),
        name="layer",
    )(counts, *tensors, keys, *vectors)[:8]


def finish(results):
    count = len(results)
    parts = []
    for k, r in enumerate(results):
        rows = r.shape[0] // (2 if r.size > 600 * 1024 else 1)
        parts += [(k, start, rows) for start in range(0, r.shape[0], rows)]

    def kernel(*refs):
        held, into, out = refs[2 * count : 3 * count], refs[-2], refs[-1]
        arrive = [
            pltpu.make_async_copy(refs[k].at[pl.ds(at, n)], held[k].at[pl.ds(at, n)], into.at[i])
            for i, (k, at, n) in enumerate(parts)
        ]
        leave = [
            pltpu.make_async_copy(held[k].at[pl.ds(at, n)], refs[count + k].at[pl.ds(at, n)], out.at[i])
            for i, (k, at, n) in enumerate(parts)
        ]
        for copy in arrive:
            copy.start()
        for copy, onward in zip(arrive, leave):
            copy.wait()
            onward.start()
        for copy in leave:
            copy.wait()

    any_space = pl.BlockSpec(memory_space=pl.ANY)
    return pl.pallas_call(
        kernel,
        in_specs=[any_space] * count,
        out_specs=[any_space] * count,
        out_shape=[jax.ShapeDtypeStruct(r.shape, r.dtype) for r in results],
        scratch_shapes=[pltpu.VMEM(r.shape, r.dtype) for r in results]
        + [pltpu.SemaphoreType.DMA((len(parts),)), pltpu.SemaphoreType.DMA((len(parts),))],
        compiler_params=pltpu.CompilerParams(vmem_limit_bytes=60 * MIB),
        name="finish",
    )(*results)


def local_kernels(
    patches, keep, ln1_gain, ln1_bias, w_qkv, b_query, b_value, w_out, b_out, ln2_gain, ln2_bias, w_fc1, b_fc1, w_fc2,
    b_fc2, cotangent,
):
    dp, rep = lax.axis_size("dp"), lax.axis_size("rep")
    images, slots, width = patches.shape
    rows = images * slots
    kept = keep.T
    image = jnp.arange(images, dtype=jnp.int32) * PAD
    ids = jnp.arange(slots, dtype=jnp.int32)[:, None]
    upto = (ids >= ids.T).astype(jnp.float32)
    ranks = matmul(upto, kept.astype(jnp.float32)).astype(jnp.int32)
    counts = ranks[-1]
    keys = jnp.stack([
        jnp.where(kept == 1, image + ranks - 1, -1), jnp.where(ids < counts, image + ids, -1)
    ]).reshape(2, rows)
    keys = jnp.pad(keys.astype(jnp.float32), ((0, 6), (0, 0)))
    flat = lambda a: jnp.swapaxes(a, 0, 1).reshape(rows, width)
    row = lambda v: v.reshape(1, -1)
    *shares, small, hidden = layer(
        counts, [flat(patches), flat(cotangent), w_qkv, w_out, w_fc1, w_fc2], keys,
        [row(v) for v in (ln1_gain, ln1_bias, b_query, b_value, b_out, ln2_gain, ln2_bias, b_fc1, b_fc2)], dp, rep,
    )
    layer_rows, grad_patches, fc1_share, fc2_share, out_share, qkv_share = finish(shares)
    mine = small[:, : width // (dp * rep)]
    unflat = lambda a: jnp.swapaxes(a.reshape(slots, images, width), 0, 1)
    return (
        unflat(layer_rows), unflat(grad_patches), mine[0], mine[1], qkv_share, mine[2], mine[3], out_share, mine[4], mine[5],
        mine[6], fc1_share, hidden[0], fc2_share, mine[7],
    )


def normalize(v):
    centred = v - jnp.mean(v, axis=-1, keepdims=True)
    return centred * lax.rsqrt(jnp.mean(centred * centred, axis=-1, keepdims=True) + NORM_EPSILON)


def affine_norm(v, gain, shift):
    return normalize(v) * gain + shift


def exchange(parts, axis, stride, count):
    size = lax.axis_size(axis)
    index = lax.axis_index(axis)
    place = (index // stride) % count
    total = lax.dynamic_index_in_dim(parts, place, 0, keepdims=False)
    for step in range(1, count):
        pairs = []
        for source in range(size):
            own = (source // stride) % count
            target = source + (((own + step) % count) - own) * stride
            pairs.append((source, target))
        sent = lax.dynamic_index_in_dim(parts, (place + step) % count, 0, keepdims=False)
        total = total + lax.ppermute(sent, axis, pairs)
    return total


def scatter_sum(grad):
    rows, columns = grad.shape
    dp, rep = lax.axis_size("dp"), lax.axis_size("rep")
    z, y = dp // 2, rep // 2
    share = rows // (dp * rep)
    parts = grad.reshape(z, 2, y, 2, share, columns)
    parts = exchange(jnp.moveaxis(parts, 3, 0), "rep", 1, 2)
    half = columns // 2
    x_first, y_first = parts[..., :half], parts[..., half:]
    x_first = exchange(jnp.moveaxis(x_first, 1, 0), "dp", 1, 2)
    y_first = exchange(jnp.moveaxis(y_first, 2, 0), "rep", 2, y)
    x_first = exchange(jnp.moveaxis(x_first, 1, 0), "rep", 2, y)
    y_first = exchange(jnp.moveaxis(y_first, 1, 0), "dp", 1, 2)
    both = jnp.concatenate([x_first, y_first], axis=-1)
    return exchange(both, "dp", 2, z)


def scatter_vectors(vectors):
    joined = jnp.concatenate([v.reshape(lax.axis_size("dp") * lax.axis_size("rep"), -1) for v in vectors], axis=1)
    total = lax.psum_scatter(joined, ("dp", "rep"), scatter_dimension=0, tiled=True)[0]
    out, start = [], 0
    for v in vectors:
        length = v.shape[0] // (lax.axis_size("dp") * lax.axis_size("rep"))
        out.append(total[start : start + length])
        start += length
    return out


def local_permutes(
    patches,
    keep,
    ln1_gain,
    ln1_bias,
    w_qkv,
    b_query,
    b_value,
    w_out,
    b_out,
    ln2_gain,
    ln2_bias,
    w_fc1,
    b_fc1,
    w_fc2,
    b_fc2,
    cotangent,
):
    images, slot_count, width = patches.shape
    row_count = images * slot_count
    table, valid_slots = select_parts(keep, slot_count)
    kept = jnp.einsum(
        "bsp,bpd->bsd", table.astype(jnp.bfloat16), patches, preferred_element_type=jnp.float32
    ).reshape(row_count, width)
    normed_one, norm_one_back = jax.vjp(affine_norm, kept, ln1_gain, ln1_bias)
    act_one = normed_one.astype(jnp.bfloat16)
    bias_all = jnp.concatenate([b_query, jnp.zeros_like(b_query), b_value])
    qkv = (matmul(act_one, w_qkv) + bias_all).astype(jnp.bfloat16)
    qkv = qkv.reshape(images, slot_count, 3, HEADS, HEAD_DIM)
    queries, key_part, values = (qkv[:, :, 0], qkv[:, :, 1], qkv[:, :, 2])
    scores = (
        jnp.einsum("blhe,bmhe->bhlm", queries, key_part, preferred_element_type=jnp.float32)
        * SCORE_SCALE
    )
    scores = jnp.where(valid_slots[:, None, None, :] > 0, scores, -1000000000.0)
    attn_probs, softmax_back = jax.vjp(partial(jax.nn.softmax, axis=-1), scores)
    probs_low = attn_probs.astype(jnp.bfloat16)
    mixed_heads = jnp.einsum(
        "bhlm,bmhe->blhe", probs_low, values, preferred_element_type=jnp.float32
    )
    mixed_heads = mixed_heads.reshape(row_count, width).astype(jnp.bfloat16)
    after_attn = kept + (matmul(mixed_heads, w_out) + b_out)
    normed_two, norm_two_back = jax.vjp(affine_norm, after_attn, ln2_gain, ln2_bias)
    act_two = normed_two.astype(jnp.bfloat16)
    pre_gelu = matmul(act_two, w_fc1) + b_fc1
    gelu_full, gelu_back = jax.vjp(partial(jax.nn.gelu, approximate=False), pre_gelu)
    gelu_out = gelu_full.astype(jnp.bfloat16)
    mlp_out = matmul(gelu_out, w_fc2) + b_fc2
    row_mask = valid_slots.reshape(row_count, 1)
    layer_out = ((after_attn + mlp_out) * row_mask).astype(jnp.bfloat16)
    layer_out = layer_out.reshape(images, slot_count, width)
    grad_out = cotangent.astype(jnp.float32).reshape(row_count, width) * row_mask
    grad_top = grad_out.astype(jnp.bfloat16)
    grad_w_fc2 = matmul(gelu_out.T, grad_top)
    grad_b_fc2 = jnp.sum(grad_top.astype(jnp.float32), axis=0)
    (grad_pre_full,) = gelu_back(matmul(grad_top, w_fc2.T))
    grad_pre = grad_pre_full.astype(jnp.bfloat16)
    grad_w_fc1 = matmul(act_two.T, grad_pre)
    grad_b_fc1 = jnp.sum(grad_pre.astype(jnp.float32), axis=0)
    grad_norm_two, grad_ln2_gain, grad_ln2_bias = norm_two_back(matmul(grad_pre, w_fc1.T))
    grad_after = grad_out + grad_norm_two
    share_w_fc2 = scatter_sum(grad_w_fc2)
    share_w_fc1 = scatter_sum(grad_w_fc1)
    grad_branch = grad_after.astype(jnp.bfloat16)
    grad_w_out = matmul(mixed_heads.T, grad_branch)
    grad_b_out = jnp.sum(grad_branch.astype(jnp.float32), axis=0)
    grad_mixed = matmul(grad_branch, w_out.T).astype(jnp.bfloat16)
    grad_mixed = grad_mixed.reshape(images, slot_count, HEADS, HEAD_DIM)
    grad_probs = jnp.einsum(
        "blhe,bmhe->bhlm", grad_mixed, values, preferred_element_type=jnp.float32
    )
    grad_values = jnp.einsum(
        "bhlm,blhe->bmhe", probs_low, grad_mixed, preferred_element_type=jnp.float32
    )
    (grad_scores_full,) = softmax_back(grad_probs)
    grad_scores = grad_scores_full.astype(jnp.bfloat16)
    grad_queries = (
        jnp.einsum("bhlm,bmhe->blhe", grad_scores, key_part, preferred_element_type=jnp.float32)
        * SCORE_SCALE
    )
    grad_keys = (
        jnp.einsum("bhlm,blhe->bmhe", grad_scores, queries, preferred_element_type=jnp.float32)
        * SCORE_SCALE
    )
    grad_qkv = jnp.stack([grad_queries, grad_keys, grad_values], axis=2)
    grad_qkv = grad_qkv.reshape(row_count, 3 * width).astype(jnp.bfloat16)
    grad_w_qkv = matmul(act_one.T, grad_qkv)
    column_sums = jnp.sum(grad_qkv.astype(jnp.float32), axis=0)
    grad_b_query = column_sums[:width]
    grad_b_value = column_sums[2 * width :]
    grad_norm_one, grad_ln1_gain, grad_ln1_bias = norm_one_back(matmul(grad_qkv, w_qkv.T))
    grad_kept = grad_after + grad_norm_one
    share_w_out = scatter_sum(grad_w_out)
    share_w_qkv = scatter_sum(grad_w_qkv)
    small = scatter_vectors(
        [grad_ln1_gain, grad_ln1_bias, grad_b_query, grad_b_value, grad_b_out, grad_ln2_gain, grad_ln2_bias, grad_b_fc1, grad_b_fc2]
    )
    grad_patches = jnp.einsum(
        "bsp,bsd->bpd",
        table,
        grad_kept.reshape(images, slot_count, width),
        precision=lax.Precision.HIGHEST,
    )
    return (
        layer_out,
        grad_patches,
        small[0],
        small[1],
        share_w_qkv,
        small[2],
        small[3],
        share_w_out,
        small[4],
        small[5],
        small[6],
        share_w_fc1,
        small[7],
        share_w_fc2,
        small[8],
    )


def solution(mesh):
    in_specs = (
        P(("dp", "rep"), None, None),
        P(("dp", "rep"), None),
        P(),
        P(),
        P(),
        P(),
        P(),
        P(),
        P(),
        P(),
        P(),
        P(),
        P(),
        P(),
        P(),
        P(("dp", "rep"), None, None),
    )
    out_specs = (
        P(("dp", "rep"), None, None),
        P(("dp", "rep"), None, None),
        P(("dp", "rep")),
        P(("dp", "rep")),
        P(("dp", "rep"), None),
        P(("dp", "rep")),
        P(("dp", "rep")),
        P(("dp", "rep"), None),
        P(("dp", "rep")),
        P(("dp", "rep")),
        P(("dp", "rep")),
        P(("dp", "rep"), None),
        P(("dp", "rep")),
        P(("dp", "rep"), None),
        P(("dp", "rep")),
    )
    fits = mesh.shape["dp"] == 8 and mesh.shape["rep"] == 4
    local = local_kernels if fits else local_permutes
    return jax.shard_map(local, mesh=mesh, in_specs=in_specs, out_specs=out_specs, check_vma=False)
```
